512 devices in a mesh: group: 8 (over x, z_hi), fsdp: 64 (over z_lo, y, core).
Axes of the slice: x: 4, y: 4, z: 16 (z_hi: 2, z_lo: 8; z = z_hi * 8 + z_lo), core: 2. Of those that a mesh axis runs over, the one named last changes fastest.
Arguments:
- hidden: bfloat16 [131072, 2304], P(('group', 'fsdp')), may hold values from -6 to 6
- grad_values: bfloat16 [131072, 1024], P(('group', 'fsdp')), may hold values from -6 to 6
- weights: float32 [8, 2304, 1024], P('group', 'fsdp'), may hold values from -6 to 6
- gains: float32 [8, 2304], P('group', 'fsdp'), may hold values from 0.5 to 1.5
- snapshot: float32 [8, 2304, 128], P('group', 'fsdp'), may hold values from -6 to 6
- outer_frag: float32 [2304, 128], P('fsdp'), may hold values from -6 to 6
- outer_moment: float32 [2304, 128], P('fsdp'), may hold values from -6 to 6
- fragment_index: int32 [1], replicated, may hold values from 0 to 7
Outputs:
- values: bfloat16 [131072, 1024], P(('group', 'fsdp'))
- grad_hidden: bfloat16 [131072, 2304], P(('group', 'fsdp'))
- new_weights: float32 [8, 2304, 1024], P('group', 'fsdp')
- new_gains: float32 [8, 2304], P('group', 'fsdp')
- new_outer: float32 [2304, 128], P('fsdp')
- new_moment: float32 [2304, 128], P('fsdp')
The draws below stay inside these ranges and needn't reach their ends.
All inputs are finite; a program needn't handle non-finite values.
Results may differ from the reference program's by a relative error of at most 0.0015.
The reference program's roundings to bfloat16 on the way (of `gain_bf`, `normed_bf` and `weight_bf`) count: a program that leaves them out, or rounds other values in their place, can miss the bound.
Values may be sent and summed in bfloat16 or wider, within the bound.
A program may use at most 128 MiB of HBM per device.

```python
import jax
import jax.numpy as jnp
from jax import lax

D = 2304
KV = 1024
FRAGS = 8
FW = 128
TOKENS = 131072
N_GROUP = 8


def levels(own_key, shape, cuts, low, top_value):
    factor_of, own = 1.0, jax.random.fold_in(own_key, 6)
    for position, shards_of in cuts:
        draws = jnp.exp(jax.random.uniform(jax.random.fold_in(own, position), (shards_of,), jnp.float32, low / len(cuts), top_value / len(cuts)))
        factor_of = factor_of * jnp.repeat(draws, shape[position] // shards_of).reshape([-1 if axis == position else 1 for axis in range(len(shape))])
    return factor_of


def bell_draw(rng, extent, width, most, pieces=(), kind=jnp.bfloat16):
    gain = levels(rng, extent, pieces, -0.22, 0.18) if pieces else 1.0
    result = jax.random.normal(rng, extent, jnp.float32) * width * gain
    return jnp.minimum(jnp.maximum(result, -most), most).astype(kind)


def setup_inputs(seed: int = 0) -> dict:
    key_list = jax.random.split(jax.random.key(seed), 9)
    hidden = bell_draw(key_list[0], (TOKENS, D), 1.0, 6.0, ((0, 512),))
    grad_values = bell_draw(key_list[1], (TOKENS, KV), 1.0, 6.0, ((0, 512),))
    weights = bell_draw(key_list[2], (N_GROUP, D, KV), 1.0, 6.0, ((0, 8), (1, 64)), jnp.float32)
    gains = jnp.clip(1.0 + 0.1 * jax.random.normal(key_list[3], (N_GROUP, D), jnp.float32), 0.5, 1.5)
    snapshot = bell_draw(key_list[4], (N_GROUP, D, FW), 1.0, 6.0, ((0, 8), (1, 64)), jnp.float32)
    outer_frag = bell_draw(key_list[5], (D, FW), 1.0, 6.0, ((0, 64),), jnp.float32)
    outer_moment = bell_draw(key_list[6], (D, FW), 0.5, 6.0, ((0, 64),), jnp.float32)
    fragment_index = jax.random.randint(key_list[7], (1,), 0, FRAGS).astype(jnp.int32)
    return {"hidden": hidden, "grad_values": grad_values, "weights": weights, "gains": gains, "snapshot": snapshot, "outer_frag": outer_frag, "outer_moment": outer_moment, "fragment_index": fragment_index}


epsilon = 1e-06
inner_rate = 0.05
gain_rate = 0.002
momentum = 0.9
outer_rate = 0.7
mixing = 0.5

def reference(hidden, grad_values, weights, gains, snapshot, outer_frag, outer_moment, fragment_index):
    factor = D ** (-0.5)
    group_tokens = hidden.shape[0] // N_GROUP
    mean_snap = lax.optimization_barrier(jnp.sum(snapshot, axis=0)) / N_GROUP
    change = outer_frag - mean_snap
    new_moment = momentum * outer_moment + change
    new_outer = outer_frag - outer_rate * (change + momentum * new_moment)
    offset = (fragment_index[0] * FW).astype(jnp.int32)
    value_list, grad_list, weight_list, gain_list = ([], [], [], [])
    for member in range(N_GROUP):
        tokens = hidden[member * group_tokens:(member + 1) * group_tokens].astype(jnp.float32)
        cotangent = grad_values[member * group_tokens:(member + 1) * group_tokens]
        inverse = lax.rsqrt(lax.optimization_barrier(jnp.mean(tokens * tokens, axis=-1, keepdims=True)) + epsilon)
        normed = tokens * inverse
        gain_bf = gains[member].astype(jnp.bfloat16)
        normed_bf = (normed * gain_bf.astype(jnp.float32)).astype(jnp.bfloat16)
        weight_bf = weights[member].astype(jnp.bfloat16)
        value_list.append((jnp.dot(normed_bf, weight_bf, preferred_element_type=jnp.float32) * factor).astype(jnp.bfloat16))
        input_grad = jnp.dot(cotangent, weight_bf.T, preferred_element_type=jnp.float32) * factor
        weight_grad = jnp.dot(normed_bf.T, cotangent, preferred_element_type=jnp.float32) * factor
        gain_grad = lax.optimization_barrier(jnp.sum(input_grad * normed, axis=0))
        scaled = input_grad * gain_bf.astype(jnp.float32)
        grad_list.append((inverse * (scaled - normed * lax.optimization_barrier(jnp.mean(scaled * normed, axis=-1, keepdims=True)))).astype(jnp.bfloat16))
        inner = weights[member] - inner_rate * weight_grad
        old_cols = lax.dynamic_slice_in_dim(inner, offset, FW, 1)
        mixed_cols = mixing * old_cols + (1.0 - mixing) * new_outer
        weight_list.append(lax.dynamic_update_slice_in_dim(inner, mixed_cols, offset, 1))
        gain_list.append(gains[member] - gain_rate * gain_grad)
    return (jnp.concatenate(value_list, 0), jnp.concatenate(grad_list, 0), jnp.stack(weight_list, 0), jnp.stack(gain_list, 0), new_outer, new_moment)
```

```python
import functools

import jax
import jax.numpy as jnp
from jax import lax
from jax.experimental import pallas as pl
from jax.experimental.pallas import tpu as pltpu
from jax.sharding import PartitionSpec as P

MESH = pl.DeviceIdType.MESH
F32 = jnp.float32
BF16 = jnp.bfloat16

D = 2304
KV = 1024
FW = 128
FRAGS = 8
TOK = 256
NZ = 8
NY = 4
NE = 8
NX = 4
ROWS = 36
CHIP = 72
SLAB = 288
HALF = 512

epsilon = 1e-06
inner_rate = 0.05
gain_rate = 0.002
momentum = 0.9
outer_rate = 0.7
mixing = 0.5
FACTOR = D ** (-0.5)


def window_start(z):
    return (SLAB * z) // 128


def order(z, s):
    near = jnp.where(z > 3, 7 - z, z)
    first = 7 - 2 * near
    k = s - first
    two_sided = jnp.where(k % 2 == 0, 2 * near - k // 2, (k - 1) // 2)
    slab = jnp.where(s < first, 7 - s, two_sided)
    slab = jnp.where(z > 3, 7 - slab, slab)
    return jnp.where(s == 7, z, slab)


def step_kernel(
    frag_ref, hid_hbm, gv_hbm, w_ref, gains_ref, snap_ref, outer_ref, mom_ref,
    values_hbm, gh_hbm, neww_ref, ggrad_ref, newo_ref, newm_ref,
    hid, gx, nbx, wp, w, stage, pack, dw, s1, r1, s2, r2, racc, sz, rz, fbuf,
    ig, vout, gh, invb, grow, gacc, g1, g2, hsrc, h1, h2, sx, szh,
    in_sem, out_sem, agz_s, agz_r, ay_s, ay_r, tw_s, tw_r, nx_s, nx_r,
    ry_s, ry_r, rz_s, rz_r, f_s, f_r,
    g1_s, g1_r, g2_s, g2_r, h1_s, h1_r, h2_s, h2_r, sx_s, sx_r, szh_s, szh_r,
):
    g = lax.axis_index("group")
    f = lax.axis_index("fsdp")
    x, zh = g // 2, g % 2
    z, e = f // NE, f % NE
    y, c = e // 2, e % 2
    yr, yl, yo = (y + 1) % NY, (y + 3) % NY, (y + 2) % NY
    twin = (g, f + 1 - 2 * c)

    def at(zz, yy):
        return (g, zz * NE + yy * 2 + c)

    right, left = at(z, yr), at(z, yl)
    up, down = at(z + 1, y), at(z - 1, y)
    e_peers = [((e + k) % NE, (g, z * NE + (e + k) % NE)) for k in range(1, NE)]
    z_peers = [((z + k) % NZ, (g, ((z + k) % NZ) * NE + e)) for k in range(1, NZ)]
    x_peers = [((x + k) % NX, (((x + k) % NX) * 2 + zh, f)) for k in range(1, NX)]
    zh_peer = (x * 2 + 1 - zh, f)

    def remote(src, dst, send, recv, device):
        return pltpu.make_async_remote_copy(
            src_ref=src, dst_ref=dst, send_sem=send, recv_sem=recv, device_id=device, device_id_type=MESH
        )

    hid_in = pltpu.make_async_copy(hid_hbm, hid, in_sem.at[0])
    gv_in = pltpu.make_async_copy(gv_hbm, gx.at[c], in_sem.at[1])
    hid_in.start()
    gv_in.start()

    barrier = pltpu.get_barrier_semaphore()
    peers = [p for _, p in e_peers] + [p for _, p in z_peers] + [p for _, p in x_peers] + [zh_peer]
    for peer in peers:
        pl.semaphore_signal(barrier, inc=1, device_id=peer, device_id_type=MESH)

    for h in range(2):
        for q in range(4):
            pack[h, ROWS * q : ROWS * (q + 1), :] = w_ref[0, :, HALF * h + 128 * q : HALF * h + 128 * (q + 1)]
    wp[c, z, y] = pack[...].astype(BF16)

    gain_own = jnp.broadcast_to(gains_ref[...].astype(BF16), (8, ROWS))
    first_lane = ROWS * f - 128 * window_start(z)
    spot = lax.broadcasted_iota(jnp.int32, (ROWS, 128), 0) + first_lane
    lane = lax.broadcasted_iota(jnp.int32, (ROWS, 128), 1)
    g1[e] = jnp.zeros((8, 128), F32)
    for r in range(3):
        hot = jnp.where(spot == lane + 128 * r, 1.0, 0.0).astype(BF16)
        g1[e, r : r + 1, :] = jnp.dot(gain_own, hot, preferred_element_type=F32)[0:1]
    sx[x] = jnp.zeros((40, 128), F32)
    sx[x, 0:ROWS, :] = snap_ref[0]

    pl.semaphore_wait(barrier, len(peers))

    def spread_start(buf, own, peer_list, send, recv, src=None):
        for index, peer in peer_list:
            source = buf.at[own] if src is None else src.at[index]
            remote(source, buf.at[own], send.at[index], recv.at[own], peer).start()

    def spread_wait(buf, own, peer_list, send, recv):
        for index, peer in peer_list:
            remote(buf.at[index], buf.at[index], send.at[index], recv.at[index], peer).wait_recv()

    def spread_done(buf, own, peer_list, send, recv, src=None):
        for index, peer in peer_list:
            source = buf.at[own] if src is None else src.at[index]
            remote(source, buf.at[own], send.at[index], recv.at[own], peer).wait_send()

    def total(buf, count):
        result = buf[0]
        for index in range(1, count):
            result = result + buf[index]
        return result

    def z_copy(direction, slab):
        return remote(
            wp.at[c, slab, y], wp.at[c, slab, y], agz_s.at[direction, slab], agz_r.at[direction, slab],
            up if direction == 0 else down,
        )

    def y_copy(kind, slab):
        device = right if kind in (0, 2) else left
        if kind < 2:
            ref = wp.at[c, slab, y]
        elif kind == 2:
            ref = wp.at[c, slab, yl, 0]
        else:
            ref = wp.at[c, slab, yr, 1]
        return remote(ref, ref, ay_s.at[kind, slab], ay_r.at[kind, slab], device)

    def y_arrival(kind, slab):
        ref = [wp.at[c, slab, yl], wp.at[c, slab, yr], wp.at[c, slab, yo, 0], wp.at[c, slab, yo, 1]][kind]
        return remote(ref, ref, ay_s.at[kind, slab], ay_r.at[kind, slab], right)

    def twin_copy(slab, core):
        return remote(wp.at[core, slab], wp.at[core, slab], tw_s.at[slab], tw_r.at[slab], twin)

    def gather_z(t):
        if t == 0:
            @pl.when(z < NZ - 1)
            def _():
                z_copy(0, z).start()

            @pl.when(z > 0)
            def _():
                z_copy(1, z).start()

            y_copy(0, z).start()
            y_copy(1, z).start()
            return

        @pl.when(z - t >= 0)
        def _():
            slab = z - t
            z_copy(0, slab).wait_recv()

            @pl.when(z < NZ - 1)
            def _():
                z_copy(0, slab).start()

            y_copy(0, slab).start()
            y_copy(1, slab).start()

        @pl.when(z + t <= NZ - 1)
        def _():
            slab = z + t
            z_copy(1, slab).wait_recv()

            @pl.when(z > 0)
            def _():
                z_copy(1, slab).start()

            y_copy(0, slab).start()
            y_copy(1, slab).start()

    def gather_y(j):
        slab = order(z, 7 - j)
        y_arrival(0, slab).wait_recv()
        y_copy(2, slab).start()
        y_arrival(1, slab).wait_recv()
        y_copy(3, slab).start()

    def gather_twin(j):
        slab = order(z, 7 - j)
        y_arrival(2, slab).wait_recv()
        y_arrival(3, slab).wait_recv()
        twin_copy(slab, c).start()

    def unpack(lo, hi):
        def one(j, _):
            slab = order(z, 7 - j)
            twin_copy(slab, 1 - c).wait_recv()
            for core in range(2):
                for yy in range(NY):
                    for h in range(2):
                        block = wp[core, slab, yy, h].astype(F32)
                        base = ROWS * (2 * yy + core)
                        for q in range(4):
                            stage[base : base + ROWS, HALF * h + 128 * q : HALF * h + 128 * (q + 1)] = block[
                                ROWS * q : ROWS * (q + 1)
                            ]
            w[pl.ds(pl.multiple_of(SLAB * slab, 16), SLAB), :] = stage[...].astype(BF16)
            return 0

        lax.fori_loop(lo, hi, one, 0)

    def norms():
        def one(r, _):
            rows = pl.ds(pl.multiple_of(32 * r, 32), 32)
            tokens = hid[rows, :].astype(F32)
            mean = jnp.sum(tokens * tokens, axis=-1, keepdims=True) / D
            invb[rows, :] = jnp.broadcast_to(lax.rsqrt(mean + epsilon), (32, 128))
            return 0

        lax.fori_loop(0, TOK // 32, one, 0)

    def normalise():
        def one(r, _):
            rows = pl.ds(pl.multiple_of(32 * r, 32), 32)
            normed = hid[rows, :].astype(F32) * invb[rows, 0:1]
            nbx[c, rows, :] = (normed * grow[0:1, :]).astype(BF16)
            return 0

        lax.fori_loop(0, TOK // 32, one, 0)

    nx_nb = lambda core: remote(nbx.at[core], nbx.at[core], nx_s.at[0], nx_r.at[0], twin)
    nx_gv = lambda core: remote(gx.at[core], gx.at[core], nx_s.at[1], nx_r.at[1], twin)

    def weight_terms():
        columns = pl.ds(pl.multiple_of(HALF * c, 128), HALF)

        def one(k, _):
            feats = pl.ds(pl.multiple_of(256 * k, 256), 256)
            dims = (((0,), (0,)), ((), ()))
            dw[feats, :] = lax.dot_general(
                nbx[0, :, feats], gx[0, :, columns], dims, preferred_element_type=F32
            ) + lax.dot_general(nbx[1, :, feats], gx[1, :, columns], dims, preferred_element_type=F32)
            return 0

        lax.fori_loop(0, D // 256, one, 0)

    def term(slab, yy, h):
        rows = pl.ds(pl.multiple_of(CHIP * (NY * slab + yy), 8), CHIP)
        return jnp.concatenate([dw[rows, 256 * h : 256 * h + 128], dw[rows, 256 * h + 128 : 256 * h + 256]], axis=0)

    def far_copy(kind, slab):
        return remote(
            s1.at[slab, kind], r1.at[slab, kind], ry_s.at[kind, slab], ry_r.at[kind, slab], right if kind == 0 else left
        )

    def near_copy(kind, slab):
        return remote(
            s2.at[slab, kind], r2.at[slab, kind], ry_s.at[2 + kind, slab], ry_r.at[2 + kind, slab],
            right if kind == 0 else left,
        )

    def chain_copy(direction, slab):
        return remote(
            sz.at[slab], rz.at[direction, slab], rz_s.at[direction, slab], rz_r.at[direction, slab],
            up if direction == 0 else down,
        )

    def reduce_far(s):
        slab = order(z, s)
        for h in range(2):
            s1[slab, h] = term(slab, yo, h).astype(BF16)
            far_copy(h, slab).start()

    def reduce_near(s):
        slab = order(z, s)
        for kind, yy in ((0, yr), (1, yl)):
            far_copy(kind, slab).wait_recv()
            s2[slab, kind, kind] = (term(slab, yy, kind) + r1[slab, kind].astype(F32)).astype(BF16)
            s2[slab, kind, 1 - kind] = term(slab, yy, 1 - kind).astype(BF16)
            near_copy(kind, slab).start()

    def reduce_row(s):
        slab = order(z, s)
        near_copy(0, slab).wait_recv()
        near_copy(1, slab).wait_recv()
        for h in range(2):
            racc[slab, h] = term(slab, y, h) + r2[slab, 0, h].astype(F32) + r2[slab, 1, h].astype(F32)

    def reduce_chain(u):
        if u == NZ - 1:
            @pl.when(z > 0)
            def _():
                chain_copy(0, z).wait_recv()
                racc[z] = racc[z] + rz[0, z].astype(F32)

            @pl.when(z < NZ - 1)
            def _():
                chain_copy(1, z).wait_recv()
                racc[z] = racc[z] + rz[1, z].astype(F32)

            return

        @pl.when(z <= u)
        def _():
            slab = NZ - 1 + z - u

            @pl.when(z > 0)
            def _():
                chain_copy(0, slab).wait_recv()
                sz[slab] = (racc[slab] + rz[0, slab].astype(F32)).astype(BF16)

            @pl.when(z == 0)
            def _():
                sz[slab] = racc[slab].astype(BF16)

            chain_copy(0, slab).start()

        @pl.when(z >= NZ - 1 - u)
        def _():
            slab = z - (NZ - 1) + u

            @pl.when(z < NZ - 1)
            def _():
                chain_copy(1, slab).wait_recv()
                sz[slab] = (racc[slab] + rz[1, slab].astype(F32)).astype(BF16)

            @pl.when(z == NZ - 1)
            def _():
                sz[slab] = racc[slab].astype(BF16)

            chain_copy(1, slab).start()

    def make_values():
        def one(n, _):
            columns = pl.ds(pl.multiple_of(256 * n, 256), 256)
            vout[:, columns] = (jnp.dot(nbx[c], w[:, columns], preferred_element_type=F32) * FACTOR).astype(BF16)
            return 0

        lax.fori_loop(0, KV // 256, one, 0)

    values_out = pltpu.make_async_copy(vout, values_hbm, out_sem.at[0])
    gh_out = pltpu.make_async_copy(gh, gh_hbm, out_sem.at[1])

    def input_gradient(lo, hi):
        def one(k, _):
            feats = pl.ds(pl.multiple_of(256 * k, 256), 256)
            ig[:, feats] = (
                lax.dot_general(gx[c], w[feats, :], (((1,), (1,)), ((), ())), preferred_element_type=F32) * FACTOR
            )
            return 0

        lax.fori_loop(lo, hi, one, 0)

    def hidden_gradient(lo, hi):
        def one(r, _):
            rows = pl.ds(pl.multiple_of(32 * r, 32), 32)
            inverse = invb[rows, 0:1]
            normed = hid[rows, :].astype(F32) * inverse
            grad = ig[rows, :]
            along = grad * normed
            gacc[...] += jnp.sum(along.reshape(4, 8, D), axis=0)
            gain = grow[0:1, :]
            mean = jnp.sum(along * gain, axis=-1, keepdims=True) / D
            gh[rows, :] = (inverse * (grad * gain - normed * mean)).astype(BF16)
            return 0

        lax.fori_loop(lo, hi, one, 0)

    gather_z(0)
    spread_start(g1, e, e_peers, g1_s, g1_r)
    spread_start(sx, x, x_peers, sx_s, sx_r)
    gv_in.wait()
    nx_gv(c).start()
    hid_in.wait()
    norms()
    spread_wait(g1, e, e_peers, g1_s, g1_r)
    g2[z] = total(g1, NE)
    spread_start(g2, z, z_peers, g2_s, g2_r)
    gather_z(1)
    gather_z(2)
    gather_y(0)
    spread_wait(g2, z, z_peers, g2_s, g2_r)
    grow[...] = jnp.zeros((8, D), F32)
    for slab in range(NZ):
        for r in range(3):
            lanes = slice(128 * (window_start(slab) + r), 128 * (window_start(slab) + r + 1))
            grow[0:1, lanes] = grow[0:1, lanes] + g2[slab, r : r + 1, :]
    normalise()
    nx_nb(c).start()
    spread_wait(sx, x, x_peers, sx_s, sx_r)
    szh[zh] = total(sx, NX)
    szh_copy = remote(szh.at[zh], szh.at[zh], szh_s, szh_r, zh_peer)
    szh_copy.start()
    gather_z(3)
    gather_y(1)
    gather_twin(0)
    nx_gv(1 - c).wait_recv()
    nx_nb(1 - c).wait_recv()
    weight_terms()
    reduce_far(0)
    reduce_far(1)
    reduce_far(2)
    gather_z(4)
    gather_y(2)
    gather_twin(1)
    gather_z(5)
    gather_y(3)
    gather_twin(2)
    reduce_near(0)
    reduce_far(3)
    gather_z(6)
    gather_y(4)
    gather_twin(3)
    reduce_near(1)
    reduce_far(4)
    gather_z(7)
    gather_y(5)
    gather_twin(4)
    reduce_row(0)
    reduce_chain(0)
    reduce_near(2)
    reduce_far(5)
    gather_y(6)
    gather_twin(5)
    reduce_row(1)
    reduce_chain(1)
    reduce_near(3)
    reduce_far(6)
    gather_y(7)
    gather_twin(6)
    unpack(0, 4)
    reduce_row(2)
    reduce_chain(2)
    reduce_near(4)
    reduce_far(7)
    gather_twin(7)
    reduce_row(3)
    reduce_chain(3)
    reduce_near(5)
    unpack(4, 8)
    reduce_row(4)
    reduce_chain(4)
    reduce_near(6)
    make_values()
    values_out.start()
    reduce_row(5)
    reduce_chain(5)
    reduce_near(7)
    input_gradient(0, 9)
    reduce_row(6)
    reduce_chain(6)
    gacc[...] = jnp.zeros((8, D), F32)
    hidden_gradient(0, 8)
    gh_out.start()
    gain_row = jnp.sum(gacc[...], axis=0, keepdims=True)
    hsrc[...] = jnp.zeros((NZ, 8, 128), F32)
    for slab in range(NZ):
        for r in range(3):
            lanes = slice(128 * (window_start(slab) + r), 128 * (window_start(slab) + r + 1))
            hsrc[slab, r : r + 1, :] = gain_row[:, lanes]
    h1[z] = hsrc[z]
    spread_start(h1, z, z_peers, h1_s, h1_r, src=hsrc)
    reduce_row(7)
    reduce_chain(7)
    fbuf[c] = racc[z]
    last = lambda core: remote(fbuf.at[core], fbuf.at[core], f_s, f_r, twin)
    last(c).start()
    spread_wait(h1, z, z_peers, h1_s, h1_r)
    h2[e] = total(h1, NZ)
    spread_start(h2, e, e_peers, h2_s, h2_r)

    remote(szh.at[1 - zh], szh.at[1 - zh], szh_s, szh_r, zh_peer).wait_recv()
    change = outer_ref[...] - (szh[0] + szh[1])[0:ROWS] / (2 * NX)
    new_moment = momentum * mom_ref[...] + change
    new_outer = outer_ref[...] - outer_rate * (change + momentum * new_moment)
    newm_ref[...] = new_moment
    newo_ref[...] = new_outer

    last(1 - c).wait_recv()
    for core in range(2):
        @pl.when(c == core)
        def _():
            for j in range(FRAGS):
                q = j % 4
                base = CHIP * (q % 2) + ROWS * core
                grad = fbuf[j // 4, q // 2, base : base + ROWS, :] * FACTOR
                inner = w_ref[0, :, 128 * j : 128 * (j + 1)] - inner_rate * grad
                mixed = mixing * inner + (1.0 - mixing) * newo_ref[...]
                neww_ref[0, :, 128 * j : 128 * (j + 1)] = jnp.where(frag_ref[0] == j, mixed, inner)

    spread_wait(h2, e, e_peers, h2_s, h2_r)
    ggrad_ref[...] = total(h2, NE)

    values_out.wait()
    gh_out.wait()
    for t in range(NZ):
        @pl.when(jnp.logical_and(z - t >= 0, z < NZ - 1))
        def _():
            z_copy(0, z - t).wait_send()

        @pl.when(jnp.logical_and(z + t <= NZ - 1, z > 0))
        def _():
            z_copy(1, z + t).wait_send()

    def drain(slab, _):
        for kind in range(4):
            y_copy(kind, slab).wait_send()
        twin_copy(slab, c).wait_send()
        for kind in range(2):
            far_copy(kind, slab).wait_send()
            near_copy(kind, slab).wait_send()

        @pl.when(slab > z)
        def _():
            chain_copy(0, slab).wait_send()

        @pl.when(slab < z)
        def _():
            chain_copy(1, slab).wait_send()

        return 0

    lax.fori_loop(0, NZ, drain, 0)
    nx_nb(c).wait_send()
    nx_gv(c).wait_send()
    last(c).wait_send()
    szh_copy.wait_send()
    spread_done(g1, e, e_peers, g1_s, g1_r)
    spread_done(g2, z, z_peers, g2_s, g2_r)
    spread_done(h1, z, z_peers, h1_s, h1_r, src=hsrc)
    spread_done(h2, e, e_peers, h2_s, h2_r)
    spread_done(sx, x, x_peers, sx_s, sx_r)


def body(hidden, grad_values, weights, gains, snapshot, outer_frag, outer_moment, fragment_index):
    vmem = pl.BlockSpec(memory_space=pltpu.VMEM)
    anywhere = pl.BlockSpec(memory_space=pl.ANY)
    dma = pltpu.SemaphoreType.DMA
    values, grad_hidden, new_weights, gain_window, new_outer, new_moment = pl.pallas_call(
        step_kernel,
        out_shape=(
            jax.ShapeDtypeStruct((TOK, KV), BF16),
            jax.ShapeDtypeStruct((TOK, D), BF16),
            jax.ShapeDtypeStruct((1, ROWS, KV), F32),
            jax.ShapeDtypeStruct((8, 128), F32),
            jax.ShapeDtypeStruct((ROWS, FW), F32),
            jax.ShapeDtypeStruct((ROWS, FW), F32),
        ),
        in_specs=[pl.BlockSpec(memory_space=pltpu.SMEM), anywhere, anywhere, vmem, vmem, vmem, vmem, vmem],
        out_specs=(anywhere, anywhere, vmem, vmem, vmem, vmem),
        scratch_shapes=[
            pltpu.VMEM((TOK, D), BF16),
            pltpu.VMEM((2, TOK, KV), BF16),
            pltpu.VMEM((2, TOK, D), BF16),
            pltpu.VMEM((2, NZ, NY, 2, 144, 128), BF16),
            pltpu.VMEM((D, KV), BF16),
            pltpu.VMEM((SLAB, KV), F32),
            pltpu.VMEM((2, 144, 128), F32),
            pltpu.VMEM((D, HALF), F32),
            pltpu.VMEM((NZ, 2, 144, 128), BF16),
            pltpu.VMEM((NZ, 2, 144, 128), BF16),
            pltpu.VMEM((NZ, 2, 2, 144, 128), BF16),
            pltpu.VMEM((NZ, 2, 2, 144, 128), BF16),
            pltpu.VMEM((NZ, 2, 144, 128), F32),
            pltpu.VMEM((NZ, 2, 144, 128), BF16),
            pltpu.VMEM((2, NZ, 2, 144, 128), BF16),
            pltpu.VMEM((2, 2, 144, 128), F32),
            pltpu.VMEM((TOK, D), F32),
            pltpu.VMEM((TOK, KV), BF16),
            pltpu.VMEM((TOK, D), BF16),
            pltpu.VMEM((TOK, 128), F32),
            pltpu.VMEM((8, D), F32),
            pltpu.VMEM((8, D), F32),
            pltpu.VMEM((NE, 8, 128), F32),
            pltpu.VMEM((NZ, 8, 128), F32),
            pltpu.VMEM((NZ, 8, 128), F32),
            pltpu.VMEM((NZ, 8, 128), F32),
            pltpu.VMEM((NE, 8, 128), F32),
            pltpu.VMEM((NX, 40, 128), F32),
            pltpu.VMEM((2, 40, 128), F32),
            dma((2,)), dma((2,)),
            dma((2, NZ)), dma((2, NZ)),
            dma((4, NZ)), dma((4, NZ)),
            dma((NZ,)), dma((NZ,)),
            dma((2,)), dma((2,)),
            dma((4, NZ)), dma((4, NZ)),
            dma((2, NZ)), dma((2, NZ)),
            dma, dma,
            dma((NE,)), dma((NE,)),
            dma((NZ,)), dma((NZ,)),
            dma((NZ,)), dma((NZ,)),
            dma((NE,)), dma((NE,)),
            dma((NX,)), dma((NX,)),
            dma, dma,
        ],
        compiler_params=pltpu.CompilerParams(
            collective_id=0, has_side_effects=True, vmem_limit_bytes=56 * 1024 * 1024
        ),
        cost_estimate=pl.CostEstimate(flops=3 * 2 * TOK * D * KV, bytes_accessed=4_000_000, transcendentals=0),
    )(fragment_index, hidden, grad_values, weights, gains, snapshot, outer_frag, outer_moment)
    f = lax.axis_index("fsdp")
    offset = ROWS * f - 128 * window_start(f // NE)
    gain_grad = lax.dynamic_slice_in_dim(gain_window.reshape(-1), offset, ROWS, 0)
    new_gains = gains - gain_rate * gain_grad[None]
    return (values, grad_hidden, new_weights, new_gains, new_outer, new_moment)


def solution(mesh):
    return jax.shard_map(
        body,
        mesh=mesh,
        in_specs=(
            P(("group", "fsdp"), None),
            P(("group", "fsdp"), None),
            P("group", "fsdp", None),
            P("group", "fsdp"),
            P("group", "fsdp", None),
            P("fsdp", None),
            P("fsdp", None),
            P(),
        ),
        out_specs=(
            P(("group", "fsdp"), None),
            P(("group", "fsdp"), None),
            P("group", "fsdp", None),
            P("group", "fsdp"),
            P("fsdp", None),
            P("fsdp", None),
        ),
        check_vma=False,
    )
```

```python
import functools

import jax
import jax.numpy as jnp
from jax import lax
from jax.experimental import pallas as pl
from jax.experimental.pallas import tpu as pltpu
from jax.sharding import PartitionSpec as P

MESH = pl.DeviceIdType.MESH
F32 = jnp.float32
BF16 = jnp.bfloat16

D = 2304
KV = 1024
FW = 128
FRAGS = 8
TOK = 256
NZ = 8
NY = 4
NE = 8
NX = 4
ROWS = 36
CHIP = 72
SLAB = 288
HALF = 512

epsilon = 1e-06
inner_rate = 0.05
gain_rate = 0.002
momentum = 0.9
outer_rate = 0.7
mixing = 0.5
FACTOR = D ** (-0.5)
BLOCK = 288
ZH = 112
VR = 64
VH = VR // 2


def window_start(z):
    return (SLAB * z) // 128


def order(z, s):
    pair, odd = z // 2, z % 2
    near = 3 - s // 2
    low = jnp.where(pair % 3 == 0, near, jnp.where(near < 2, 1 - near, near))
    which = jnp.where(pair > 1, 3 - low, low)
    return 2 * which + jnp.where(s % 2 == 0, 1 - odd, odd)


def step_kernel(
    frag_ref, hid_hbm, gv_hbm, w_hbm, gains_hbm, snap_hbm, outer_hbm, mom_hbm,
    values_hbm, gh_hbm, neww_hbm, newg_hbm, newo_hbm, newm_hbm,
    hid, gx, nbx, nbg, wp, w, stage, pack, dw, s1, r1, s2, r2, racc, sp, rp, sz, rz,
    vacc, vs1, vr1, vs2, vr2, vz, rv, fbuf,
    ig, vout, gh, invb, grow, gacc, g0, g1, g2, hsrc, h1, h2, sx, szh,
    w_ref, gains_ref, snap_ref, outer_ref, mom_ref, neww_ref, newg_ref, newo_ref, newm_ref,
    in_sem, out_sem, agz_s, agz_r, agp_s, agp_r, agv_s, agv_r, ay_s, ay_r, av_s, av_r, tw_s, tw_r, nx_s, nx_r,
    ry_s, ry_r, rp_s, rp_r, rz_s, rz_r, rv_s, rv_r, vy_s, vy_r, f_s, f_r,
    g0_s, g0_r, g1_s, g1_r, g2_s, g2_r, h1_s, h1_r, h2_s, h2_r, sx_s, sx_r, szh_s, szh_r, token,
):
    g = lax.axis_index("group")
    f = lax.axis_index("fsdp")
    x, zh = g // 2, g % 2
    z, e = f // NE, f % NE
    y, c = e // 2, e % 2
    yr, yl, yo = (y + 1) % NY, (y + 3) % NY, (y + 2) % NY
    twin = (g, f + 1 - 2 * c)

    def at(zz, yy):
        return (g, zz * NE + yy * 2 + c)

    right, left = at(z, yr), at(z, yl)
    up, down = at(z + 1, y), at(z - 1, y)
    mate, up_two, down_two = at(z + 1 - 2 * (z % 2), y), at(z + 2, y), at(z - 2, y)
    pair, z_mate = z // 2, z + 1 - 2 * (z % 2)
    pairs = NZ // 2
    e_peers = [((e + k) % NE, (g, z * NE + (e + k) % NE)) for k in range(1, NE)]
    z_peers = [((z + k) % NZ, (g, ((z + k) % NZ) * NE + e)) for k in range(1, NZ)]
    xr, xl, xo = (x + 1) % NX, (x + 3) % NX, (x + 2) % NX
    x_right, x_left = (xr * 2 + zh, f), (xl * 2 + zh, f)
    after = (x * 2 + (zh + (z + 1) // NZ) % 2, ((z + 1) % NZ) * NE + e)
    before = (x * 2 + (zh + (NZ - z) // NZ) % 2, ((z + NZ - 1) % NZ) * NE + e)
    zh_peer = (x * 2 + 1 - zh, f)

    def remote(src, dst, send, recv, device):
        return pltpu.make_async_remote_copy(
            src_ref=src, dst_ref=dst, send_sem=send, recv_sem=recv, device_id=device, device_id_type=MESH
        )

    barrier = pltpu.get_barrier_semaphore()
    peers = [before, after, right, left, x_right, x_left, twin]
    two_after, two_before = at((z + 2) % NZ, y), at((z + NZ - 2) % NZ, y)
    peers += [two_after, two_before]
    for peer in peers:
        pl.semaphore_signal(barrier, inc=1, device_id=peer, device_id_type=MESH)

    w_in = pltpu.make_async_copy(w_hbm, w_ref, in_sem.at[0])
    gains_in = pltpu.make_async_copy(gains_hbm, gains_ref, in_sem.at[1])
    snap_in = pltpu.make_async_copy(snap_hbm, snap_ref, in_sem.at[2])
    hid_in = pltpu.make_async_copy(hid_hbm, hid, in_sem.at[3])
    gv_in = pltpu.make_async_copy(gv_hbm, gx.at[c], in_sem.at[4])
    outer_in = pltpu.make_async_copy(outer_hbm, outer_ref, in_sem.at[5])
    mom_in = pltpu.make_async_copy(mom_hbm, mom_ref, in_sem.at[6])
    for copy in (gains_in, w_in, hid_in, gv_in, snap_in, outer_in, mom_in):
        copy.start()

    def own_columns(j):
        return pl.ds(j, ROWS, stride=FRAGS)

    def pack_own():
        w_in.wait()
        for q in range(FRAGS):
            pack[ROWS * q : ROWS * (q + 1), :] = w_ref[own_columns(q), :]
        wp[c, z, y] = pack[...].astype(BF16)

    first_lane = ROWS * f - 128 * window_start(z)
    spot = lax.broadcasted_iota(jnp.int32, (ROWS, 128), 0) + first_lane
    lane = lax.broadcasted_iota(jnp.int32, (ROWS, 128), 1)

    def place_gains():
        gains_in.wait()
        gain_own = jnp.broadcast_to(gains_ref[...].astype(BF16), (8, ROWS))
        g0[c] = jnp.zeros((8, 128), F32)
        for r in range(3):
            hot = jnp.where(spot == lane + 128 * r, 1.0, 0.0).astype(BF16)
            g0[c, r : r + 1, :] = jnp.dot(gain_own, hot, preferred_element_type=F32)[0:1]

    def gain_twin(core):
        return remote(g0.at[core], g0.at[core], g0_s, g0_r, twin)

    def gain_y(kind):
        row = y if kind < 2 else yl
        return remote(g1.at[row], g1.at[row], g1_s.at[kind], g1_r.at[kind], left if kind == 1 else right)

    def gain_y_arrival(kind):
        row = (yl, yr, yo)[kind]
        return remote(g1.at[row], g1.at[row], g1_s.at[kind], g1_r.at[kind], right)

    def gain_z(direction, slab):
        ref = g2.at[slab]
        return remote(ref, ref, g2_s.at[direction, slab], g2_r.at[direction, slab], up if direction == 0 else down)

    def gain_chip():
        gain_twin(1 - c).wait_recv()
        g1[y] = g0[0] + g0[1]
        gain_y(0).start()
        gain_y(1).start()

    def gain_near():
        gain_y_arrival(0).wait_recv()
        gain_y(2).start()

    def gain_slab():
        gain_y_arrival(1).wait_recv()
        gain_y_arrival(2).wait_recv()
        g2[z] = total(g1, NY)
        both_ways(lambda direction: gain_z(direction, z).start())

    def gather_gain(t):
        for direction, slab, here, more in ((0, z - t, z - t >= 0, z < NZ - 1), (1, z + t, z + t <= NZ - 1, z > 0)):
            @pl.when(here)
            def _():
                gain_z(direction, slab).wait_recv()

                @pl.when(more)
                def _():
                    gain_z(direction, slab).start()

    def snap_x(kind):
        row = x if kind < 2 else xl
        return remote(sx.at[row], sx.at[row], sx_s.at[kind], sx_r.at[kind], x_left if kind == 1 else x_right)

    def snap_x_arrival(kind):
        row = (xl, xr, xo)[kind]
        return remote(sx.at[row], sx.at[row], sx_s.at[kind], sx_r.at[kind], x_right)

    def place_snapshot():
        snap_in.wait()
        sx[x] = jnp.zeros((40, 128), F32)
        sx[x, 0:ROWS, :] = snap_ref[...].reshape(ROWS, 128)
        snap_x(0).start()
        snap_x(1).start()

    def snapshot_near():
        snap_x_arrival(0).wait_recv()
        snap_x(2).start()

    def pass_token(t):
        if t > 0:
            pl.semaphore_wait(token.at[t - 1], 1)
        if t < NZ - 1:
            pl.semaphore_signal(token.at[t], inc=1, device_id=after, device_id_type=MESH)

    def barrier_wait():
        pl.semaphore_wait(barrier, len(peers))

    def spread_start(buf, own, peer_list, send, recv, src=None):
        for index, peer in peer_list:
            source = buf.at[own] if src is None else src.at[index]
            remote(source, buf.at[own], send.at[index], recv.at[own], peer).start()

    def spread_wait(buf, own, peer_list, send, recv):
        for index, peer in peer_list:
            remote(buf.at[index], buf.at[index], send.at[index], recv.at[index], peer).wait_recv()

    def spread_done(buf, own, peer_list, send, recv, src=None):
        for index, peer in peer_list:
            source = buf.at[own] if src is None else src.at[index]
            remote(source, buf.at[own], send.at[index], recv.at[own], peer).wait_send()

    def total(buf, count):
        result = buf[0]
        for index in range(1, count):
            result = result + buf[index]
        return result

    first = pl.ds(0, 2 * ZH)
    halves = (pl.ds(0, ZH), pl.ds(ZH, ZH))
    final = pl.ds(2 * ZH, VR)

    def z_copy(direction, slab):
        ref = wp.at[c, slab, y, first]
        return remote(
            ref, ref, agz_s.at[direction, slab], agz_r.at[direction, slab], up_two if direction == 0 else down_two
        )

    def mate_copy(slab):
        ref = wp.at[c, slab, y, first]
        return remote(ref, ref, agp_s.at[slab], agp_r.at[slab], mate)

    def v_copy(direction, slab, yy):
        ref = wp.at[c, slab, yy, final]
        return remote(
            ref, ref, agv_s.at[direction, slab, yy], agv_r.at[direction, slab, yy], up if direction == 0 else down
        )

    def y_copy(kind, slab):
        device = right if kind in (0, 2) else left
        if kind < 2:
            ref = wp.at[c, slab, y, first]
        elif kind == 2:
            ref = wp.at[c, slab, yl, halves[0]]
        else:
            ref = wp.at[c, slab, yr, halves[1]]
        return remote(ref, ref, ay_s.at[kind, slab], ay_r.at[kind, slab], device)

    def y_arrival(kind, slab):
        ref = [
            wp.at[c, slab, yl, first], wp.at[c, slab, yr, first], wp.at[c, slab, yo, halves[0]],
            wp.at[c, slab, yo, halves[1]],
        ][kind]
        return remote(ref, ref, ay_s.at[kind, slab], ay_r.at[kind, slab], right)

    low, high = pl.ds(0, VH), pl.ds(VH, VH)
    final_low, final_high = pl.ds(2 * ZH, VH), pl.ds(2 * ZH + VH, VH)

    def vy_copy(kind):
        device = right if kind in (0, 2) else left
        if kind < 2:
            ref = wp.at[c, z, y, final]
        elif kind == 2:
            ref = wp.at[c, z, yl, final_low]
        else:
            ref = wp.at[c, z, yr, final_high]
        return remote(ref, ref, av_s.at[kind], av_r.at[kind], device)

    def vy_arrival(kind):
        ref = [
            wp.at[c, z, yl, final], wp.at[c, z, yr, final], wp.at[c, z, yo, final_low], wp.at[c, z, yo, final_high],
        ][kind]
        return remote(ref, ref, av_s.at[kind], av_r.at[kind], right)

    def twin_copy(slab, core):
        return remote(wp.at[core, slab], wp.at[core, slab], tw_s.at[slab], tw_r.at[slab], twin)

    def both_ways(send):
        @pl.when(z < NZ - 1)
        def _():
            send(0)

        @pl.when(z > 0)
        def _():
            send(1)

    def both_ways_two(send):
        @pl.when(pair < pairs - 1)
        def _():
            send(0)

        @pl.when(pair > 0)
        def _():
            send(1)

    def gather_own():
        vy_copy(0).start()
        vy_copy(1).start()
        both_ways_two(lambda direction: z_copy(direction, z).start())
        mate_copy(z).start()
        both_ways(lambda direction: v_copy(direction, z, y).start())
        y_copy(0, z).start()
        y_copy(1, z).start()

    def gather_near():
        vy_arrival(0).wait_recv()
        vy_copy(2).start()
        both_ways(lambda direction: v_copy(direction, z, yl).start())
        vy_arrival(1).wait_recv()
        vy_copy(3).start()
        both_ways(lambda direction: v_copy(direction, z, yr).start())

    def gather_far():
        vy_arrival(2).wait_recv()
        vy_arrival(3).wait_recv()
        both_ways(lambda direction: v_copy(direction, z, yo).start())

    v_order = (y, yl, yr, yo)

    def gather_z(t):
        for direction, slab, here, more in (
            (0, z - 2 * t, pair >= t, pair < pairs - 1), (1, z + 2 * t, pair + t < pairs, pair > 0),
        ):
            @pl.when(here)
            def _():
                z_copy(direction, slab).wait_recv()

                @pl.when(more)
                def _():
                    z_copy(direction, slab).start()

                mate_copy(slab).start()
                y_copy(0, slab).start()
                y_copy(1, slab).start()

    def gather_mate(t):
        sides = ((z_mate, pair >= 0),) if t == 0 else ((z_mate - 2 * t, pair >= t), (z_mate + 2 * t, pair + t < pairs))
        for slab, here in sides:
            @pl.when(here)
            def _():
                mate_copy(slab).wait_recv()
                y_copy(0, slab).start()
                y_copy(1, slab).start()

    def gather_v(t):
        for direction, slab, here, more in ((0, z - t, z - t >= 0, z < NZ - 1), (1, z + t, z + t <= NZ - 1, z > 0)):
            @pl.when(here)
            def _():
                for yy in v_order:
                    v_copy(direction, slab, yy).wait_recv()

                    @pl.when(more)
                    def _():
                        v_copy(direction, slab, yy).start()

    def gather_y(j):
        slab = order(z, 7 - j)
        y_arrival(0, slab).wait_recv()
        y_copy(2, slab).start()
        y_arrival(1, slab).wait_recv()
        y_copy(3, slab).start()

    def gather_twin(j):
        slab = order(z, 7 - j)
        y_arrival(2, slab).wait_recv()
        y_arrival(3, slab).wait_recv()
        twin_copy(slab, c).start()

    def unpack(lo, hi):
        def one(j, _):
            slab = order(z, 7 - j)
            twin_copy(slab, 1 - c).wait_recv()
            for core in range(2):
                for yy in range(NY):
                    block = wp[core, slab, yy].astype(F32)
                    base = ROWS * (2 * yy + core)
                    for q in range(FRAGS):
                        stage[base : base + ROWS, 128 * q : 128 * (q + 1)] = block[ROWS * q : ROWS * (q + 1)]
            w[pl.ds(pl.multiple_of(SLAB * slab, 16), SLAB), :] = stage[...].astype(BF16)
            return 0

        lax.fori_loop(lo, hi, one, 0)

    def normalise(lo, hi):
        def one(r, _):
            rows = pl.ds(pl.multiple_of(32 * r, 32), 32)
            tokens = hid[rows, :].astype(F32)
            inverse = lax.rsqrt(jnp.sum(tokens * tokens, axis=-1, keepdims=True) / D + epsilon)
            invb[rows, :] = jnp.broadcast_to(inverse, (32, 128))
            nbx[c, rows, :] = (tokens * inverse).astype(BF16)
            return 0

        lax.fori_loop(lo, hi, one, 0)

    def gain_vector():
        grow[...] = jnp.zeros((8, D), F32)
        for slab in range(NZ):
            for r in range(3):
                lanes = slice(128 * (window_start(slab) + r), 128 * (window_start(slab) + r + 1))
                grow[0:1, lanes] = grow[0:1, lanes] + g2[slab, r : r + 1, :]

    def apply_gain():
        def one(r, _):
            rows = pl.ds(pl.multiple_of(32 * r, 32), 32)
            normed = hid[rows, :].astype(F32) * invb[rows, 0:1]
            nbg[rows, :] = (normed * grow[0:1, :]).astype(BF16)
            return 0

        lax.fori_loop(0, TOK // 32, one, 0)

    def nx_nb(core, half):
        ref = nbx.at[core, pl.ds(half * TOK // 2, TOK // 2)]
        return remote(ref, ref, nx_s.at[half], nx_r.at[half], twin)

    def nx_gv(core):
        return remote(gx.at[core], gx.at[core], nx_s.at[2], nx_r.at[2], twin)

    def weight_terms(core, lo, hi):
        columns = pl.ds(pl.multiple_of(HALF * c, 128), HALF)

        def one(k, _):
            feats = pl.ds(pl.multiple_of(256 * k, 256), 256)
            terms = lax.dot_general(
                nbx[core, :, feats], gx[core, :, columns], (((0,), (0,)), ((), ())), preferred_element_type=F32
            )
            dw[feats, :] = terms if core is c else dw[feats, :] + terms
            return 0

        lax.fori_loop(lo, hi, one, 0)

    def term(slab, yy, row, count):
        base = pl.multiple_of(CHIP * (NY * slab + yy), 8)
        parts, end = [], row + count
        while row < end:
            q, r = row // CHIP, row % CHIP
            count = min(CHIP - r, end - row)
            parts.append(dw[pl.ds(base + r, count), 128 * q : 128 * (q + 1)])
            row += count
        return jnp.concatenate(parts, axis=0)

    def far_copy(kind, slab):
        return remote(
            s1.at[slab, kind], r1.at[slab, kind], ry_s.at[kind, slab], ry_r.at[kind, slab], right if kind == 0 else left
        )

    def near_copy(kind, slab):
        return remote(
            s2.at[slab, kind], r2.at[slab, kind], ry_s.at[2 + kind, slab], ry_r.at[2 + kind, slab],
            right if kind == 0 else left,
        )

    def chain_copy(direction, slab):
        return remote(
            sz.at[slab], rz.at[direction, slab], rz_s.at[direction, slab], rz_r.at[direction, slab],
            up_two if direction == 0 else down_two,
        )

    def pair_copy(slab):
        return remote(sp.at[slab // 2], rp.at[slab // 2], rp_s.at[slab // 2], rp_r.at[slab // 2], mate)

    def reduce_pair(i):
        slab = order(z, 2 * i)
        sp[slab // 2] = racc[slab].astype(BF16)
        pair_copy(slab).start()

    def reduce_pair_wait(i):
        slab = order(z, 2 * i + 1)
        pair_copy(slab).wait_recv()
        racc[slab] = racc[slab] + rp[slab // 2].astype(F32)

    def chain_v_copy(direction, slab, yy):
        return remote(
            vz.at[slab, yy], rv.at[direction, slab, yy], rv_s.at[direction, slab, yy], rv_r.at[direction, slab, yy],
            up if direction == 0 else down,
        )

    def reduce_far(s):
        slab = order(z, s)
        for kind in range(2):
            s1[slab, kind] = term(slab, yo, ZH * kind, ZH).astype(BF16)
            far_copy(kind, slab).start()

    def reduce_near(s):
        slab = order(z, s)
        for kind, yy in ((0, yr), (1, yl)):
            far_copy(kind, slab).wait_recv()
            s2[slab, kind, kind] = (term(slab, yy, ZH * kind, ZH) + r1[slab, kind].astype(F32)).astype(BF16)
            s2[slab, kind, 1 - kind] = term(slab, yy, ZH * (1 - kind), ZH).astype(BF16)
            near_copy(kind, slab).start()

    def reduce_row(s):
        slab = order(z, s)
        near_copy(0, slab).wait_recv()
        near_copy(1, slab).wait_recv()
        for p in range(2):
            racc[slab, p] = term(slab, y, ZH * p, ZH) + r2[slab, 0, p].astype(F32) + r2[slab, 1, p].astype(F32)

    def reduce_chain(u):
        reduce_pair_wait(u)
        if u == pairs - 1:
            for direction, here in ((0, pair > 0), (1, pair < pairs - 1)):
                @pl.when(here)
                def _():
                    chain_copy(direction, z).wait_recv()
                    racc[z] = racc[z] + rz[direction, z].astype(F32)

            return

        far = pairs - 1 - u
        for direction, slab, here, later in (
            (0, z + 2 * far, pair <= u, pair > 0), (1, z - 2 * far, pair >= far, pair < pairs - 1),
        ):
            @pl.when(here)
            def _():
                @pl.when(later)
                def _():
                    chain_copy(direction, slab).wait_recv()
                    sz[slab] = (racc[slab] + rz[direction, slab].astype(F32)).astype(BF16)

                @pl.when(jnp.logical_not(later))
                def _():
                    sz[slab] = racc[slab].astype(BF16)

                chain_copy(direction, slab).start()

    def reduce_v(u):
        if u == NZ - 1:
            for k in (2, 1, 3, 0):
                yy = (y + k) % NY
                vacc[k] = term(z, yy, 2 * ZH, VR)
                for direction, here in ((0, z > 0), (1, z < NZ - 1)):
                    @pl.when(here)
                    def _():
                        chain_v_copy(direction, z, yy).wait_recv()
                        vacc[k] = vacc[k] + rv[direction, z, yy].astype(F32)

                if k == 2:
                    vs1[...] = vacc[2].astype(BF16)
                    v_far(0).start()
                    v_far(1).start()
            return

        for direction, slab, here, later in (
            (0, NZ - 1 + z - u, z <= u, z > 0), (1, z - (NZ - 1) + u, z >= NZ - 1 - u, z < NZ - 1),
        ):
            @pl.when(here)
            def _():
                for k in (2, 1, 3, 0):
                    yy = (y + k) % NY

                    @pl.when(later)
                    def _():
                        chain_v_copy(direction, slab, yy).wait_recv()
                        vz[slab, yy] = (term(slab, yy, 2 * ZH, VR) + rv[direction, slab, yy].astype(F32)).astype(BF16)

                    @pl.when(jnp.logical_not(later))
                    def _():
                        vz[slab, yy] = term(slab, yy, 2 * ZH, VR).astype(BF16)

                    chain_v_copy(direction, slab, yy).start()

    def v_far(kind):
        part = low if kind == 0 else high
        return remote(vs1.at[part], vr1.at[part], vy_s.at[kind], vy_r.at[kind], right if kind == 0 else left)

    def v_near(kind):
        return remote(vs2.at[kind], vr2.at[kind], vy_s.at[2 + kind], vy_r.at[2 + kind], right if kind == 0 else left)

    def reduce_v_near():
        v_far(0).wait_recv()
        vs2[0] = jnp.concatenate(
            [vacc[1, 0:VH] + vr1[0:VH].astype(F32), vacc[1, VH:VR]], axis=0
        ).astype(BF16)
        v_near(0).start()
        v_far(1).wait_recv()
        vs2[1] = jnp.concatenate(
            [vacc[3, 0:VH], vacc[3, VH:VR] + vr1[VH:VR].astype(F32)], axis=0
        ).astype(BF16)
        v_near(1).start()

    def reduce_v_row():
        v_near(0).wait_recv()
        v_near(1).wait_recv()
        fbuf[c, 2 * ZH : BLOCK] = vacc[0] + vr2[0].astype(F32) + vr2[1].astype(F32)

    def make_values():
        def one(n, _):
            columns = pl.ds(pl.multiple_of(256 * n, 256), 256)
            vout[:, columns] = (jnp.dot(nbg[...], w[:, columns], preferred_element_type=F32) * FACTOR).astype(BF16)
            return 0

        lax.fori_loop(0, KV // 256, one, 0)

    def input_gradient(lo, hi):
        def one(k, _):
            feats = pl.ds(pl.multiple_of(256 * k, 256), 256)
            ig[:, feats] = (
                lax.dot_general(gx[c], w[feats, :], (((1,), (1,)), ((), ())), preferred_element_type=F32) * FACTOR
            )
            return 0

        lax.fori_loop(lo, hi, one, 0)

    def hidden_gradient(lo, hi):
        def one(r, _):
            rows = pl.ds(pl.multiple_of(32 * r, 32), 32)
            inverse = invb[rows, 0:1]
            normed = hid[rows, :].astype(F32) * inverse
            grad = ig[rows, :]
            along = grad * normed
            gacc[...] += jnp.sum(along.reshape(4, 8, D), axis=0)
            gain = grow[0:1, :]
            mean = jnp.sum(along * gain, axis=-1, keepdims=True) / D
            gh[rows, :] = (inverse * (grad * gain - normed * mean)).astype(BF16)
            return 0

        lax.fori_loop(lo, hi, one, 0)

    def gain_terms():
        gain_row = jnp.sum(gacc[...], axis=0, keepdims=True)
        hsrc[...] = jnp.zeros((NZ, 8, 128), F32)
        for slab in range(NZ):
            for r in range(3):
                lanes = slice(128 * (window_start(slab) + r), 128 * (window_start(slab) + r + 1))
                hsrc[slab, r : r + 1, :] = gain_row[:, lanes]
        h1[z] = hsrc[z]
        spread_start(h1, z, z_peers, h1_s, h1_r, src=hsrc)

    def gain_second():
        spread_wait(h1, z, z_peers, h1_s, h1_r)
        h2[e] = total(h1, NZ)
        spread_start(h2, e, e_peers, h2_s, h2_r)

    def gain_step():
        spread_wait(h2, e, e_peers, h2_s, h2_r)
        window = total(h2, NE)
        gain_grad = jnp.zeros((8, ROWS), F32)
        for r in range(3):
            hot = jnp.where(spot == lane + 128 * r, 1.0, 0.0)
            gain_grad = gain_grad + lax.dot_general(
                jnp.broadcast_to(window[r : r + 1], (8, 128)), hot, (((1,), (1,)), ((), ())),
                precision=lax.Precision.HIGHEST, preferred_element_type=F32,
            )
        newg_ref[...] = gains_ref[...] - gain_rate * gain_grad[0:1]
        out(3).start()

    def snapshot_second():
        snap_x_arrival(1).wait_recv()
        snap_x_arrival(2).wait_recv()
        szh[zh] = total(sx, NX)
        szh_copy(zh).start()

    def szh_copy(half):
        return remote(szh.at[half], szh.at[half], szh_s, szh_r, zh_peer)

    def outer_step():
        outer_in.wait()
        mom_in.wait()
        szh_copy(1 - zh).wait_recv()
        change = outer_ref[...] - (szh[0] + szh[1])[0:ROWS] / (2 * NX)
        new_moment = momentum * mom_ref[...] + change
        newm_ref[...] = new_moment
        newo_ref[...] = outer_ref[...] - outer_rate * (change + momentum * new_moment)
        out(4).start()
        out(5).start()

    def last(core):
        return remote(fbuf.at[core], fbuf.at[core], f_s, f_r, twin)

    def inner_step():
        last(1 - c).wait_recv()
        row_of = lax.broadcasted_iota(jnp.int32, (ROWS, ROWS), 0)
        column_of = lax.broadcasted_iota(jnp.int32, (ROWS, ROWS), 1)
        gain_bf = jnp.broadcast_to(gains_ref[...].astype(BF16).astype(F32), (ROWS, ROWS))
        scale = jnp.sum(jnp.where(row_of == column_of, gain_bf, 0.0), axis=1, keepdims=True) * FACTOR
        for core in range(2):
            @pl.when(c == core)
            def _():
                for j in range(FRAGS):
                    row = CHIP * (j % 4) + ROWS * core
                    grad = fbuf[j // 4, row : row + ROWS, :] * scale
                    inner = w_ref[own_columns(j), :] - inner_rate * grad
                    mixed = mixing * inner + (1.0 - mixing) * newo_ref[...]
                    neww_ref[own_columns(j), :] = jnp.where(frag_ref[0] == j, mixed, inner)

        out(2).start()

    results = (
        (vout, values_hbm), (gh, gh_hbm), (neww_ref, neww_hbm), (newg_ref, newg_hbm), (newo_ref, newo_hbm),
        (newm_ref, newm_hbm),
    )

    def out(index):
        return pltpu.make_async_copy(results[index][0], results[index][1], out_sem.at[index])

    def drain():
        for t in range(NZ):
            for direction, slab, here in (
                (0, z - t, jnp.logical_and(z - t >= 0, z < NZ - 1)), (1, z + t, jnp.logical_and(z + t <= NZ - 1, z > 0)),
            ):
                @pl.when(here)
                def _():
                    gain_z(direction, slab).wait_send()
                    for yy in range(NY):
                        v_copy(direction, slab, yy).wait_send()

        for t in range(pairs):
            for direction, slab, here in (
                (0, z - 2 * t, jnp.logical_and(pair >= t, pair < pairs - 1)),
                (1, z + 2 * t, jnp.logical_and(pair + t < pairs, pair > 0)),
            ):
                @pl.when(here)
                def _():
                    z_copy(direction, slab).wait_send()

        def one(slab, _):
            for kind in range(4):
                y_copy(kind, slab).wait_send()
            twin_copy(slab, c).wait_send()
            for kind in range(2):
                far_copy(kind, slab).wait_send()
                near_copy(kind, slab).wait_send()

            for direction, here in ((0, slab > z), (1, slab < z)):
                @pl.when(here)
                def _():
                    for yy in range(NY):
                        chain_v_copy(direction, slab, yy).wait_send()

                @pl.when(jnp.logical_and(here, slab % 2 == z % 2))
                def _():
                    chain_copy(direction, slab).wait_send()

            @pl.when(slab % 2 == z % 2)
            def _():
                mate_copy(slab).wait_send()

            @pl.when(slab % 2 != z % 2)
            def _():
                pair_copy(slab).wait_send()

            return 0

        lax.fori_loop(0, NZ, one, 0)
        for kind in range(4):
            vy_copy(kind).wait_send()
        for kind in range(2):
            v_far(kind).wait_send()
            v_near(kind).wait_send()
        nx_nb(c, 0).wait_send()
        nx_nb(c, 1).wait_send()
        nx_gv(c).wait_send()
        last(c).wait_send()
        szh_copy(zh).wait_send()
        gain_twin(c).wait_send()
        for kind in range(3):
            gain_y(kind).wait_send()
            snap_x(kind).wait_send()
        spread_done(h1, z, z_peers, h1_s, h1_r, src=hsrc)

    place_gains()
    pack_own()
    barrier_wait()
    gain_twin(c).start()
    gather_own()
    pass_token(0)
    gv_in.wait()
    nx_gv(c).start()
    hid_in.wait()
    normalise(0, 4)
    nx_nb(c, 0).start()
    normalise(4, 8)
    nx_nb(c, 1).start()
    gain_chip()
    place_snapshot()
    gather_near()
    weight_terms(c, 0, 5)
    gather_far()
    gather_mate(0)
    gather_z(1)
    weight_terms(c, 5, 9)
    gather_v(1)
    gather_y(0)
    pass_token(1)
    gain_near()
    nx_gv(1 - c).wait_recv()
    nx_nb(1 - c, 0).wait_recv()
    nx_nb(1 - c, 1).wait_recv()
    weight_terms(1 - c, 0, 5)
    gather_y(1)
    gather_mate(1)
    weight_terms(1 - c, 5, 9)
    gather_z(2)
    gather_v(2)
    reduce_v(0)
    reduce_far(0)
    reduce_far(1)
    gain_slab()
    snapshot_near()
    pass_token(2)
    gather_v(3)
    gather_y(2)
    gather_mate(2)
    gather_twin(0)
    reduce_v(1)
    gather_z(3)
    gather_y(3)
    gather_twin(1)
    reduce_near(0)
    reduce_near(1)
    reduce_far(2)
    reduce_far(3)
    pass_token(3)
    gather_gain(1)
    gather_v(4)
    reduce_v(2)
    gather_mate(3)
    gather_y(4)
    gather_twin(2)
    reduce_row(0)
    reduce_row(1)
    reduce_pair(0)
    reduce_near(2)
    reduce_near(3)
    pass_token(4)
    gather_gain(2)
    gather_v(5)
    reduce_v(3)
    gather_y(5)
    gather_twin(3)
    reduce_far(4)
    reduce_far(5)
    reduce_chain(0)
    pass_token(5)
    gather_gain(3)
    gather_v(6)
    reduce_v(4)
    gather_y(6)
    gather_twin(4)
    unpack(0, 2)
    reduce_row(2)
    reduce_row(3)
    reduce_pair(1)
    reduce_near(4)
    reduce_near(5)
    reduce_far(6)
    reduce_far(7)
    pass_token(6)
    gather_gain(4)
    gather_v(7)
    gather_y(7)
    gather_twin(5)
    reduce_v(5)
    reduce_chain(1)
    pass_token(7)
    snapshot_second()
    gather_twin(6)
    unpack(2, 4)
    reduce_row(4)
    reduce_row(5)
    reduce_pair(2)
    reduce_near(6)
    reduce_near(7)
    gather_gain(5)
    gather_twin(7)
    reduce_v(6)
    gather_gain(6)
    unpack(4, 6)
    reduce_chain(2)
    gather_gain(7)
    gain_vector()
    reduce_v(7)
    apply_gain()
    reduce_row(6)
    reduce_row(7)
    reduce_pair(3)
    unpack(6, 8)
    input_gradient(0, 5)
    reduce_v_near()
    input_gradient(5, 9)
    reduce_chain(3)
    fbuf[c, 0 : 2 * ZH] = racc[z].reshape(2 * ZH, 128)
    gacc[...] = jnp.zeros((8, D), F32)
    hidden_gradient(0, 8)
    out(1).start()
    gain_terms()
    reduce_v_row()
    last(c).start()
    make_values()
    out(0).start()
    outer_step()
    inner_step()
    gain_second()
    drain()
    gain_step()
    spread_done(h2, e, e_peers, h2_s, h2_r)
    for index in range(6):
        out(index).wait()


def place_kernel(*refs):
    sources, targets, held, in_sem, out_sem = refs[:6], refs[6:12], refs[12:18], refs[18], refs[19]
    arrive = [pltpu.make_async_copy(s, t, in_sem.at[i]) for i, (s, t) in enumerate(zip(sources, held))]
    leave = [pltpu.make_async_copy(s, t, out_sem.at[i]) for i, (s, t) in enumerate(zip(held, targets))]
    for copy in arrive:
        copy.start()
    for one, other in zip(arrive, leave):
        one.wait()
        other.start()
    for copy in leave:
        copy.wait()


def body(hidden, grad_values, weights, gains, snapshot, outer_frag, outer_moment, fragment_index):
    anywhere = pl.BlockSpec(memory_space=pl.ANY)
    dma = pltpu.SemaphoreType.DMA
    vmem = pltpu.VMEM
    shapes = (
        jax.ShapeDtypeStruct((TOK, KV), BF16),
        jax.ShapeDtypeStruct((TOK, D), BF16),
        jax.ShapeDtypeStruct((ROWS * FRAGS, 128), F32),
        jax.ShapeDtypeStruct((1, ROWS), F32),
        jax.ShapeDtypeStruct((ROWS, FW), F32),
        jax.ShapeDtypeStruct((ROWS, FW), F32),
    )
    results = pl.pallas_call(
        step_kernel,
        out_shape=shapes,
        in_specs=[pl.BlockSpec(memory_space=pltpu.SMEM)] + [anywhere] * 7,
        out_specs=(anywhere,) * 6,
        scratch_shapes=[
            vmem((TOK, D), BF16),
            vmem((2, TOK, KV), BF16),
            vmem((2, TOK, D), BF16),
            vmem((TOK, D), BF16),
            vmem((2, NZ, NY, BLOCK, 128), BF16),
            vmem((D, KV), BF16),
            vmem((SLAB, KV), F32),
            vmem((BLOCK, 128), F32),
            vmem((D, HALF), F32),
            vmem((NZ, 2, ZH, 128), BF16),
            vmem((NZ, 2, ZH, 128), BF16),
            vmem((NZ, 2, 2, ZH, 128), BF16),
            vmem((NZ, 2, 2, ZH, 128), BF16),
            vmem((NZ, 2, ZH, 128), F32),
            vmem((NZ // 2, 2, ZH, 128), BF16),
            vmem((NZ // 2, 2, ZH, 128), BF16),
            vmem((NZ, 2, ZH, 128), BF16),
            vmem((2, NZ, 2, ZH, 128), BF16),
            vmem((NY, VR, 128), F32),
            vmem((VR, 128), BF16),
            vmem((VR, 128), BF16),
            vmem((2, VR, 128), BF16),
            vmem((2, VR, 128), BF16),
            vmem((NZ, NY, VR, 128), BF16),
            vmem((2, NZ, NY, VR, 128), BF16),
            vmem((2, BLOCK, 128), F32),
            vmem((TOK, D), F32),
            vmem((TOK, KV), BF16),
            vmem((TOK, D), BF16),
            vmem((TOK, 128), F32),
            vmem((8, D), F32),
            vmem((8, D), F32),
            vmem((2, 8, 128), F32),
            vmem((NY, 8, 128), F32),
            vmem((NZ, 8, 128), F32),
            vmem((NZ, 8, 128), F32),
            vmem((NZ, 8, 128), F32),
            vmem((NE, 8, 128), F32),
            vmem((NX, 40, 128), F32),
            vmem((2, 40, 128), F32),
            vmem((ROWS * FRAGS, 128), F32),
            vmem((1, ROWS), F32),
            vmem((ROWS, 1, FW), F32),
            vmem((ROWS, FW), F32),
            vmem((ROWS, FW), F32),
            vmem((ROWS * FRAGS, 128), F32),
            vmem((1, ROWS), F32),
            vmem((ROWS, FW), F32),
            vmem((ROWS, FW), F32),
            dma((7,)), dma((6,)),
            dma((2, NZ)), dma((2, NZ)),
            dma((NZ,)), dma((NZ,)),
            dma((2, NZ, NY)), dma((2, NZ, NY)),
            dma((4, NZ)), dma((4, NZ)),
            dma((4,)), dma((4,)),
            dma((NZ,)), dma((NZ,)),
            dma((3,)), dma((3,)),
            dma((4, NZ)), dma((4, NZ)),
            dma((NZ // 2,)), dma((NZ // 2,)),
            dma((2, NZ)), dma((2, NZ)),
            dma((2, NZ, NY)), dma((2, NZ, NY)),
            dma((4,)), dma((4,)),
            dma, dma,
            dma, dma,
            dma((3,)), dma((3,)),
            dma((2, NZ)), dma((2, NZ)),
            dma((NZ,)), dma((NZ,)),
            dma((NE,)), dma((NE,)),
            dma((3,)), dma((3,)),
            dma, dma,
            pltpu.SemaphoreType.REGULAR((7,)),
        ],
        compiler_params=pltpu.CompilerParams(
            collective_id=0, has_side_effects=True, vmem_limit_bytes=56 * 1024 * 1024
        ),
        cost_estimate=pl.CostEstimate(flops=3 * 2 * TOK * D * KV, bytes_accessed=4_000_000, transcendentals=0),
    )(
        fragment_index, hidden, grad_values, weights.reshape(ROWS * FRAGS, 128), gains,
        snapshot.reshape(ROWS, 1, FW), outer_frag, outer_moment,
    )
    values, grad_hidden, new_weights, new_gains, new_outer, new_moment = pl.pallas_call(
        place_kernel,
        out_shape=shapes,
        in_specs=[anywhere] * 6,
        out_specs=(anywhere,) * 6,
        scratch_shapes=[vmem(shape.shape, shape.dtype) for shape in shapes] + [dma((6,)), dma((6,))],
        compiler_params=pltpu.CompilerParams(vmem_limit_bytes=60 * 1024 * 1024),
    )(*results)
    return (values, grad_hidden, new_weights.reshape(1, ROWS, KV), new_gains, new_outer, new_moment)


def solution(mesh):
    return jax.shard_map(
        body,
        mesh=mesh,
        in_specs=(
            P(("group", "fsdp"), None),
            P(("group", "fsdp"), None),
            P("group", "fsdp", None),
            P("group", "fsdp"),
            P("group", "fsdp", None),
            P("fsdp", None),
            P("fsdp", None),
            P(),
        ),
        out_specs=(
            P(("group", "fsdp"), None),
            P(("group", "fsdp"), None),
            P("group", "fsdp", None),
            P("group", "fsdp"),
            P("fsdp", None),
            P("fsdp", None),
        ),
        check_vma=False,
    )
```

```python
import functools

import jax
import jax.numpy as jnp
from jax import lax
from jax.experimental import pallas as pl
from jax.experimental.pallas import tpu as pltpu
from jax.sharding import PartitionSpec as P

MESH = pl.DeviceIdType.MESH
F32 = jnp.float32
BF16 = jnp.bfloat16

D = 2304
KV = 1024
FW = 128
FRAGS = 8
TOK = 256
NZ = 8
NY = 4
NE = 8
NX = 4
ROWS = 36
CHIP = 72
SLAB = 288
HALF = 512

epsilon = 1e-06
inner_rate = 0.05
gain_rate = 0.002
momentum = 0.9
outer_rate = 0.7
mixing = 0.5
FACTOR = D ** (-0.5)
BLOCK = 288
AH = BLOCK // 2
ZH = 112
VR = 64
VH = VR // 2


def window_start(z):
    return (SLAB * z) // 128


def order(z, s):
    pair, odd = z // 2, z % 2
    near = 3 - s // 2
    low = jnp.where(pair % 3 == 0, near, jnp.where(near < 2, 1 - near, near))
    which = jnp.where(pair > 1, 3 - low, low)
    return 2 * which + jnp.where(s % 2 == 0, 1 - odd, odd)


def step_kernel(
    frag_ref, hid_hbm, gv_hbm, w_hbm, gains_hbm, snap_hbm, outer_hbm, mom_hbm,
    values_hbm, gh_hbm, neww_hbm, newg_hbm, newo_hbm, newm_hbm,
    hid, gx, nbx, nbg, wp, w, stage, pack, dw, s1, r1, s2, r2, racc, sp, rp, sz, rz,
    vacc, vs1, vr1, vs2, vr2, vz, rv, fbuf,
    ig, vf, vout, gh, invb, grow, gacc, g0, g1, g2, hsrc, h1, h2, sx, szh,
    w_ref, gains_ref, snap_ref, outer_ref, mom_ref, neww_ref, newg_ref, newo_ref, newm_ref,
    in_sem, out_sem, agz_s, agz_r, agp_s, agp_r, ay_s, ay_r, tw_s, tw_r, nx_s, nx_r,
    ry_s, ry_r, rp_s, rp_r, rz_s, rz_r, rv_s, rv_r, vy_s, vy_r, f_s, f_r,
    g0_s, g0_r, g1_s, g1_r, g2_s, g2_r, gm_s, gm_r, h1_s, h1_r, h2_s, h2_r, sx_s, sx_r, szh_s, szh_r, token,
):
    g = lax.axis_index("group")
    f = lax.axis_index("fsdp")
    x, zh = g // 2, g % 2
    z, e = f // NE, f % NE
    y, c = e // 2, e % 2
    yr, yl, yo = (y + 1) % NY, (y + 3) % NY, (y + 2) % NY
    twin = (g, f + 1 - 2 * c)

    def at(zz, yy):
        return (g, zz * NE + yy * 2 + c)

    right, left = at(z, yr), at(z, yl)
    up, down = at(z + 1, y), at(z - 1, y)
    mate, up_two, down_two = at(z + 1 - 2 * (z % 2), y), at(z + 2, y), at(z - 2, y)
    pair, z_mate = z // 2, z + 1 - 2 * (z % 2)
    pairs = NZ // 2
    e_peers = [((e + k) % NE, (g, z * NE + (e + k) % NE)) for k in range(1, NE)]
    z_peers = [((z + k) % NZ, (g, ((z + k) % NZ) * NE + e)) for k in range(1, NZ)]
    xr, xl, xo = (x + 1) % NX, (x + 3) % NX, (x + 2) % NX
    x_right, x_left = (xr * 2 + zh, f), (xl * 2 + zh, f)
    after = (x * 2 + (zh + (z + 1) // NZ) % 2, ((z + 1) % NZ) * NE + e)
    before = (x * 2 + (zh + (NZ - z) // NZ) % 2, ((z + NZ - 1) % NZ) * NE + e)
    zh_peer = (x * 2 + 1 - zh, f)

    def remote(src, dst, send, recv, device):
        return pltpu.make_async_remote_copy(
            src_ref=src, dst_ref=dst, send_sem=send, recv_sem=recv, device_id=device, device_id_type=MESH
        )

    def received(ref, sem):
        remote(ref, ref, sem, sem, twin).wait_recv()

    def sent(ref, sem):
        remote(ref, ref, sem, sem, twin).wait_send()

    barrier = pltpu.get_barrier_semaphore()
    peers = [before, after, right, left, x_right, x_left, twin]
    two_after, two_before = at((z + 2) % NZ, y), at((z + NZ - 2) % NZ, y)
    peers += [two_after, two_before]
    for peer in peers:
        pl.semaphore_signal(barrier, inc=1, device_id=peer, device_id_type=MESH)

    w_in = pltpu.make_async_copy(w_hbm, w_ref, in_sem.at[0])
    gains_in = pltpu.make_async_copy(gains_hbm, gains_ref, in_sem.at[1])
    snap_in = pltpu.make_async_copy(snap_hbm, snap_ref, in_sem.at[2])
    hid_in = pltpu.make_async_copy(hid_hbm, hid, in_sem.at[3])
    gv_in = pltpu.make_async_copy(gv_hbm, gx.at[c], in_sem.at[4])
    outer_in = pltpu.make_async_copy(outer_hbm, outer_ref, in_sem.at[5])
    mom_in = pltpu.make_async_copy(mom_hbm, mom_ref, in_sem.at[6])
    for copy in (gains_in, w_in, hid_in, gv_in, snap_in, outer_in, mom_in):
        copy.start()

    def own_columns(j):
        return pl.ds(j, ROWS, stride=FRAGS)

    def pack_own():
        w_in.wait()
        for q in range(FRAGS):
            pack[ROWS * q : ROWS * (q + 1), :] = w_ref[own_columns(q), :]
        wp[c, z, y] = pack[...].astype(BF16)

    first_lane = ROWS * f - 128 * window_start(z)
    spot = lax.broadcasted_iota(jnp.int32, (ROWS, 128), 0) + first_lane
    lane = lax.broadcasted_iota(jnp.int32, (ROWS, 128), 1)

    def place_gains():
        gains_in.wait()
        gain_own = jnp.broadcast_to(gains_ref[...].astype(BF16), (8, ROWS))
        g0[c] = jnp.zeros((8, 128), F32)
        for r in range(3):
            hot = jnp.where(spot == lane + 128 * r, 1.0, 0.0).astype(BF16)
            g0[c, r : r + 1, :] = jnp.dot(gain_own, hot, preferred_element_type=F32)[0:1]

    def gain_twin(core):
        return remote(g0.at[core], g0.at[core], g0_s, g0_r, twin)

    def gain_y(kind):
        row = y if kind < 2 else yl
        return remote(
            g1.at[row], g1.at[row], g1_s, g1_r.at[0 if kind == 0 else 1], left if kind == 1 else right
        )

    def gain_z(direction, slab):
        ref = g2.at[slab]
        return remote(
            ref, ref, g2_s.at[direction, slab // 2], g2_r.at[slab // 2], up_two if direction == 0 else down_two
        )

    def gain_mate(slab):
        return remote(g2.at[slab], g2.at[slab], gm_s, gm_r, mate)

    def gain_chip():
        gain_twin(1 - c).wait_recv()
        g1[y] = g0[0] + g0[1]
        gain_y(0).start()
        gain_y(1).start()

    def gain_near():
        received(g1.at[yl], g1_r.at[0])
        gain_y(2).start()

    def gain_slab():
        received(g1.at[pl.ds(0, 2)], g1_r.at[1])
        g2[z] = total(g1, NY)
        both_ways_two(lambda direction: gain_z(direction, z).start())
        gain_mate(z).start()

    def gather_gain(t):
        for direction, slab, here, more in (
            (0, z - 2 * t, pair >= t, pair < pairs - 1), (1, z + 2 * t, pair + t < pairs, pair > 0),
        ):
            @pl.when(here)
            def _():
                gain_z(direction, slab).wait_recv()

                @pl.when(more)
                def _():
                    gain_z(direction, slab).start()

                gain_mate(slab).start()

    def gain_all():
        received(g2.at[pl.ds(0, pairs)], gm_r)

    def snap_x(kind):
        row = x if kind < 2 else xl
        return remote(
            sx.at[row], sx.at[row], sx_s, sx_r.at[0 if kind == 0 else 1], x_left if kind == 1 else x_right
        )

    def place_snapshot():
        snap_in.wait()
        sx[x] = jnp.zeros((40, 128), F32)
        sx[x, 0:ROWS, :] = snap_ref[...].reshape(ROWS, 128)
        snap_x(0).start()
        snap_x(1).start()

    def snapshot_near():
        received(sx.at[xl], sx_r.at[0])
        snap_x(2).start()

    def pass_token(t):
        if t > 0:
            pl.semaphore_wait(token.at[t - 1], 1)
        if t < NZ - 1:
            pl.semaphore_signal(token.at[t], inc=1, device_id=after, device_id_type=MESH)

    def barrier_wait():
        pl.semaphore_wait(barrier, len(peers))

    def spread_start(buf, own, peer_list, send, recv):
        for _, peer in peer_list:
            remote(buf.at[own], buf.at[own], send, recv, peer).start()

    def total(buf, count):
        result = buf[0]
        for index in range(1, count):
            result = result + buf[index]
        return result

    halves = (pl.ds(0, AH), pl.ds(AH, AH))

    def z_copy(direction, slab):
        ref = wp.at[c, slab, y]
        return remote(
            ref, ref, agz_s.at[direction, slab // 2], agz_r.at[slab // 2], up_two if direction == 0 else down_two
        )

    def mate_copy(slab):
        ref = wp.at[c, slab, y]
        return remote(ref, ref, agp_s, agp_r.at[slab // 2], mate)

    def y_copy(kind, slab):
        device = right if kind in (0, 2) else left
        if kind < 2:
            ref = wp.at[c, slab, y]
        elif kind == 2:
            ref = wp.at[c, slab, yl, halves[0]]
        else:
            ref = wp.at[c, slab, yr, halves[1]]
        return remote(ref, ref, ay_s, ay_r.at[kind // 2, slab], device)

    low, high = pl.ds(0, VH), pl.ds(VH, VH)

    def twin_copy(slab, core):
        return remote(wp.at[core, slab], wp.at[core, slab], tw_s, tw_r.at[slab], twin)

    def both_ways_two(send):
        @pl.when(pair < pairs - 1)
        def _():
            send(0)

        @pl.when(pair > 0)
        def _():
            send(1)

    def gather_own():
        both_ways_two(lambda direction: z_copy(direction, z).start())
        y_copy(0, z).start()
        y_copy(1, z).start()
        mate_copy(z).start()

    def gather_z(t):
        for direction, slab, here, more in (
            (0, z - 2 * t, pair >= t, pair < pairs - 1), (1, z + 2 * t, pair + t < pairs, pair > 0),
        ):
            @pl.when(here)
            def _():
                z_copy(direction, slab).wait_recv()

                @pl.when(more)
                def _():
                    z_copy(direction, slab).start()

                mate_copy(slab).start()
                y_copy(0, slab).start()
                y_copy(1, slab).start()

    def gather_mate(t):
        sides = ((z_mate, pair >= 0),) if t == 0 else ((z_mate - 2 * t, pair >= t), (z_mate + 2 * t, pair + t < pairs))
        for slab, here in sides:
            @pl.when(here)
            def _():
                mate_copy(slab).wait_recv()
                y_copy(0, slab).start()
                y_copy(1, slab).start()

    def gather_y(j):
        slab = order(z, 7 - j)
        received(wp.at[c, slab, pl.ds(0, 2)], ay_r.at[0, slab])
        y_copy(2, slab).start()
        y_copy(3, slab).start()

    def gather_twin(j):
        slab = order(z, 7 - j)
        received(wp.at[c, slab, yo], ay_r.at[1, slab])
        twin_copy(slab, c).start()

    def unpack(lo, hi):
        def one(j, _):
            slab = order(z, 7 - j)
            twin_copy(slab, 1 - c).wait_recv()
            for core in range(2):
                for yy in range(NY):
                    block = wp[core, slab, yy].astype(F32)
                    base = ROWS * (2 * yy + core)
                    for q in range(FRAGS):
                        stage[base : base + ROWS, 128 * q : 128 * (q + 1)] = block[ROWS * q : ROWS * (q + 1)]
            w[pl.ds(pl.multiple_of(SLAB * slab, 16), SLAB), :] = stage[...].astype(BF16)
            return 0

        lax.fori_loop(lo, hi, one, 0)

    def normalise(lo, hi):
        def one(r, _):
            rows = pl.ds(pl.multiple_of(32 * r, 32), 32)
            tokens = hid[rows, :].astype(F32)
            inverse = lax.rsqrt(jnp.sum(tokens * tokens, axis=-1, keepdims=True) / D + epsilon)
            invb[rows, :] = jnp.broadcast_to(inverse, (32, 128))
            nbx[c, rows, :] = (tokens * inverse).astype(BF16)
            return 0

        lax.fori_loop(lo, hi, one, 0)

    def gain_vector():
        grow[...] = jnp.zeros((8, D), F32)
        for slab in range(NZ):
            for r in range(3):
                lanes = slice(128 * (window_start(slab) + r), 128 * (window_start(slab) + r + 1))
                grow[0:1, lanes] = grow[0:1, lanes] + g2[slab, r : r + 1, :]

    def apply_gain():
        def one(r, _):
            rows = pl.ds(pl.multiple_of(32 * r, 32), 32)
            normed = hid[rows, :].astype(F32) * invb[rows, 0:1]
            nbg[rows, :] = (normed * grow[0:1, :]).astype(BF16)
            return 0

        lax.fori_loop(0, TOK // 32, one, 0)

    def nx_nb(core, half):
        ref = nbx.at[core, pl.ds(half * TOK // 2, TOK // 2)]
        return remote(ref, ref, nx_s.at[0], nx_r.at[0], twin)

    def nx_gv(core):
        return remote(gx.at[core], gx.at[core], nx_s.at[1], nx_r.at[1], twin)

    def weight_terms(core, lo, hi):
        columns = pl.ds(pl.multiple_of(HALF * c, 128), HALF)

        def one(k, _):
            feats = pl.ds(pl.multiple_of(256 * k, 256), 256)
            terms = lax.dot_general(
                nbx[core, :, feats], gx[core, :, columns], (((0,), (0,)), ((), ())), preferred_element_type=F32
            )
            dw[feats, :] = terms if core is c else dw[feats, :] + terms
            return 0

        lax.fori_loop(lo, hi, one, 0)

    def term(slab, yy, row, count):
        base = pl.multiple_of(CHIP * (NY * slab + yy), 8)
        parts, end = [], row + count
        while row < end:
            q, r = row // CHIP, row % CHIP
            count = min(CHIP - r, end - row)
            parts.append(dw[pl.ds(base + r, count), 128 * q : 128 * (q + 1)])
            row += count
        return jnp.concatenate(parts, axis=0)

    def far_copy(kind, slab):
        return remote(
            s1.at[slab, kind], r1.at[slab, kind], ry_s.at[0], ry_r.at[0, slab], right if kind == 0 else left
        )

    def near_copy(kind, slab):
        return remote(
            s2.at[slab, kind], r2.at[slab, kind], ry_s.at[1], ry_r.at[1, slab],
            right if kind == 0 else left,
        )

    def chain_copy(direction, slab):
        return remote(
            sz.at[slab], rz.at[direction, slab], rz_s, rz_r.at[direction, slab // 2],
            up_two if direction == 0 else down_two,
        )

    def pair_copy(slab):
        return remote(sp.at[slab // 2], rp.at[slab // 2], rp_s, rp_r.at[slab // 2], mate)

    def reduce_pair(i):
        slab = order(z, 2 * i)
        sp[slab // 2] = racc[slab].astype(BF16)
        pair_copy(slab).start()

    def reduce_pair_wait(i):
        slab = order(z, 2 * i + 1)
        pair_copy(slab).wait_recv()
        racc[slab] = racc[slab] + rp[slab // 2].astype(F32)

    def chain_v_copy(direction, slab):
        return remote(
            vz.at[slab], rv.at[direction, slab], rv_s, rv_r.at[direction, slab], up if direction == 0 else down
        )

    def reduce_far(s):
        slab = order(z, s)
        for kind in range(2):
            s1[slab, kind] = term(slab, yo, ZH * kind, ZH).astype(BF16)
            far_copy(kind, slab).start()

    def reduce_near(s):
        slab = order(z, s)
        received(r1.at[slab], ry_r.at[0, slab])
        for kind, yy in ((0, yr), (1, yl)):
            s2[slab, kind, kind] = (term(slab, yy, ZH * kind, ZH) + r1[slab, kind].astype(F32)).astype(BF16)
            s2[slab, kind, 1 - kind] = term(slab, yy, ZH * (1 - kind), ZH).astype(BF16)
            near_copy(kind, slab).start()

    def reduce_row(s):
        slab = order(z, s)
        received(r2.at[slab], ry_r.at[1, slab])
        for p in range(2):
            racc[slab, p] = term(slab, y, ZH * p, ZH) + r2[slab, 0, p].astype(F32) + r2[slab, 1, p].astype(F32)

    def reduce_chain(u):
        reduce_pair_wait(u)
        if u == pairs - 1:
            for direction, here in ((0, pair > 0), (1, pair < pairs - 1)):
                @pl.when(here)
                def _():
                    chain_copy(direction, z).wait_recv()
                    racc[z] = racc[z] + rz[direction, z].astype(F32)

            return

        far = pairs - 1 - u
        for direction, slab, here, later in (
            (0, z + 2 * far, pair <= u, pair > 0), (1, z - 2 * far, pair >= far, pair < pairs - 1),
        ):
            @pl.when(here)
            def _():
                @pl.when(later)
                def _():
                    chain_copy(direction, slab).wait_recv()
                    sz[slab] = (racc[slab] + rz[direction, slab].astype(F32)).astype(BF16)

                @pl.when(jnp.logical_not(later))
                def _():
                    sz[slab] = racc[slab].astype(BF16)

                chain_copy(direction, slab).start()

    def reduce_v(u):
        if u == NZ - 1:
            for direction, here in ((0, z > 0), (1, z < NZ - 1)):
                @pl.when(here)
                def _():
                    chain_v_copy(direction, z).wait_recv()

            for k in (2, 1, 3, 0):
                yy = (y + k) % NY
                vacc[k] = term(z, yy, 2 * ZH, VR)
                for direction, here in ((0, z > 0), (1, z < NZ - 1)):
                    @pl.when(here)
                    def _():
                        vacc[k] = vacc[k] + rv[direction, z, yy].astype(F32)

                if k == 2:
                    vs1[...] = vacc[2].astype(BF16)
                    v_far(0).start()
                    v_far(1).start()
            return

        for direction, slab, here, later in (
            (0, NZ - 1 + z - u, z <= u, z > 0), (1, z - (NZ - 1) + u, z >= NZ - 1 - u, z < NZ - 1),
        ):
            @pl.when(here)
            def _():
                @pl.when(later)
                def _():
                    chain_v_copy(direction, slab).wait_recv()
                    for yy in range(NY):
                        vz[slab, yy] = (term(slab, yy, 2 * ZH, VR) + rv[direction, slab, yy].astype(F32)).astype(BF16)

                @pl.when(jnp.logical_not(later))
                def _():
                    for yy in range(NY):
                        vz[slab, yy] = term(slab, yy, 2 * ZH, VR).astype(BF16)

                chain_v_copy(direction, slab).start()

    def v_far(kind):
        part = low if kind == 0 else high
        return remote(vs1.at[part], vr1.at[part], vy_s.at[0], vy_r.at[0], right if kind == 0 else left)

    def v_near(kind):
        return remote(vs2.at[kind], vr2.at[kind], vy_s.at[1], vy_r.at[1], right if kind == 0 else left)

    def reduce_v_near():
        received(vr1, vy_r.at[0])
        vs2[0] = jnp.concatenate(
            [vacc[1, 0:VH] + vr1[0:VH].astype(F32), vacc[1, VH:VR]], axis=0
        ).astype(BF16)
        v_near(0).start()
        vs2[1] = jnp.concatenate(
            [vacc[3, 0:VH], vacc[3, VH:VR] + vr1[VH:VR].astype(F32)], axis=0
        ).astype(BF16)
        v_near(1).start()

    def reduce_v_row():
        received(vr2, vy_r.at[1])
        fbuf[c, 2 * ZH : BLOCK] = vacc[0] + vr2[0].astype(F32) + vr2[1].astype(F32)

    near_half, far_half = z // 4, 1 - z // 4

    def make_values(half, done):
        feats = pl.ds(pl.multiple_of(D // 2 * half, 128), D // 2)

        def one(n, _):
            columns = pl.ds(pl.multiple_of(256 * n, 256), 256)
            part = jnp.dot(nbg[:, feats], w[feats, columns], preferred_element_type=F32)
            if done:
                vout[:, columns] = ((vf[:, columns] + part) * FACTOR).astype(BF16)
            else:
                vf[:, columns] = part
            return 0

        lax.fori_loop(0, KV // 256, one, 0)

    def input_gradient(half):
        def one(k, _):
            feats = pl.ds(pl.multiple_of(D // 2 * half + 384 * k, 128), 384)
            grad = lax.dot_general(gx[c], w[feats, :], (((1,), (1,)), ((), ())), preferred_element_type=F32) * FACTOR
            ig[:, feats] = grad
            normed = hid[:, feats].astype(F32) * invb[:, 0:1]
            gacc[:, feats] = jnp.sum((grad * normed).reshape(TOK // 8, 8, 384), axis=0)
            return 0

        lax.fori_loop(0, D // 2 // 384, one, 0)

    def hidden_gradient(lo, hi):
        def one(r, _):
            rows = pl.ds(pl.multiple_of(32 * r, 32), 32)
            inverse = invb[rows, 0:1]
            normed = hid[rows, :].astype(F32) * inverse
            grad = ig[rows, :]
            along = grad * normed
            gain = grow[0:1, :]
            mean = jnp.sum(along * gain, axis=-1, keepdims=True) / D
            gh[rows, :] = (inverse * (grad * gain - normed * mean)).astype(BF16)
            return 0

        lax.fori_loop(lo, hi, one, 0)

    def gain_terms(half):
        for side in range(2):
            @pl.when(half == side)
            def _():
                for slab in range(4 * side, 4 * side + 4):
                    hsrc[slab] = jnp.zeros((8, 128), F32)
                    for r in range(3):
                        lanes = slice(128 * (window_start(slab) + r), 128 * (window_start(slab) + r + 1))
                        hsrc[slab, r : r + 1, :] = jnp.sum(gacc[:, lanes], axis=0, keepdims=True)

                    @pl.when(z != slab)
                    def _():
                        remote(hsrc.at[slab], h1.at[z], h1_s, h1_r, (g, slab * NE + e)).start()

    def gain_second():
        received(h1.at[pl.ds(0, NZ - 1)], h1_r)
        h1[z] = hsrc[z]
        h2[e] = total(h1, NZ)
        spread_start(h2, e, e_peers, h2_s, h2_r)

    def gain_step():
        received(h2.at[pl.ds(0, NE - 1)], h2_r)
        window = total(h2, NE)
        gain_grad = jnp.zeros((8, ROWS), F32)
        for r in range(3):
            hot = jnp.where(spot == lane + 128 * r, 1.0, 0.0)
            gain_grad = gain_grad + lax.dot_general(
                jnp.broadcast_to(window[r : r + 1], (8, 128)), hot, (((1,), (1,)), ((), ())),
                precision=lax.Precision.HIGHEST, preferred_element_type=F32,
            )
        newg_ref[...] = gains_ref[...] - gain_rate * gain_grad[0:1]
        out(3).start()

    def snapshot_second():
        received(sx.at[pl.ds(0, 2)], sx_r.at[1])
        szh[zh] = total(sx, NX)
        szh_copy(zh).start()

    def szh_copy(half):
        return remote(szh.at[half], szh.at[half], szh_s, szh_r, zh_peer)

    def outer_step():
        outer_in.wait()
        mom_in.wait()
        szh_copy(1 - zh).wait_recv()
        change = outer_ref[...] - (szh[0] + szh[1])[0:ROWS] / (2 * NX)
        new_moment = momentum * mom_ref[...] + change
        newm_ref[...] = new_moment
        newo_ref[...] = outer_ref[...] - outer_rate * (change + momentum * new_moment)
        out(4).start()
        out(5).start()

    def last(core):
        return remote(fbuf.at[core], fbuf.at[core], f_s, f_r, twin)

    def inner_step():
        last(1 - c).wait_recv()
        row_of = lax.broadcasted_iota(jnp.int32, (ROWS, ROWS), 0)
        column_of = lax.broadcasted_iota(jnp.int32, (ROWS, ROWS), 1)
        gain_bf = jnp.broadcast_to(gains_ref[...].astype(BF16).astype(F32), (ROWS, ROWS))
        scale = jnp.sum(jnp.where(row_of == column_of, gain_bf, 0.0), axis=1, keepdims=True) * FACTOR
        for core in range(2):
            @pl.when(c == core)
            def _():
                for j in range(FRAGS):
                    row = CHIP * (j % 4) + ROWS * core
                    grad = fbuf[j // 4, row : row + ROWS, :] * scale
                    inner = w_ref[own_columns(j), :] - inner_rate * grad
                    mixed = mixing * inner + (1.0 - mixing) * newo_ref[...]
                    neww_ref[own_columns(j), :] = jnp.where(frag_ref[0] == j, mixed, inner)

        out(2).start()

    results = (
        (vout, values_hbm), (gh, gh_hbm), (neww_ref, neww_hbm), (newg_ref, newg_hbm), (newo_ref, newo_hbm),
        (newm_ref, newm_hbm),
    )

    def out(index):
        return pltpu.make_async_copy(results[index][0], results[index][1], out_sem.at[index])

    def results_wait():
        for index in range(6):
            out(index).wait()

    def drain():
        for t in range(pairs):
            for direction, slab, here in (
                (0, z - 2 * t, jnp.logical_and(pair >= t, pair < pairs - 1)),
                (1, z + 2 * t, jnp.logical_and(pair + t < pairs, pair > 0)),
            ):
                @pl.when(here)
                def _():
                    z_copy(direction, slab).wait_send()
                    gain_z(direction, slab).wait_send()

        sent(wp.at[0, 0], agp_s)
        sent(wp.at[0, pl.ds(0, 6)], ay_s)
        sent(wp.at[0], tw_s)
        sent(s1, ry_s.at[0])
        sent(s2, ry_s.at[1])
        sent(sp, rp_s)
        sent(sz.at[pl.ds(0, pairs - 1)], rz_s)
        sent(vz.at[pl.ds(0, NZ - 1)], rv_s)
        sent(vs1, vy_s.at[0])
        sent(vs2, vy_s.at[1])
        sent(nbx.at[0], nx_s.at[0])
        sent(gx.at[0], nx_s.at[1])
        sent(fbuf.at[0], f_s)
        sent(szh.at[0], szh_s)
        sent(g0.at[0], g0_s)
        sent(g1.at[pl.ds(0, 3)], g1_s)
        sent(g2.at[pl.ds(0, pairs)], gm_s)
        sent(sx.at[pl.ds(0, 3)], sx_s)
        sent(hsrc.at[pl.ds(0, NZ - 1)], h1_s)
        sent(h2.at[pl.ds(0, NE - 1)], h2_s)

    place_gains()
    pack_own()
    barrier_wait()
    gain_twin(c).start()
    gather_own()
    gv_in.wait()
    nx_gv(c).start()
    hid_in.wait()
    normalise(0, 4)
    nx_nb(c, 0).start()
    normalise(4, 8)
    nx_nb(c, 1).start()
    gain_chip()
    place_snapshot()
    weight_terms(c, 0, 5)
    weight_terms(c, 5, 9)
    gain_near()
    gather_y(0)
    gather_mate(0)
    nx_gv(1 - c).wait_recv()
    received(nbx.at[1 - c], nx_r.at[0])
    weight_terms(1 - c, 0, 5)
    gather_z(1)
    weight_terms(1 - c, 5, 9)
    reduce_v(0)
    pass_token(0)
    reduce_far(0)
    reduce_far(1)
    gain_slab()
    gather_y(1)
    gather_twin(0)
    gather_mate(1)
    gather_z(2)
    snapshot_near()
    reduce_v(1)
    pass_token(1)
    reduce_near(0)
    reduce_near(1)
    gather_y(2)
    gather_gain(1)
    gather_mate(2)
    gather_twin(1)
    reduce_v(2)
    gather_y(3)
    gather_z(3)
    pass_token(2)
    reduce_far(2)
    reduce_far(3)
    gather_twin(2)
    gather_gain(2)
    gather_y(4)
    reduce_v(3)
    gather_mate(3)
    gather_twin(3)
    pass_token(3)
    gather_y(5)
    reduce_row(0)
    reduce_row(1)
    reduce_pair(0)
    reduce_near(2)
    reduce_near(3)
    gather_gain(3)
    reduce_v(4)
    gather_twin(4)
    gather_y(6)
    unpack(0, 4)
    pass_token(4)
    reduce_far(4)
    reduce_far(5)
    reduce_chain(0)
    input_gradient(near_half)
    gain_terms(near_half)
    pass_token(5)
    gather_twin(5)
    gather_y(7)
    reduce_v(5)
    reduce_row(2)
    reduce_row(3)
    reduce_pair(1)
    reduce_near(4)
    reduce_near(5)
    pass_token(6)
    reduce_far(6)
    reduce_far(7)
    gather_twin(6)
    gather_twin(7)
    reduce_v(6)
    reduce_chain(1)
    pass_token(7)
    snapshot_second()
    gain_all()
    gain_vector()
    unpack(4, 6)
    reduce_row(4)
    reduce_row(5)
    reduce_pair(2)
    reduce_near(6)
    reduce_near(7)
    unpack(6, 8)
    input_gradient(far_half)
    gain_terms(far_half)
    reduce_v(7)
    apply_gain()
    reduce_row(6)
    reduce_row(7)
    reduce_pair(3)
    reduce_v_near()
    reduce_chain(2)
    make_values(near_half, False)
    hidden_gradient(0, 8)
    out(1).start()
    reduce_v_row()
    reduce_chain(3)
    fbuf[c, 0 : 2 * ZH] = racc[z].reshape(2 * ZH, 128)
    last(c).start()
    gain_second()
    make_values(far_half, True)
    out(0).start()
    outer_step()
    inner_step()
    drain()
    gain_step()
    results_wait()


def place_kernel(*refs):
    sources, targets, held, in_sem, out_sem = refs[:6], refs[6:12], refs[12:18], refs[18], refs[19]
    arrive = [pltpu.make_async_copy(s, t, in_sem.at[i]) for i, (s, t) in enumerate(zip(sources, held))]
    leave = [pltpu.make_async_copy(s, t, out_sem.at[i]) for i, (s, t) in enumerate(zip(held, targets))]
    for copy in arrive:
        copy.start()
    for one, other in zip(arrive, leave):
        one.wait()
        other.start()
    for copy in leave:
        copy.wait()


def body(hidden, grad_values, weights, gains, snapshot, outer_frag, outer_moment, fragment_index):
    anywhere = pl.BlockSpec(memory_space=pl.ANY)
    dma = pltpu.SemaphoreType.DMA
    vmem = pltpu.VMEM
    shapes = (
        jax.ShapeDtypeStruct((TOK, KV), BF16),
        jax.ShapeDtypeStruct((TOK, D), BF16),
        jax.ShapeDtypeStruct((ROWS * FRAGS, 128), F32),
        jax.ShapeDtypeStruct((1, ROWS), F32),
        jax.ShapeDtypeStruct((ROWS, FW), F32),
        jax.ShapeDtypeStruct((ROWS, FW), F32),
    )
    results = pl.pallas_call(
        step_kernel,
        out_shape=shapes,
        in_specs=[pl.BlockSpec(memory_space=pltpu.SMEM)] + [anywhere] * 7,
        out_specs=(anywhere,) * 6,
        scratch_shapes=[
            vmem((TOK, D), BF16),
            vmem((2, TOK, KV), BF16),
            vmem((2, TOK, D), BF16),
            vmem((TOK, D), BF16),
            vmem((2, NZ, NY, BLOCK, 128), BF16),
            vmem((D, KV), BF16),
            vmem((SLAB, KV), F32),
            vmem((BLOCK, 128), F32),
            vmem((D, HALF), F32),
            vmem((NZ, 2, ZH, 128), BF16),
            vmem((NZ, 2, ZH, 128), BF16),
            vmem((NZ, 2, 2, ZH, 128), BF16),
            vmem((NZ, 2, 2, ZH, 128), BF16),
            vmem((NZ, 2, ZH, 128), F32),
            vmem((NZ // 2, 2, ZH, 128), BF16),
            vmem((NZ // 2, 2, ZH, 128), BF16),
            vmem((NZ, 2, ZH, 128), BF16),
            vmem((2, NZ, 2, ZH, 128), BF16),
            vmem((NY, VR, 128), F32),
            vmem((VR, 128), BF16),
            vmem((VR, 128), BF16),
            vmem((2, VR, 128), BF16),
            vmem((2, VR, 128), BF16),
            vmem((NZ, NY, VR, 128), BF16),
            vmem((2, NZ, NY, VR, 128), BF16),
            vmem((2, BLOCK, 128), F32),
            vmem((TOK, D), F32),
            vmem((TOK, KV), F32),
            vmem((TOK, KV), BF16),
            vmem((TOK, D), BF16),
            vmem((TOK, 128), F32),
            vmem((8, D), F32),
            vmem((8, D), F32),
            vmem((2, 8, 128), F32),
            vmem((NY, 8, 128), F32),
            vmem((NZ, 8, 128), F32),
            vmem((NZ, 8, 128), F32),
            vmem((NZ, 8, 128), F32),
            vmem((NE, 8, 128), F32),
            vmem((NX, 40, 128), F32),
            vmem((2, 40, 128), F32),
            vmem((ROWS * FRAGS, 128), F32),
            vmem((1, ROWS), F32),
            vmem((ROWS, 1, FW), F32),
            vmem((ROWS, FW), F32),
            vmem((ROWS, FW), F32),
            vmem((ROWS * FRAGS, 128), F32),
            vmem((1, ROWS), F32),
            vmem((ROWS, FW), F32),
            vmem((ROWS, FW), F32),
            dma((7,)), dma((6,)),
            dma((2, NZ // 2)), dma((NZ // 2,)), dma, dma((NZ // 2,)),
            dma, dma((2, NZ)),
            dma, dma((NZ,)),
            dma((2,)), dma((2,)),
            dma((2,)), dma((2, NZ)),
            dma, dma((NZ // 2,)),
            dma, dma((2, NZ // 2)),
            dma, dma((2, NZ)),
            dma((2,)), dma((2,)),
            dma, dma,
            dma, dma,
            dma, dma((2,)),
            dma((2, NZ // 2)), dma((NZ // 2,)), dma, dma,
            dma, dma, dma, dma,
            dma, dma((2,)),
            dma, dma,
            pltpu.SemaphoreType.REGULAR((7,)),
        ],
        compiler_params=pltpu.CompilerParams(
            collective_id=0, has_side_effects=True, vmem_limit_bytes=56 * 1024 * 1024,
        ),
        cost_estimate=pl.CostEstimate(flops=3 * 2 * TOK * D * KV, bytes_accessed=4_000_000, transcendentals=0),
    )(
        fragment_index, hidden, grad_values, weights.reshape(ROWS * FRAGS, 128), gains,
        snapshot.reshape(ROWS, 1, FW), outer_frag, outer_moment,
    )
    values, grad_hidden, new_weights, new_gains, new_outer, new_moment = pl.pallas_call(
        place_kernel,
        out_shape=shapes,
        in_specs=[anywhere] * 6,
        out_specs=(anywhere,) * 6,
        scratch_shapes=[vmem(shape.shape, shape.dtype) for shape in shapes] + [dma((6,)), dma((6,))],
        compiler_params=pltpu.CompilerParams(vmem_limit_bytes=60 * 1024 * 1024),
    )(*results)
    return (values, grad_hidden, new_weights.reshape(1, ROWS, KV), new_gains, new_outer, new_moment)


def solution(mesh):
    return jax.shard_map(
        body,
        mesh=mesh,
        in_specs=(
            P(("group", "fsdp"), None),
            P(("group", "fsdp"), None),
            P("group", "fsdp", None),
            P("group", "fsdp"),
            P("group", "fsdp", None),
            P("fsdp", None),
            P("fsdp", None),
            P(),
        ),
        out_specs=(
            P(("group", "fsdp"), None),
            P(("group", "fsdp"), None),
            P("group", "fsdp", None),
            P("group", "fsdp"),
            P("fsdp", None),
            P("fsdp", None),
        ),
        check_vma=False,
    )
```

```python
import functools

import jax
import jax.numpy as jnp
from jax import lax
from jax.experimental import pallas as pl
from jax.experimental.pallas import tpu as pltpu
from jax.sharding import PartitionSpec as P

MESH = pl.DeviceIdType.MESH
F32 = jnp.float32
BF16 = jnp.bfloat16

D = 2304
KV = 1024
FW = 128
FRAGS = 8
TOK = 256
NZ = 8
NY = 4
NE = 8
NX = 4
ROWS = 36
CHIP = 72
SLAB = 288
HALF = 512

epsilon = 1e-06
inner_rate = 0.05
gain_rate = 0.002
momentum = 0.9
outer_rate = 0.7
mixing = 0.5
FACTOR = D ** (-0.5)
BLOCK = 288
AH = BLOCK // 2
ZH = 112
VR = 64
VH = VR // 2


def window_start(z):
    return (SLAB * z) // 128


def order(z, s):
    pair, odd = z // 2, z % 2
    near = 3 - s // 2
    low = jnp.where(pair % 3 == 0, near, jnp.where(near < 2, 1 - near, near))
    which = jnp.where(pair > 1, 3 - low, low)
    return 2 * which + jnp.where(s % 2 == 0, 1 - odd, odd)


def step_kernel(
    frag_ref, hid_hbm, gv_hbm, w_hbm, gains_hbm, snap_hbm, outer_hbm, mom_hbm,
    values_hbm, gh_hbm, neww_hbm, newg_hbm, newo_hbm, newm_hbm,
    hid, gx, nbx, nbg, wp, w, stage, pack, dw, s1, r1, s2, r2, racc, sp, rp, sz, rz,
    vacc, vs1, vr1, vs2, vr2, vz, rv, fbuf,
    ig, vf, vout, gh, invb, grow, gacc, g0, g1, g2, hsrc, h1, h2, sx, szh,
    w_ref, gains_ref, snap_ref, outer_ref, mom_ref, neww_ref, newg_ref, newo_ref, newm_ref,
    in_sem, out_sem, agz_s, agz_r, agp_s, agp_r, ay_s, ay_r, tw_s, tw_r, nx_s, nx_r,
    ry_s, ry_r, rp_s, rp_r, rz_s, rz_r, rv_s, rv_r, vy_s, vy_r, f_s, f_r,
    g0_s, g0_r, g1_s, g1_r, g2_s, g2_r, gm_s, gm_r, h1_s, h1_r, h2_s, h2_r, sx_s, sx_r, szh_s, szh_r, token,
):
    g = lax.axis_index("group")
    f = lax.axis_index("fsdp")
    x, zh = g // 2, g % 2
    z, e = f // NE, f % NE
    y, c = e // 2, e % 2
    yr, yl, yo = (y + 1) % NY, (y + 3) % NY, (y + 2) % NY
    twin = (g, f + 1 - 2 * c)

    def at(zz, yy):
        return (g, zz * NE + yy * 2 + c)

    right, left = at(z, yr), at(z, yl)
    up, down = at(z + 1, y), at(z - 1, y)
    mate, up_two, down_two = at(z + 1 - 2 * (z % 2), y), at(z + 2, y), at(z - 2, y)
    pair, z_mate = z // 2, z + 1 - 2 * (z % 2)
    pairs = NZ // 2
    e_peers = [((e + k) % NE, (g, z * NE + (e + k) % NE)) for k in range(1, NE)]
    z_peers = [((z + k) % NZ, (g, ((z + k) % NZ) * NE + e)) for k in range(1, NZ)]
    xr, xl, xo = (x + 1) % NX, (x + 3) % NX, (x + 2) % NX
    x_right, x_left = (xr * 2 + zh, f), (xl * 2 + zh, f)
    after = (x * 2 + (zh + (z + 1) // NZ) % 2, ((z + 1) % NZ) * NE + e)
    before = (x * 2 + (zh + (NZ - z) // NZ) % 2, ((z + NZ - 1) % NZ) * NE + e)
    zh_peer = (x * 2 + 1 - zh, f)

    def remote(src, dst, send, recv, device):
        return pltpu.make_async_remote_copy(
            src_ref=src, dst_ref=dst, send_sem=send, recv_sem=recv, device_id=device, device_id_type=MESH
        )

    def received(ref, sem):
        remote(ref, ref, sem, sem, twin).wait_recv()

    def sent(ref, sem):
        remote(ref, ref, sem, sem, twin).wait_send()

    barrier = pltpu.get_barrier_semaphore()
    peers = [before, after, right, left, x_right, x_left, twin]
    two_after, two_before = at((z + 2) % NZ, y), at((z + NZ - 2) % NZ, y)
    peers += [two_after, two_before]
    for peer in peers:
        pl.semaphore_signal(barrier, inc=1, device_id=peer, device_id_type=MESH)

    w_in = pltpu.make_async_copy(w_hbm, w_ref, in_sem.at[0])
    gains_in = pltpu.make_async_copy(gains_hbm, gains_ref, in_sem.at[1])
    snap_in = pltpu.make_async_copy(snap_hbm, snap_ref, in_sem.at[2])
    hid_in = pltpu.make_async_copy(hid_hbm, hid, in_sem.at[3])
    gv_in = pltpu.make_async_copy(gv_hbm, gx.at[c], in_sem.at[4])
    outer_in = pltpu.make_async_copy(outer_hbm, outer_ref, in_sem.at[5])
    mom_in = pltpu.make_async_copy(mom_hbm, mom_ref, in_sem.at[6])
    for copy in (gains_in, w_in, hid_in, gv_in, snap_in, outer_in, mom_in):
        copy.start()

    def own_columns(j):
        return pl.ds(j, ROWS, stride=FRAGS)

    def pack_own():
        w_in.wait()
        for q in range(FRAGS):
            pack[ROWS * q : ROWS * (q + 1), :] = w_ref[own_columns(q), :]
        wp[c, z, y] = pack[...].astype(BF16)

    first_lane = ROWS * f - 128 * window_start(z)
    spot = lax.broadcasted_iota(jnp.int32, (ROWS, 128), 0) + first_lane
    lane = lax.broadcasted_iota(jnp.int32, (ROWS, 128), 1)

    def place_gains():
        gains_in.wait()
        gain_own = jnp.broadcast_to(gains_ref[...].astype(BF16), (8, ROWS))
        g0[c] = jnp.zeros((8, 128), F32)
        for r in range(3):
            hot = jnp.where(spot == lane + 128 * r, 1.0, 0.0).astype(BF16)
            g0[c, r : r + 1, :] = jnp.dot(gain_own, hot, preferred_element_type=F32)[0:1]

    def gain_twin(core):
        return remote(g0.at[core], g0.at[core], g0_s, g0_r, twin)

    def gain_y(kind):
        row = y if kind < 2 else yl
        return remote(
            g1.at[row], g1.at[row], g1_s, g1_r.at[0 if kind == 0 else 1], left if kind == 1 else right
        )

    def gain_z(direction, slab):
        ref = g2.at[slab]
        return remote(
            ref, ref, g2_s.at[direction, slab // 2], g2_r.at[slab // 2], up_two if direction == 0 else down_two
        )

    def gain_mate(slab):
        return remote(g2.at[slab], g2.at[slab], gm_s, gm_r, mate)

    def gain_chip():
        gain_twin(1 - c).wait_recv()
        g1[y] = g0[0] + g0[1]
        gain_y(0).start()
        gain_y(1).start()

    def gain_near():
        received(g1.at[yl], g1_r.at[0])
        gain_y(2).start()

    def gain_slab():
        received(g1.at[pl.ds(0, 2)], g1_r.at[1])
        g2[z] = total(g1, NY)
        both_ways_two(lambda direction: gain_z(direction, z).start())
        gain_mate(z).start()

    def gather_gain(t):
        for direction, slab, here, more in (
            (0, z - 2 * t, pair >= t, pair < pairs - 1), (1, z + 2 * t, pair + t < pairs, pair > 0),
        ):
            @pl.when(here)
            def _():
                gain_z(direction, slab).wait_recv()

                @pl.when(more)
                def _():
                    gain_z(direction, slab).start()

                gain_mate(slab).start()

    def gain_all():
        received(g2.at[pl.ds(0, pairs)], gm_r)

    def snap_x(kind):
        row = x if kind < 2 else xl
        return remote(
            sx.at[row], sx.at[row], sx_s, sx_r.at[0 if kind == 0 else 1], x_left if kind == 1 else x_right
        )

    def place_snapshot():
        snap_in.wait()
        sx[x] = jnp.zeros((40, 128), F32)
        sx[x, 0:ROWS, :] = snap_ref[...].reshape(ROWS, 128)
        snap_x(0).start()
        snap_x(1).start()

    def snapshot_near():
        received(sx.at[xl], sx_r.at[0])
        snap_x(2).start()

    def pass_token(t):
        if t > 0:
            pl.semaphore_wait(token.at[t - 1], 1)
        if t < NZ - 1:
            pl.semaphore_signal(token.at[t], inc=1, device_id=after, device_id_type=MESH)

    def barrier_wait():
        pl.semaphore_wait(barrier, len(peers))

    def spread_start(buf, own, peer_list, send, recv):
        for _, peer in peer_list:
            remote(buf.at[own], buf.at[own], send, recv, peer).start()

    def total(buf, count):
        result = buf[0]
        for index in range(1, count):
            result = result + buf[index]
        return result

    halves = (pl.ds(0, AH), pl.ds(AH, AH))

    def z_copy(direction, slab):
        ref = wp.at[c, slab, y]
        return remote(
            ref, ref, agz_s.at[direction, slab // 2], agz_r.at[slab // 2], up_two if direction == 0 else down_two
        )

    def mate_copy(slab):
        ref = wp.at[c, slab, y]
        return remote(ref, ref, agp_s, agp_r.at[slab // 2], mate)

    def y_copy(kind, slab):
        device = right if kind in (0, 2) else left
        if kind < 2:
            ref = wp.at[c, slab, y]
        elif kind == 2:
            ref = wp.at[c, slab, yl, halves[0]]
        else:
            ref = wp.at[c, slab, yr, halves[1]]
        return remote(ref, ref, ay_s, ay_r.at[kind // 2, slab], device)

    low, high = pl.ds(0, VH), pl.ds(VH, VH)

    def twin_copy(slab, core):
        return remote(wp.at[core, slab], wp.at[core, slab], tw_s, tw_r.at[slab], twin)

    def both_ways_two(send):
        @pl.when(pair < pairs - 1)
        def _():
            send(0)

        @pl.when(pair > 0)
        def _():
            send(1)

    def gather_own():
        both_ways_two(lambda direction: z_copy(direction, z).start())
        y_copy(0, z).start()
        y_copy(1, z).start()
        mate_copy(z).start()

    def gather_z(t):
        for direction, slab, here, more in (
            (0, z - 2 * t, pair >= t, pair < pairs - 1), (1, z + 2 * t, pair + t < pairs, pair > 0),
        ):
            @pl.when(here)
            def _():
                z_copy(direction, slab).wait_recv()

                @pl.when(more)
                def _():
                    z_copy(direction, slab).start()

                mate_copy(slab).start()
                y_copy(0, slab).start()
                y_copy(1, slab).start()

    def gather_mate(t):
        sides = ((z_mate, pair >= 0),) if t == 0 else ((z_mate - 2 * t, pair >= t), (z_mate + 2 * t, pair + t < pairs))
        for slab, here in sides:
            @pl.when(here)
            def _():
                mate_copy(slab).wait_recv()
                y_copy(0, slab).start()
                y_copy(1, slab).start()

    def gather_y(j):
        slab = order(z, 7 - j)
        received(wp.at[c, slab, pl.ds(0, 2)], ay_r.at[0, slab])
        y_copy(2, slab).start()
        y_copy(3, slab).start()

    def gather_twin(j):
        slab = order(z, 7 - j)
        received(wp.at[c, slab, yo], ay_r.at[1, slab])
        twin_copy(slab, c).start()

    def unpack(lo, hi):
        def one(j, _):
            slab = order(z, 7 - j)
            twin_copy(slab, 1 - c).wait_recv()
            for core in range(2):
                for yy in range(NY):
                    block = wp[core, slab, yy].astype(F32)
                    base = ROWS * (2 * yy + core)
                    for q in range(FRAGS):
                        stage[base : base + ROWS, 128 * q : 128 * (q + 1)] = block[ROWS * q : ROWS * (q + 1)]
            w[pl.ds(pl.multiple_of(SLAB * slab, 16), SLAB), :] = stage[...].astype(BF16)
            return 0

        lax.fori_loop(lo, hi, one, 0)

    def normalise(lo, hi):
        def one(r, _):
            rows = pl.ds(pl.multiple_of(32 * r, 32), 32)
            tokens = hid[rows, :].astype(F32)
            inverse = lax.rsqrt(jnp.sum(tokens * tokens, axis=-1, keepdims=True) / D + epsilon)
            invb[rows, :] = jnp.broadcast_to(inverse, (32, 128))
            nbx[c, rows, :] = (tokens * inverse).astype(BF16)
            return 0

        lax.fori_loop(lo, hi, one, 0)

    def gain_vector():
        grow[...] = jnp.zeros((8, D), F32)
        for slab in range(NZ):
            for r in range(3):
                lanes = slice(128 * (window_start(slab) + r), 128 * (window_start(slab) + r + 1))
                grow[0:1, lanes] = grow[0:1, lanes] + g2[slab, r : r + 1, :]

    def apply_gain():
        def one(r, _):
            rows = pl.ds(pl.multiple_of(32 * r, 32), 32)
            normed = hid[rows, :].astype(F32) * invb[rows, 0:1]
            nbg[rows, :] = (normed * grow[0:1, :]).astype(BF16)
            return 0

        lax.fori_loop(0, TOK // 32, one, 0)

    def nx_nb(core, half):
        ref = nbx.at[core, pl.ds(half * TOK // 2, TOK // 2)]
        return remote(ref, ref, nx_s.at[0], nx_r.at[0], twin)

    def nx_gv(core):
        return remote(gx.at[core], gx.at[core], nx_s.at[1], nx_r.at[1], twin)

    def weight_terms(core, lo, hi):
        columns = pl.ds(pl.multiple_of(HALF * c, 128), HALF)

        def one(k, _):
            feats = pl.ds(pl.multiple_of(256 * k, 256), 256)
            terms = lax.dot_general(
                nbx[core, :, feats], gx[core, :, columns], (((0,), (0,)), ((), ())), preferred_element_type=F32
            )
            dw[feats, :] = terms if core is c else dw[feats, :] + terms
            return 0

        lax.fori_loop(lo, hi, one, 0)

    def term(slab, yy, row, count):
        base = pl.multiple_of(CHIP * (NY * slab + yy), 8)
        parts, end = [], row + count
        while row < end:
            q, r = row // CHIP, row % CHIP
            count = min(CHIP - r, end - row)
            parts.append(dw[pl.ds(base + r, count), 128 * q : 128 * (q + 1)])
            row += count
        return jnp.concatenate(parts, axis=0)

    def far_copy(kind, slab):
        return remote(
            s1.at[slab, kind], r1.at[slab, kind], ry_s.at[0], ry_r.at[0, slab], right if kind == 0 else left
        )

    def near_copy(kind, slab):
        return remote(
            s2.at[slab, kind], r2.at[slab, kind], ry_s.at[1], ry_r.at[1, slab],
            right if kind == 0 else left,
        )

    def chain_copy(direction, slab):
        return remote(
            sz.at[slab], rz.at[direction, slab], rz_s, rz_r.at[direction, slab // 2],
            up_two if direction == 0 else down_two,
        )

    def pair_copy(slab):
        return remote(sp.at[slab // 2], rp.at[slab // 2], rp_s, rp_r.at[slab // 2], mate)

    def reduce_pair(i):
        slab = order(z, 2 * i)
        sp[slab // 2] = racc[slab].astype(BF16)
        pair_copy(slab).start()

    def reduce_pair_wait(i):
        slab = order(z, 2 * i + 1)
        pair_copy(slab).wait_recv()
        racc[slab] = racc[slab] + rp[slab // 2].astype(F32)

    def chain_v_copy(direction, slab):
        return remote(
            vz.at[slab], rv.at[direction, slab], rv_s, rv_r.at[direction, slab], up if direction == 0 else down
        )

    def reduce_far(s):
        slab = order(z, s)
        for kind in range(2):
            s1[slab, kind] = term(slab, yo, ZH * kind, ZH).astype(BF16)
            far_copy(kind, slab).start()

    def reduce_near(s):
        slab = order(z, s)
        received(r1.at[slab], ry_r.at[0, slab])
        for kind, yy in ((0, yr), (1, yl)):
            s2[slab, kind, kind] = (term(slab, yy, ZH * kind, ZH) + r1[slab, kind].astype(F32)).astype(BF16)
            s2[slab, kind, 1 - kind] = term(slab, yy, ZH * (1 - kind), ZH).astype(BF16)
            near_copy(kind, slab).start()

    def reduce_row(s):
        slab = order(z, s)
        received(r2.at[slab], ry_r.at[1, slab])
        for p in range(2):
            racc[slab, p] = term(slab, y, ZH * p, ZH) + r2[slab, 0, p].astype(F32) + r2[slab, 1, p].astype(F32)

    def reduce_chain(u):
        reduce_pair_wait(u)
        if u == pairs - 1:
            for direction, here in ((0, pair > 0), (1, pair < pairs - 1)):
                @pl.when(here)
                def _():
                    chain_copy(direction, z).wait_recv()
                    racc[z] = racc[z] + rz[direction, z].astype(F32)

            return

        far = pairs - 1 - u
        for direction, slab, here, later in (
            (0, z + 2 * far, pair <= u, pair > 0), (1, z - 2 * far, pair >= far, pair < pairs - 1),
        ):
            @pl.when(here)
            def _():
                @pl.when(later)
                def _():
                    chain_copy(direction, slab).wait_recv()
                    sz[slab] = (racc[slab] + rz[direction, slab].astype(F32)).astype(BF16)

                @pl.when(jnp.logical_not(later))
                def _():
                    sz[slab] = racc[slab].astype(BF16)

                chain_copy(direction, slab).start()

    def reduce_v(u):
        if u == NZ - 1:
            for direction, here in ((0, z > 0), (1, z < NZ - 1)):
                @pl.when(here)
                def _():
                    chain_v_copy(direction, z).wait_recv()

            for k in (2, 1, 3, 0):
                yy = (y + k) % NY
                vacc[k] = term(z, yy, 2 * ZH, VR)
                for direction, here in ((0, z > 0), (1, z < NZ - 1)):
                    @pl.when(here)
                    def _():
                        vacc[k] = vacc[k] + rv[direction, z, yy].astype(F32)

                if k == 2:
                    vs1[...] = vacc[2].astype(BF16)
                    v_far(0).start()
                    v_far(1).start()
            return

        for direction, slab, here, later in (
            (0, NZ - 1 + z - u, z <= u, z > 0), (1, z - (NZ - 1) + u, z >= NZ - 1 - u, z < NZ - 1),
        ):
            @pl.when(here)
            def _():
                @pl.when(later)
                def _():
                    chain_v_copy(direction, slab).wait_recv()
                    for yy in range(NY):
                        vz[slab, yy] = (term(slab, yy, 2 * ZH, VR) + rv[direction, slab, yy].astype(F32)).astype(BF16)

                @pl.when(jnp.logical_not(later))
                def _():
                    for yy in range(NY):
                        vz[slab, yy] = term(slab, yy, 2 * ZH, VR).astype(BF16)

                chain_v_copy(direction, slab).start()

    def v_far(kind):
        part = low if kind == 0 else high
        return remote(vs1.at[part], vr1.at[part], vy_s.at[0], vy_r.at[0], right if kind == 0 else left)

    def v_near(kind):
        return remote(vs2.at[kind], vr2.at[kind], vy_s.at[1], vy_r.at[1], right if kind == 0 else left)

    def reduce_v_near():
        received(vr1, vy_r.at[0])
        vs2[0] = jnp.concatenate(
            [vacc[1, 0:VH] + vr1[0:VH].astype(F32), vacc[1, VH:VR]], axis=0
        ).astype(BF16)
        v_near(0).start()
        vs2[1] = jnp.concatenate(
            [vacc[3, 0:VH], vacc[3, VH:VR] + vr1[VH:VR].astype(F32)], axis=0
        ).astype(BF16)
        v_near(1).start()

    def reduce_v_row():
        received(vr2, vy_r.at[1])
        fbuf[c, 2 * ZH : BLOCK] = vacc[0] + vr2[0].astype(F32) + vr2[1].astype(F32)

    near_half, far_half = z // 4, 1 - z // 4

    def make_values(half, done):
        feats = pl.ds(pl.multiple_of(D // 2 * half, 128), D // 2)

        def one(n, _):
            columns = pl.ds(pl.multiple_of(256 * n, 256), 256)
            part = jnp.dot(nbg[:, feats], w[feats, columns], preferred_element_type=F32)
            if done:
                vout[:, columns] = ((vf[:, columns] + part) * FACTOR).astype(BF16)
            else:
                vf[:, columns] = part
            return 0

        lax.fori_loop(0, KV // 256, one, 0)

    def input_gradient(half):
        def one(k, _):
            feats = pl.ds(pl.multiple_of(D // 2 * half + 384 * k, 128), 384)
            grad = lax.dot_general(gx[c], w[feats, :], (((1,), (1,)), ((), ())), preferred_element_type=F32) * FACTOR
            ig[:, feats] = grad
            normed = hid[:, feats].astype(F32) * invb[:, 0:1]
            gacc[:, feats] = jnp.sum((grad * normed).reshape(TOK // 8, 8, 384), axis=0)
            return 0

        lax.fori_loop(0, D // 2 // 384, one, 0)

    def hidden_gradient(lo, hi):
        def one(r, _):
            rows = pl.ds(pl.multiple_of(32 * r, 32), 32)
            inverse = invb[rows, 0:1]
            normed = hid[rows, :].astype(F32) * inverse
            grad = ig[rows, :]
            along = grad * normed
            gain = grow[0:1, :]
            mean = jnp.sum(along * gain, axis=-1, keepdims=True) / D
            gh[rows, :] = (inverse * (grad * gain - normed * mean)).astype(BF16)
            return 0

        lax.fori_loop(lo, hi, one, 0)

    def gain_terms(half):
        for side in range(2):
            @pl.when(half == side)
            def _():
                for slab in range(4 * side, 4 * side + 4):
                    hsrc[slab] = jnp.zeros((8, 128), F32)
                    for r in range(3):
                        lanes = slice(128 * (window_start(slab) + r), 128 * (window_start(slab) + r + 1))
                        hsrc[slab, r : r + 1, :] = jnp.sum(gacc[:, lanes], axis=0, keepdims=True)

                    @pl.when(z != slab)
                    def _():
                        remote(hsrc.at[slab], h1.at[z], h1_s, h1_r, (g, slab * NE + e)).start()

    def gain_second():
        received(h1.at[pl.ds(0, NZ - 1)], h1_r)
        h1[z] = hsrc[z]
        h2[e] = total(h1, NZ)
        spread_start(h2, e, e_peers, h2_s, h2_r)

    def gain_step():
        received(h2.at[pl.ds(0, NE - 1)], h2_r)
        window = total(h2, NE)
        gain_grad = jnp.zeros((8, ROWS), F32)
        for r in range(3):
            hot = jnp.where(spot == lane + 128 * r, 1.0, 0.0)
            gain_grad = gain_grad + lax.dot_general(
                jnp.broadcast_to(window[r : r + 1], (8, 128)), hot, (((1,), (1,)), ((), ())),
                precision=lax.Precision.HIGHEST, preferred_element_type=F32,
            )
        newg_ref[...] = gains_ref[...] - gain_rate * gain_grad[0:1]
        out(3).start()

    def snapshot_second():
        received(sx.at[pl.ds(0, 2)], sx_r.at[1])
        szh[zh] = total(sx, NX)
        szh_copy(zh).start()

    def szh_copy(half):
        return remote(szh.at[half], szh.at[half], szh_s, szh_r, zh_peer)

    def outer_step():
        outer_in.wait()
        mom_in.wait()
        szh_copy(1 - zh).wait_recv()
        change = outer_ref[...] - (szh[0] + szh[1])[0:ROWS] / (2 * NX)
        new_moment = momentum * mom_ref[...] + change
        newm_ref[...] = new_moment
        newo_ref[...] = outer_ref[...] - outer_rate * (change + momentum * new_moment)
        out(4).start()
        out(5).start()

    def last(core):
        return remote(fbuf.at[core], fbuf.at[core], f_s, f_r, twin)

    def inner_step():
        last(1 - c).wait_recv()
        row_of = lax.broadcasted_iota(jnp.int32, (ROWS, ROWS), 0)
        column_of = lax.broadcasted_iota(jnp.int32, (ROWS, ROWS), 1)
        gain_bf = jnp.broadcast_to(gains_ref[...].astype(BF16).astype(F32), (ROWS, ROWS))
        scale = jnp.sum(jnp.where(row_of == column_of, gain_bf, 0.0), axis=1, keepdims=True) * FACTOR
        for core in range(2):
            @pl.when(c == core)
            def _():
                for j in range(FRAGS):
                    row = CHIP * (j % 4) + ROWS * core
                    grad = fbuf[j // 4, row : row + ROWS, :] * scale
                    inner = w_ref[own_columns(j), :] - inner_rate * grad
                    mixed = mixing * inner + (1.0 - mixing) * newo_ref[...]
                    neww_ref[own_columns(j), :] = jnp.where(frag_ref[0] == j, mixed, inner)

        out(2).start()

    results = (
        (vout, values_hbm), (gh, gh_hbm), (neww_ref, neww_hbm), (newg_ref, newg_hbm), (newo_ref, newo_hbm),
        (newm_ref, newm_hbm),
    )

    def out(index):
        return pltpu.make_async_copy(results[index][0], results[index][1], out_sem.at[index])

    def results_wait():
        for index in range(6):
            out(index).wait()

    def drain():
        for t in range(pairs):
            for direction, slab, here in (
                (0, z - 2 * t, jnp.logical_and(pair >= t, pair < pairs - 1)),
                (1, z + 2 * t, jnp.logical_and(pair + t < pairs, pair > 0)),
            ):
                @pl.when(here)
                def _():
                    z_copy(direction, slab).wait_send()
                    gain_z(direction, slab).wait_send()

        sent(wp.at[0, 0], agp_s)
        sent(wp.at[0, pl.ds(0, 6)], ay_s)
        sent(wp.at[0], tw_s)
        sent(s1, ry_s.at[0])
        sent(s2, ry_s.at[1])
        sent(sp, rp_s)
        sent(sz.at[pl.ds(0, pairs - 1)], rz_s)
        sent(vz.at[pl.ds(0, NZ - 1)], rv_s)
        sent(vs1, vy_s.at[0])
        sent(vs2, vy_s.at[1])
        sent(nbx.at[0], nx_s.at[0])
        sent(gx.at[0], nx_s.at[1])
        sent(fbuf.at[0], f_s)
        sent(szh.at[0], szh_s)
        sent(g0.at[0], g0_s)
        sent(g1.at[pl.ds(0, 3)], g1_s)
        sent(g2.at[pl.ds(0, pairs)], gm_s)
        sent(sx.at[pl.ds(0, 3)], sx_s)
        sent(hsrc.at[pl.ds(0, NZ - 1)], h1_s)
        sent(h2.at[pl.ds(0, NE - 1)], h2_s)

    place_gains()
    pack_own()
    barrier_wait()
    gain_twin(c).start()
    gather_own()
    pass_token(0)
    gv_in.wait()
    nx_gv(c).start()
    hid_in.wait()
    normalise(0, 4)
    nx_nb(c, 0).start()
    normalise(4, 8)
    nx_nb(c, 1).start()
    gain_chip()
    place_snapshot()
    weight_terms(c, 0, 5)
    weight_terms(c, 5, 9)
    gain_near()
    gather_y(0)
    gather_mate(0)
    nx_gv(1 - c).wait_recv()
    received(nbx.at[1 - c], nx_r.at[0])
    weight_terms(1 - c, 0, 5)
    gather_z(1)
    pass_token(1)
    weight_terms(1 - c, 5, 9)
    reduce_v(0)
    reduce_far(0)
    reduce_far(1)
    pass_token(2)
    gain_slab()
    gather_y(1)
    gather_twin(0)
    gather_mate(1)
    gather_z(2)
    snapshot_near()
    reduce_v(1)
    pass_token(3)
    reduce_near(0)
    reduce_near(1)
    gather_y(2)
    gather_gain(1)
    gather_mate(2)
    pass_token(4)
    gather_twin(1)
    reduce_v(2)
    gather_y(3)
    gather_z(3)
    pass_token(5)
    reduce_far(2)
    reduce_far(3)
    gather_twin(2)
    gather_gain(2)
    gather_y(4)
    reduce_v(3)
    gather_mate(3)
    gather_twin(3)
    pass_token(6)
    gather_y(5)
    reduce_row(0)
    reduce_row(1)
    reduce_pair(0)
    reduce_near(2)
    reduce_near(3)
    pass_token(7)
    snapshot_second()
    gather_gain(3)
    reduce_v(4)
    gather_twin(4)
    gather_y(6)
    unpack(0, 4)
    reduce_far(4)
    reduce_far(5)
    reduce_chain(0)
    input_gradient(near_half)
    gain_terms(near_half)
    gather_twin(5)
    gather_y(7)
    reduce_v(5)
    reduce_row(2)
    reduce_row(3)
    reduce_pair(1)
    gain_all()
    gain_vector()
    apply_gain()
    reduce_near(4)
    reduce_near(5)
    reduce_far(6)
    reduce_far(7)
    gather_twin(6)
    gather_twin(7)
    make_values(near_half, False)
    reduce_v(6)
    reduce_chain(1)
    unpack(4, 6)
    reduce_row(4)
    reduce_row(5)
    reduce_pair(2)
    reduce_near(6)
    reduce_near(7)
    unpack(6, 8)
    input_gradient(far_half)
    gain_terms(far_half)
    reduce_v(7)
    reduce_row(6)
    reduce_pair(3)
    reduce_row(7)
    reduce_chain(2)
    reduce_v_near()
    hidden_gradient(0, 8)
    out(1).start()
    gain_second()
    reduce_v_row()
    reduce_chain(3)
    fbuf[c, 0 : 2 * ZH] = racc[z].reshape(2 * ZH, 128)
    last(c).start()
    make_values(far_half, True)
    out(0).start()
    outer_step()
    drain()
    inner_step()
    gain_step()
    results_wait()


def place_kernel(*refs):
    sources, targets, held, in_sem, out_sem = refs[:6], refs[6:12], refs[12:18], refs[18], refs[19]
    slices = [(1, pl.ds(64 * k, 64)) for k in range(4)] + [(0, pl.ds(128 * k, 128)) for k in range(2)]
    parts = [(s.at[rows], h.at[rows], t.at[rows]) for i, rows in slices for s, h, t in [(sources[i], held[i], targets[i])]]
    parts += [(sources[i], held[i], targets[i]) for i in range(2, 6)]
    arrive = [pltpu.make_async_copy(s, h, in_sem.at[k]) for k, (s, h, _) in enumerate(parts)]
    leave = [pltpu.make_async_copy(h, t, out_sem.at[k]) for k, (_, h, t) in enumerate(parts)]
    for copy in arrive:
        copy.start()
    for one, other in zip(arrive, leave):
        one.wait()
        other.start()
    for copy in leave:
        copy.wait()


def body(hidden, grad_values, weights, gains, snapshot, outer_frag, outer_moment, fragment_index):
    anywhere = pl.BlockSpec(memory_space=pl.ANY)
    dma = pltpu.SemaphoreType.DMA
    vmem = pltpu.VMEM
    shapes = (
        jax.ShapeDtypeStruct((TOK, KV), BF16),
        jax.ShapeDtypeStruct((TOK, D), BF16),
        jax.ShapeDtypeStruct((ROWS * FRAGS, 128), F32),
        jax.ShapeDtypeStruct((1, ROWS), F32),
        jax.ShapeDtypeStruct((ROWS, FW), F32),
        jax.ShapeDtypeStruct((ROWS, FW), F32),
    )
    results = pl.pallas_call(
        step_kernel,
        out_shape=shapes,
        in_specs=[pl.BlockSpec(memory_space=pltpu.SMEM)] + [anywhere] * 7,
        out_specs=(anywhere,) * 6,
        scratch_shapes=[
            vmem((TOK, D), BF16),
            vmem((2, TOK, KV), BF16),
            vmem((2, TOK, D), BF16),
            vmem((TOK, D), BF16),
            vmem((2, NZ, NY, BLOCK, 128), BF16),
            vmem((D, KV), BF16),
            vmem((SLAB, KV), F32),
            vmem((BLOCK, 128), F32),
            vmem((D, HALF), F32),
            vmem((NZ, 2, ZH, 128), BF16),
            vmem((NZ, 2, ZH, 128), BF16),
            vmem((NZ, 2, 2, ZH, 128), BF16),
            vmem((NZ, 2, 2, ZH, 128), BF16),
            vmem((NZ, 2, ZH, 128), F32),
            vmem((NZ // 2, 2, ZH, 128), BF16),
            vmem((NZ // 2, 2, ZH, 128), BF16),
            vmem((NZ, 2, ZH, 128), BF16),
            vmem((2, NZ, 2, ZH, 128), BF16),
            vmem((NY, VR, 128), F32),
            vmem((VR, 128), BF16),
            vmem((VR, 128), BF16),
            vmem((2, VR, 128), BF16),
            vmem((2, VR, 128), BF16),
            vmem((NZ, NY, VR, 128), BF16),
            vmem((2, NZ, NY, VR, 128), BF16),
            vmem((2, BLOCK, 128), F32),
            vmem((TOK, D), F32),
            vmem((TOK, KV), F32),
            vmem((TOK, KV), BF16),
            vmem((TOK, D), BF16),
            vmem((TOK, 128), F32),
            vmem((8, D), F32),
            vmem((8, D), F32),
            vmem((2, 8, 128), F32),
            vmem((NY, 8, 128), F32),
            vmem((NZ, 8, 128), F32),
            vmem((NZ, 8, 128), F32),
            vmem((NZ, 8, 128), F32),
            vmem((NE, 8, 128), F32),
            vmem((NX, 40, 128), F32),
            vmem((2, 40, 128), F32),
            vmem((ROWS * FRAGS, 128), F32),
            vmem((1, ROWS), F32),
            vmem((ROWS, 1, FW), F32),
            vmem((ROWS, FW), F32),
            vmem((ROWS, FW), F32),
            vmem((ROWS * FRAGS, 128), F32),
            vmem((1, ROWS), F32),
            vmem((ROWS, FW), F32),
            vmem((ROWS, FW), F32),
            dma((7,)), dma((6,)),
            dma((2, NZ // 2)), dma((NZ // 2,)), dma, dma((NZ // 2,)),
            dma, dma((2, NZ)),
            dma, dma((NZ,)),
            dma((2,)), dma((2,)),
            dma((2,)), dma((2, NZ)),
            dma, dma((NZ // 2,)),
            dma, dma((2, NZ // 2)),
            dma, dma((2, NZ)),
            dma((2,)), dma((2,)),
            dma, dma,
            dma, dma,
            dma, dma((2,)),
            dma((2, NZ // 2)), dma((NZ // 2,)), dma, dma,
            dma, dma, dma, dma,
            dma, dma((2,)),
            dma, dma,
            pltpu.SemaphoreType.REGULAR((7,)),
        ],
        compiler_params=pltpu.CompilerParams(
            collective_id=0, has_side_effects=True, vmem_limit_bytes=56 * 1024 * 1024,
        ),
        cost_estimate=pl.CostEstimate(flops=3 * 2 * TOK * D * KV, bytes_accessed=4_000_000, transcendentals=0),
    )(
        fragment_index, hidden, grad_values, weights.reshape(ROWS * FRAGS, 128), gains,
        snapshot.reshape(ROWS, 1, FW), outer_frag, outer_moment,
    )
    values, grad_hidden, new_weights, new_gains, new_outer, new_moment = pl.pallas_call(
        place_kernel,
        out_shape=shapes,
        in_specs=[anywhere] * 6,
        out_specs=(anywhere,) * 6,
        scratch_shapes=[vmem(shape.shape, shape.dtype) for shape in shapes] + [dma((10,)), dma((10,))],
        compiler_params=pltpu.CompilerParams(vmem_limit_bytes=60 * 1024 * 1024),
    )(*results)
    return (values, grad_hidden, new_weights.reshape(1, ROWS, KV), new_gains, new_outer, new_moment)


def solution(mesh):
    return jax.shard_map(
        body,
        mesh=mesh,
        in_specs=(
            P(("group", "fsdp"), None),
            P(("group", "fsdp"), None),
            P("group", "fsdp", None),
            P("group", "fsdp"),
            P("group", "fsdp", None),
            P("fsdp", None),
            P("fsdp", None),
            P(),
        ),
        out_specs=(
            P(("group", "fsdp"), None),
            P(("group", "fsdp"), None),
            P("group", "fsdp", None),
            P("group", "fsdp"),
            P("fsdp", None),
            P("fsdp", None),
        ),
        check_vma=False,
    )
```

```python
import functools

import jax
import jax.numpy as jnp
from jax import lax
from jax.experimental import pallas as pl
from jax.experimental.pallas import tpu as pltpu
from jax.sharding import PartitionSpec as P

MESH = pl.DeviceIdType.MESH
F32 = jnp.float32
BF16 = jnp.bfloat16

D = 2304
KV = 1024
FW = 128
FRAGS = 8
TOK = 256
NZ = 8
NY = 4
NE = 8
NX = 4
ROWS = 36
CHIP = 72
SLAB = 288
HALF = 512

epsilon = 1e-06
inner_rate = 0.05
gain_rate = 0.002
momentum = 0.9
outer_rate = 0.7
mixing = 0.5
FACTOR = D ** (-0.5)
BLOCK = 288
AH = BLOCK // 2
ZH = 112
VR = 64
VH = VR // 2


def window_start(z):
    return (SLAB * z) // 128


def order(z, s):
    pair, odd = z // 2, z % 2
    near = 3 - s // 2
    low = jnp.where(pair % 3 == 0, near, jnp.where(near < 2, 1 - near, near))
    which = jnp.where(pair > 1, 3 - low, low)
    return 2 * which + jnp.where(s % 2 == 0, 1 - odd, odd)


def step_kernel(
    frag_ref, hid_hbm, gv_hbm, w_hbm, gains_hbm, snap_hbm, outer_hbm, mom_hbm,
    values_hbm, gh_hbm, neww_hbm, newg_hbm, newo_hbm, newm_hbm,
    hid, gx, nbx, nbg, wp, w, stage, pack, dw, s1, r1, s2, r2, racc, sp, rp, sz, rz,
    vacc, vs1, vr1, vs2, vr2, vz, rv, fbuf,
    ig, vf, vout, gh, invb, grow, gacc, g0, g1, g2, hsrc, h1, h2, sx, szh,
    w_ref, gains_ref, snap_ref, outer_ref, mom_ref, neww_ref, newg_ref, newo_ref, newm_ref,
    in_sem, out_sem, agz_s, agz_r, agp_s, agp_r, ay_s, ay_r, tw_s, tw_r, nx_s, nx_r,
    ry_s, ry_r, rp_s, rp_r, rz_s, rz_r, rv_s, rv_r, vy_s, vy_r, f_s, f_r,
    g0_s, g0_r, g1_s, g1_r, g2_s, g2_r, gm_s, gm_r, h1_s, h1_r, h2_s, h2_r, sx_s, sx_r, szh_s, szh_r, token,
):
    g = lax.axis_index("group")
    f = lax.axis_index("fsdp")
    x, zh = g // 2, g % 2
    z, e = f // NE, f % NE
    y, c = e // 2, e % 2
    yr, yl, yo = (y + 1) % NY, (y + 3) % NY, (y + 2) % NY
    twin = (g, f + 1 - 2 * c)

    def at(zz, yy):
        return (g, zz * NE + yy * 2 + c)

    right, left = at(z, yr), at(z, yl)
    up, down = at(z + 1, y), at(z - 1, y)
    mate, up_two, down_two = at(z + 1 - 2 * (z % 2), y), at(z + 2, y), at(z - 2, y)
    pair, z_mate = z // 2, z + 1 - 2 * (z % 2)
    pairs = NZ // 2
    e_peers = [((e + k) % NE, (g, z * NE + (e + k) % NE)) for k in range(1, NE)]
    z_peers = [((z + k) % NZ, (g, ((z + k) % NZ) * NE + e)) for k in range(1, NZ)]
    xr, xl, xo = (x + 1) % NX, (x + 3) % NX, (x + 2) % NX
    x_right, x_left = (xr * 2 + zh, f), (xl * 2 + zh, f)
    after = (x * 2 + (zh + (z + 1) // NZ) % 2, ((z + 1) % NZ) * NE + e)
    before = (x * 2 + (zh + (NZ - z) // NZ) % 2, ((z + NZ - 1) % NZ) * NE + e)
    zh_peer = (x * 2 + 1 - zh, f)

    def remote(src, dst, send, recv, device):
        return pltpu.make_async_remote_copy(
            src_ref=src, dst_ref=dst, send_sem=send, recv_sem=recv, device_id=device, device_id_type=MESH
        )

    def received(ref, sem):
        remote(ref, ref, sem, sem, twin).wait_recv()

    def sent(ref, sem):
        remote(ref, ref, sem, sem, twin).wait_send()

    barrier = pltpu.get_barrier_semaphore()
    peers = [before, after, right, left, x_right, x_left, twin]
    two_after, two_before = at((z + 2) % NZ, y), at((z + NZ - 2) % NZ, y)
    peers += [two_after, two_before]
    for peer in peers:
        pl.semaphore_signal(barrier, inc=1, device_id=peer, device_id_type=MESH)

    w_in = pltpu.make_async_copy(w_hbm, w_ref, in_sem.at[0])
    gains_in = pltpu.make_async_copy(gains_hbm, gains_ref, in_sem.at[1])
    snap_in = pltpu.make_async_copy(snap_hbm, snap_ref, in_sem.at[2])
    hid_in = pltpu.make_async_copy(hid_hbm, hid, in_sem.at[3])
    gv_in = pltpu.make_async_copy(gv_hbm, gx.at[c], in_sem.at[4])
    outer_in = pltpu.make_async_copy(outer_hbm, outer_ref, in_sem.at[5])
    mom_in = pltpu.make_async_copy(mom_hbm, mom_ref, in_sem.at[6])
    for copy in (gains_in, w_in, hid_in, gv_in, snap_in, outer_in, mom_in):
        copy.start()

    def own_columns(j):
        return pl.ds(j, ROWS, stride=FRAGS)

    def pack_own():
        w_in.wait()
        for q in range(FRAGS):
            pack[ROWS * q : ROWS * (q + 1), :] = w_ref[own_columns(q), :]
        wp[c, z, y] = pack[...].astype(BF16)

    first_lane = ROWS * f - 128 * window_start(z)
    spot = lax.broadcasted_iota(jnp.int32, (ROWS, 128), 0) + first_lane
    lane = lax.broadcasted_iota(jnp.int32, (ROWS, 128), 1)

    def place_gains():
        gains_in.wait()
        gain_own = jnp.broadcast_to(gains_ref[...].astype(BF16), (8, ROWS))
        g0[c] = jnp.zeros((8, 128), F32)
        for r in range(3):
            hot = jnp.where(spot == lane + 128 * r, 1.0, 0.0).astype(BF16)
            g0[c, r : r + 1, :] = jnp.dot(gain_own, hot, preferred_element_type=F32)[0:1]

    def gain_twin(core):
        return remote(g0.at[core], g0.at[core], g0_s, g0_r, twin)

    def gain_y(kind):
        row = y if kind < 2 else yl
        return remote(
            g1.at[row], g1.at[row], g1_s, g1_r.at[0 if kind == 0 else 1], left if kind == 1 else right
        )

    def gain_z(direction, slab):
        ref = g2.at[slab]
        return remote(
            ref, ref, g2_s.at[direction, slab // 2], g2_r.at[slab // 2], up_two if direction == 0 else down_two
        )

    def gain_mate(slab):
        return remote(g2.at[slab], g2.at[slab], gm_s, gm_r, mate)

    def gain_chip():
        gain_twin(1 - c).wait_recv()
        g1[y] = g0[0] + g0[1]
        gain_y(0).start()
        gain_y(1).start()

    def gain_near():
        received(g1.at[yl], g1_r.at[0])
        gain_y(2).start()

    def gain_slab():
        received(g1.at[pl.ds(0, 2)], g1_r.at[1])
        g2[z] = total(g1, NY)
        both_ways_two(lambda direction: gain_z(direction, z).start())
        gain_mate(z).start()

    def gather_gain(t):
        for direction, slab, here, more in (
            (0, z - 2 * t, pair >= t, pair < pairs - 1), (1, z + 2 * t, pair + t < pairs, pair > 0),
        ):
            @pl.when(here)
            def _():
                gain_z(direction, slab).wait_recv()

                @pl.when(more)
                def _():
                    gain_z(direction, slab).start()

                gain_mate(slab).start()

    def gain_all():
        received(g2.at[pl.ds(0, pairs)], gm_r)

    def snap_x(kind):
        row = x if kind < 2 else xl
        return remote(
            sx.at[row], sx.at[row], sx_s, sx_r.at[0 if kind == 0 else 1], x_left if kind == 1 else x_right
        )

    def place_snapshot():
        snap_in.wait()
        sx[x] = jnp.zeros((40, 128), F32)
        sx[x, 0:ROWS, :] = snap_ref[...].reshape(ROWS, 128)
        snap_x(0).start()
        snap_x(1).start()

    def snapshot_near():
        received(sx.at[xl], sx_r.at[0])
        snap_x(2).start()

    def pass_token(t):
        if t > 0:
            pl.semaphore_wait(token.at[t - 1], 1)
        if t < NZ - 1:
            pl.semaphore_signal(token.at[t], inc=1, device_id=after, device_id_type=MESH)

    def barrier_wait():
        pl.semaphore_wait(barrier, len(peers))

    def spread_start(buf, own, peer_list, send, recv):
        for _, peer in peer_list:
            remote(buf.at[own], buf.at[own], send, recv, peer).start()

    def total(buf, count):
        result = buf[0]
        for index in range(1, count):
            result = result + buf[index]
        return result

    halves = (pl.ds(0, AH), pl.ds(AH, AH))

    def z_copy(direction, slab):
        ref = wp.at[c, slab, y]
        return remote(
            ref, ref, agz_s.at[direction, slab // 2], agz_r.at[slab // 2], up_two if direction == 0 else down_two
        )

    def mate_copy(slab):
        ref = wp.at[c, slab, y]
        return remote(ref, ref, agp_s, agp_r.at[slab // 2], mate)

    def y_copy(kind, slab):
        device = right if kind in (0, 2) else left
        if kind < 2:
            ref = wp.at[c, slab, y]
        elif kind == 2:
            ref = wp.at[c, slab, yl, halves[0]]
        else:
            ref = wp.at[c, slab, yr, halves[1]]
        return remote(ref, ref, ay_s, ay_r.at[kind // 2, slab], device)

    low, high = pl.ds(0, VH), pl.ds(VH, VH)

    def twin_copy(slab, core):
        return remote(wp.at[core, slab], wp.at[core, slab], tw_s, tw_r.at[slab], twin)

    def both_ways_two(send):
        @pl.when(pair < pairs - 1)
        def _():
            send(0)

        @pl.when(pair > 0)
        def _():
            send(1)

    def gather_own():
        both_ways_two(lambda direction: z_copy(direction, z).start())
        y_copy(0, z).start()
        y_copy(1, z).start()
        mate_copy(z).start()

    def gather_z(t):
        for direction, slab, here, more in (
            (0, z - 2 * t, pair >= t, pair < pairs - 1), (1, z + 2 * t, pair + t < pairs, pair > 0),
        ):
            @pl.when(here)
            def _():
                z_copy(direction, slab).wait_recv()

                @pl.when(more)
                def _():
                    z_copy(direction, slab).start()

                mate_copy(slab).start()
                y_copy(0, slab).start()
                y_copy(1, slab).start()

    def gather_mate(t):
        sides = ((z_mate, pair >= 0),) if t == 0 else ((z_mate - 2 * t, pair >= t), (z_mate + 2 * t, pair + t < pairs))
        for slab, here in sides:
            @pl.when(here)
            def _():
                mate_copy(slab).wait_recv()
                y_copy(0, slab).start()
                y_copy(1, slab).start()

    def gather_y(j):
        slab = order(z, 7 - j)
        received(wp.at[c, slab, pl.ds(0, 2)], ay_r.at[0, slab])
        y_copy(2, slab).start()
        y_copy(3, slab).start()

    def gather_twin(j):
        slab = order(z, 7 - j)
        received(wp.at[c, slab, yo], ay_r.at[1, slab])
        twin_copy(slab, c).start()

    def unpack(lo, hi):
        def one(j, _):
            slab = order(z, 7 - j)
            twin_copy(slab, 1 - c).wait_recv()
            for core in range(2):
                for yy in range(NY):
                    block = wp[core, slab, yy].astype(F32)
                    base = ROWS * (2 * yy + core)
                    for q in range(FRAGS):
                        stage[base : base + ROWS, 128 * q : 128 * (q + 1)] = block[ROWS * q : ROWS * (q + 1)]
            w[pl.ds(pl.multiple_of(SLAB * slab, 16), SLAB), :] = stage[...].astype(BF16)
            return 0

        lax.fori_loop(lo, hi, one, 0)

    def normalise(lo, hi):
        def one(r, _):
            rows = pl.ds(pl.multiple_of(32 * r, 32), 32)
            tokens = hid[rows, :].astype(F32)
            inverse = lax.rsqrt(jnp.sum(tokens * tokens, axis=-1, keepdims=True) / D + epsilon)
            invb[rows, :] = jnp.broadcast_to(inverse, (32, 128))
            nbx[c, rows, :] = (tokens * inverse).astype(BF16)
            return 0

        lax.fori_loop(lo, hi, one, 0)

    def gain_vector():
        grow[...] = jnp.zeros((8, D), F32)
        for slab in range(NZ):
            for r in range(3):
                lanes = slice(128 * (window_start(slab) + r), 128 * (window_start(slab) + r + 1))
                grow[0:1, lanes] = grow[0:1, lanes] + g2[slab, r : r + 1, :]

    def apply_gain():
        def one(r, _):
            rows = pl.ds(pl.multiple_of(32 * r, 32), 32)
            normed = hid[rows, :].astype(F32) * invb[rows, 0:1]
            nbg[rows, :] = (normed * grow[0:1, :]).astype(BF16)
            return 0

        lax.fori_loop(0, TOK // 32, one, 0)

    def nx_nb(core, half):
        ref = nbx.at[core, pl.ds(half * TOK // 2, TOK // 2)]
        return remote(ref, ref, nx_s.at[0], nx_r.at[0], twin)

    def nx_gv(core):
        return remote(gx.at[core], gx.at[core], nx_s.at[1], nx_r.at[1], twin)

    def weight_terms(core, lo, hi):
        columns = pl.ds(pl.multiple_of(HALF * c, 128), HALF)

        def one(k, _):
            feats = pl.ds(pl.multiple_of(256 * k, 256), 256)
            terms = lax.dot_general(
                nbx[core, :, feats], gx[core, :, columns], (((0,), (0,)), ((), ())), preferred_element_type=F32
            )
            dw[feats, :] = terms if core is c else dw[feats, :] + terms
            return 0

        lax.fori_loop(lo, hi, one, 0)

    def term(slab, yy, row, count):
        base = pl.multiple_of(CHIP * (NY * slab + yy), 8)
        parts, end = [], row + count
        while row < end:
            q, r = row // CHIP, row % CHIP
            count = min(CHIP - r, end - row)
            parts.append(dw[pl.ds(base + r, count), 128 * q : 128 * (q + 1)])
            row += count
        return jnp.concatenate(parts, axis=0)

    def far_copy(kind, slab):
        return remote(
            s1.at[slab, kind], r1.at[slab, kind], ry_s.at[0], ry_r.at[0, slab], right if kind == 0 else left
        )

    def near_copy(kind, slab):
        return remote(
            s2.at[slab, kind], r2.at[slab, kind], ry_s.at[1], ry_r.at[1, slab],
            right if kind == 0 else left,
        )

    def chain_copy(direction, slab):
        return remote(
            sz.at[slab], rz.at[direction, slab], rz_s, rz_r.at[direction, slab // 2],
            up_two if direction == 0 else down_two,
        )

    def pair_copy(slab):
        return remote(sp.at[slab // 2], rp.at[slab // 2], rp_s, rp_r.at[slab // 2], mate)

    def reduce_pair(i):
        slab = order(z, 2 * i)
        sp[slab // 2] = racc[slab].astype(BF16)
        pair_copy(slab).start()

    def reduce_pair_wait(i):
        slab = order(z, 2 * i + 1)
        pair_copy(slab).wait_recv()
        racc[slab] = racc[slab] + rp[slab // 2].astype(F32)

    def chain_v_copy(direction, slab):
        return remote(
            vz.at[slab], rv.at[direction, slab], rv_s, rv_r.at[direction, slab], up if direction == 0 else down
        )

    def reduce_far(s):
        slab = order(z, s)
        for kind in range(2):
            s1[slab, kind] = term(slab, yo, ZH * kind, ZH).astype(BF16)
            far_copy(kind, slab).start()

    def reduce_near(s):
        slab = order(z, s)
        received(r1.at[slab], ry_r.at[0, slab])
        for kind, yy in ((0, yr), (1, yl)):
            s2[slab, kind, kind] = (term(slab, yy, ZH * kind, ZH) + r1[slab, kind].astype(F32)).astype(BF16)
            s2[slab, kind, 1 - kind] = term(slab, yy, ZH * (1 - kind), ZH).astype(BF16)
            near_copy(kind, slab).start()

    def reduce_row(s):
        slab = order(z, s)
        received(r2.at[slab], ry_r.at[1, slab])
        for p in range(2):
            racc[slab, p] = term(slab, y, ZH * p, ZH) + r2[slab, 0, p].astype(F32) + r2[slab, 1, p].astype(F32)

    def reduce_chain(u):
        reduce_pair_wait(u)
        if u == pairs - 1:
            for direction, here in ((0, pair > 0), (1, pair < pairs - 1)):
                @pl.when(here)
                def _():
                    chain_copy(direction, z).wait_recv()
                    racc[z] = racc[z] + rz[direction, z].astype(F32)

            return

        far = pairs - 1 - u
        for direction, slab, here, later in (
            (0, z + 2 * far, pair <= u, pair > 0), (1, z - 2 * far, pair >= far, pair < pairs - 1),
        ):
            @pl.when(here)
            def _():
                @pl.when(later)
                def _():
                    chain_copy(direction, slab).wait_recv()
                    sz[slab] = (racc[slab] + rz[direction, slab].astype(F32)).astype(BF16)

                @pl.when(jnp.logical_not(later))
                def _():
                    sz[slab] = racc[slab].astype(BF16)

                chain_copy(direction, slab).start()

    def reduce_v(u):
        if u == NZ - 1:
            for direction, here in ((0, z > 0), (1, z < NZ - 1)):
                @pl.when(here)
                def _():
                    chain_v_copy(direction, z).wait_recv()

            for k in (2, 1, 3, 0):
                yy = (y + k) % NY
                vacc[k] = term(z, yy, 2 * ZH, VR)
                for direction, here in ((0, z > 0), (1, z < NZ - 1)):
                    @pl.when(here)
                    def _():
                        vacc[k] = vacc[k] + rv[direction, z, yy].astype(F32)

                if k == 2:
                    vs1[...] = vacc[2].astype(BF16)
                    v_far(0).start()
                    v_far(1).start()
            return

        for direction, slab, here, later in (
            (0, NZ - 1 + z - u, z <= u, z > 0), (1, z - (NZ - 1) + u, z >= NZ - 1 - u, z < NZ - 1),
        ):
            @pl.when(here)
            def _():
                @pl.when(later)
                def _():
                    chain_v_copy(direction, slab).wait_recv()
                    for yy in range(NY):
                        vz[slab, yy] = (term(slab, yy, 2 * ZH, VR) + rv[direction, slab, yy].astype(F32)).astype(BF16)

                @pl.when(jnp.logical_not(later))
                def _():
                    for yy in range(NY):
                        vz[slab, yy] = term(slab, yy, 2 * ZH, VR).astype(BF16)

                chain_v_copy(direction, slab).start()

    def v_far(kind):
        part = low if kind == 0 else high
        return remote(vs1.at[part], vr1.at[part], vy_s.at[0], vy_r.at[0], right if kind == 0 else left)

    def v_near(kind):
        return remote(vs2.at[kind], vr2.at[kind], vy_s.at[1], vy_r.at[1], right if kind == 0 else left)

    def reduce_v_near():
        received(vr1, vy_r.at[0])
        vs2[0] = jnp.concatenate(
            [vacc[1, 0:VH] + vr1[0:VH].astype(F32), vacc[1, VH:VR]], axis=0
        ).astype(BF16)
        v_near(0).start()
        vs2[1] = jnp.concatenate(
            [vacc[3, 0:VH], vacc[3, VH:VR] + vr1[VH:VR].astype(F32)], axis=0
        ).astype(BF16)
        v_near(1).start()

    def reduce_v_row():
        received(vr2, vy_r.at[1])
        fbuf[c, 2 * ZH : BLOCK] = vacc[0] + vr2[0].astype(F32) + vr2[1].astype(F32)

    near_half, far_half = z // 4, 1 - z // 4

    def last_values(core):
        @pl.when(c == core)
        def _():
            make_values(far_half, True)
            out(0).start()

    def make_values(half, done):
        feats = pl.ds(pl.multiple_of(D // 2 * half, 128), D // 2)

        def one(n, _):
            columns = pl.ds(pl.multiple_of(512 * n, 512), 512)
            part = jnp.dot(nbg[:, feats], w[feats, columns], preferred_element_type=F32)
            if done:
                vout[:, columns] = ((vf[:, columns] + part) * FACTOR).astype(BF16)
            else:
                vf[:, columns] = part
            return 0

        lax.fori_loop(0, KV // 512, one, 0)

    def input_gradient(half):
        def one(k, _):
            feats = pl.ds(pl.multiple_of(D // 2 * half + 384 * k, 128), 384)
            grad = lax.dot_general(gx[c], w[feats, :], (((1,), (1,)), ((), ())), preferred_element_type=F32) * FACTOR
            ig[:, feats] = grad
            normed = hid[:, feats].astype(F32) * invb[:, 0:1]
            gacc[:, feats] = jnp.sum((grad * normed).reshape(TOK // 8, 8, 384), axis=0)
            return 0

        lax.fori_loop(0, D // 2 // 384, one, 0)

    def hidden_gradient(lo, hi):
        def one(r, _):
            rows = pl.ds(pl.multiple_of(32 * r, 32), 32)
            inverse = invb[rows, 0:1]
            normed = hid[rows, :].astype(F32) * inverse
            grad = ig[rows, :]
            along = grad * normed
            gain = grow[0:1, :]
            mean = jnp.sum(along * gain, axis=-1, keepdims=True) / D
            gh[rows, :] = (inverse * (grad * gain - normed * mean)).astype(BF16)
            return 0

        lax.fori_loop(lo, hi, one, 0)

    def gain_terms(half):
        for side in range(2):
            @pl.when(half == side)
            def _():
                for slab in range(4 * side, 4 * side + 4):
                    hsrc[slab] = jnp.zeros((8, 128), F32)
                    for r in range(3):
                        lanes = slice(128 * (window_start(slab) + r), 128 * (window_start(slab) + r + 1))
                        hsrc[slab, r : r + 1, :] = jnp.sum(gacc[:, lanes], axis=0, keepdims=True)

                    @pl.when(z != slab)
                    def _():
                        remote(hsrc.at[slab], h1.at[z], h1_s, h1_r, (g, slab * NE + e)).start()

    def gain_second():
        received(h1.at[pl.ds(0, NZ - 1)], h1_r)
        h1[z] = hsrc[z]
        h2[e] = total(h1, NZ)
        spread_start(h2, e, e_peers, h2_s, h2_r)

    def gain_step():
        received(h2.at[pl.ds(0, NE - 1)], h2_r)
        window = total(h2, NE)
        gain_grad = jnp.zeros((8, ROWS), F32)
        for r in range(3):
            hot = jnp.where(spot == lane + 128 * r, 1.0, 0.0)
            gain_grad = gain_grad + lax.dot_general(
                jnp.broadcast_to(window[r : r + 1], (8, 128)), hot, (((1,), (1,)), ((), ())),
                precision=lax.Precision.HIGHEST, preferred_element_type=F32,
            )
        newg_ref[...] = gains_ref[...] - gain_rate * gain_grad[0:1]
        out(3).start()

    def snapshot_second():
        received(sx.at[pl.ds(0, 2)], sx_r.at[1])
        szh[zh] = total(sx, NX)
        szh_copy(zh).start()

    def szh_copy(half):
        return remote(szh.at[half], szh.at[half], szh_s, szh_r, zh_peer)

    def outer_step():
        outer_in.wait()
        mom_in.wait()
        szh_copy(1 - zh).wait_recv()
        change = outer_ref[...] - (szh[0] + szh[1])[0:ROWS] / (2 * NX)
        new_moment = momentum * mom_ref[...] + change
        newm_ref[...] = new_moment
        newo_ref[...] = outer_ref[...] - outer_rate * (change + momentum * new_moment)
        out(4).start()
        out(5).start()

    def last(core):
        return remote(fbuf.at[core], fbuf.at[core], f_s, f_r, twin)

    def inner_step():
        last(1 - c).wait_recv()
        row_of = lax.broadcasted_iota(jnp.int32, (ROWS, ROWS), 0)
        column_of = lax.broadcasted_iota(jnp.int32, (ROWS, ROWS), 1)
        gain_bf = jnp.broadcast_to(gains_ref[...].astype(BF16).astype(F32), (ROWS, ROWS))
        scale = jnp.sum(jnp.where(row_of == column_of, gain_bf, 0.0), axis=1, keepdims=True) * FACTOR
        for core in range(2):
            @pl.when(c == core)
            def _():
                for j in range(FRAGS):
                    row = CHIP * (j % 4) + ROWS * core
                    grad = fbuf[j // 4, row : row + ROWS, :] * scale
                    inner = w_ref[own_columns(j), :] - inner_rate * grad
                    mixed = mixing * inner + (1.0 - mixing) * newo_ref[...]
                    neww_ref[own_columns(j), :] = jnp.where(frag_ref[0] == j, mixed, inner)

        out(2).start()

    results = (
        (vout, values_hbm), (gh, gh_hbm), (neww_ref, neww_hbm), (newg_ref, newg_hbm), (newo_ref, newo_hbm),
        (newm_ref, newm_hbm),
    )

    def out(index):
        return pltpu.make_async_copy(results[index][0], results[index][1], out_sem.at[index])

    def results_wait():
        for index in range(6):
            out(index).wait()

    def drain():
        for t in range(pairs):
            for direction, slab, here in (
                (0, z - 2 * t, jnp.logical_and(pair >= t, pair < pairs - 1)),
                (1, z + 2 * t, jnp.logical_and(pair + t < pairs, pair > 0)),
            ):
                @pl.when(here)
                def _():
                    z_copy(direction, slab).wait_send()
                    gain_z(direction, slab).wait_send()

        sent(wp.at[0, 0], agp_s)
        sent(wp.at[0, pl.ds(0, 6)], ay_s)
        sent(wp.at[0], tw_s)
        sent(s1, ry_s.at[0])
        sent(s2, ry_s.at[1])
        sent(sp, rp_s)
        sent(sz.at[pl.ds(0, pairs - 1)], rz_s)
        sent(vz.at[pl.ds(0, NZ - 1)], rv_s)
        sent(vs1, vy_s.at[0])
        sent(vs2, vy_s.at[1])
        sent(nbx.at[0], nx_s.at[0])
        sent(gx.at[0], nx_s.at[1])
        sent(fbuf.at[0], f_s)
        sent(szh.at[0], szh_s)
        sent(g0.at[0], g0_s)
        sent(g1.at[pl.ds(0, 3)], g1_s)
        sent(g2.at[pl.ds(0, pairs)], gm_s)
        sent(sx.at[pl.ds(0, 3)], sx_s)
        sent(hsrc.at[pl.ds(0, NZ - 1)], h1_s)
        sent(h2.at[pl.ds(0, NE - 1)], h2_s)

    place_gains()
    pack_own()
    barrier_wait()
    gain_twin(c).start()
    gather_own()
    pass_token(0)
    gv_in.wait()
    nx_gv(c).start()
    hid_in.wait()
    normalise(0, 4)
    nx_nb(c, 0).start()
    normalise(4, 8)
    nx_nb(c, 1).start()
    gain_chip()
    place_snapshot()
    weight_terms(c, 0, 5)
    weight_terms(c, 5, 9)
    gain_near()
    gather_y(0)
    gather_mate(0)
    nx_gv(1 - c).wait_recv()
    received(nbx.at[1 - c], nx_r.at[0])
    weight_terms(1 - c, 0, 5)
    gather_z(1)
    pass_token(1)
    weight_terms(1 - c, 5, 9)
    reduce_v(0)
    reduce_far(0)
    reduce_far(1)
    pass_token(2)
    gain_slab()
    gather_y(1)
    gather_twin(0)
    gather_mate(1)
    gather_z(2)
    snapshot_near()
    reduce_v(1)
    pass_token(3)
    reduce_near(0)
    reduce_near(1)
    gather_y(2)
    gather_gain(1)
    gather_mate(2)
    pass_token(4)
    gather_twin(1)
    reduce_v(2)
    gather_y(3)
    gather_z(3)
    pass_token(5)
    reduce_far(2)
    reduce_far(3)
    gather_twin(2)
    gather_gain(2)
    gather_y(4)
    reduce_v(3)
    gather_mate(3)
    gather_twin(3)
    pass_token(6)
    gather_y(5)
    reduce_row(0)
    reduce_row(1)
    reduce_pair(0)
    reduce_near(2)
    reduce_near(3)
    pass_token(7)
    snapshot_second()
    gather_gain(3)
    reduce_v(4)
    gather_twin(4)
    gather_y(6)
    unpack(0, 4)
    reduce_far(4)
    reduce_far(5)
    reduce_chain(0)
    input_gradient(near_half)
    gain_terms(near_half)
    gather_twin(5)
    gather_y(7)
    reduce_v(5)
    reduce_row(2)
    reduce_row(3)
    reduce_pair(1)
    gain_all()
    gain_vector()
    apply_gain()
    reduce_near(4)
    reduce_near(5)
    reduce_far(6)
    reduce_far(7)
    gather_twin(6)
    gather_twin(7)
    reduce_v(6)
    reduce_chain(1)
    unpack(4, 8)
    input_gradient(far_half)
    gain_terms(far_half)
    reduce_row(4)
    reduce_row(5)
    reduce_pair(2)
    reduce_near(6)
    reduce_near(7)
    reduce_v(7)
    make_values(near_half, False)
    reduce_chain(2)
    reduce_row(6)
    reduce_pair(3)
    reduce_row(7)
    reduce_v_near()
    hidden_gradient(0, 8)
    out(1).start()
    gain_second()
    reduce_v_row()
    reduce_chain(3)
    fbuf[c, 0 : 2 * ZH] = racc[z].reshape(2 * ZH, 128)
    last(c).start()
    outer_step()
    last_values(1)
    inner_step()
    last_values(0)
    drain()
    gain_step()
    results_wait()


def place_kernel(*refs):
    sources, targets, held, in_sem, out_sem = refs[:6], refs[6:12], refs[12:18], refs[18], refs[19]
    slices = [(1, pl.ds(64 * k, 64)) for k in range(4)] + [(0, pl.ds(128 * k, 128)) for k in range(2)]
    parts = [(s.at[rows], h.at[rows], t.at[rows]) for i, rows in slices for s, h, t in [(sources[i], held[i], targets[i])]]
    parts += [(sources[i], held[i], targets[i]) for i in range(2, 6)]
    arrive = [pltpu.make_async_copy(s, h, in_sem.at[k]) for k, (s, h, _) in enumerate(parts)]
    leave = [pltpu.make_async_copy(h, t, out_sem.at[k]) for k, (_, h, t) in enumerate(parts)]
    for copy in arrive:
        copy.start()
    for one, other in zip(arrive, leave):
        one.wait()
        other.start()
    for copy in leave:
        copy.wait()


def body(hidden, grad_values, weights, gains, snapshot, outer_frag, outer_moment, fragment_index):
    anywhere = pl.BlockSpec(memory_space=pl.ANY)
    dma = pltpu.SemaphoreType.DMA
    vmem = pltpu.VMEM
    shapes = (
        jax.ShapeDtypeStruct((TOK, KV), BF16),
        jax.ShapeDtypeStruct((TOK, D), BF16),
        jax.ShapeDtypeStruct((ROWS * FRAGS, 128), F32),
        jax.ShapeDtypeStruct((1, ROWS), F32),
        jax.ShapeDtypeStruct((ROWS, FW), F32),
        jax.ShapeDtypeStruct((ROWS, FW), F32),
    )
    results = pl.pallas_call(
        step_kernel,
        out_shape=shapes,
        in_specs=[pl.BlockSpec(memory_space=pltpu.SMEM)] + [anywhere] * 7,
        out_specs=(anywhere,) * 6,
        scratch_shapes=[
            vmem((TOK, D), BF16),
            vmem((2, TOK, KV), BF16),
            vmem((2, TOK, D), BF16),
            vmem((TOK, D), BF16),
            vmem((2, NZ, NY, BLOCK, 128), BF16),
            vmem((D, KV), BF16),
            vmem((SLAB, KV), F32),
            vmem((BLOCK, 128), F32),
            vmem((D, HALF), F32),
            vmem((NZ, 2, ZH, 128), BF16),
            vmem((NZ, 2, ZH, 128), BF16),
            vmem((NZ, 2, 2, ZH, 128), BF16),
            vmem((NZ, 2, 2, ZH, 128), BF16),
            vmem((NZ, 2, ZH, 128), F32),
            vmem((NZ // 2, 2, ZH, 128), BF16),
            vmem((NZ // 2, 2, ZH, 128), BF16),
            vmem((NZ, 2, ZH, 128), BF16),
            vmem((2, NZ, 2, ZH, 128), BF16),
            vmem((NY, VR, 128), F32),
            vmem((VR, 128), BF16),
            vmem((VR, 128), BF16),
            vmem((2, VR, 128), BF16),
            vmem((2, VR, 128), BF16),
            vmem((NZ, NY, VR, 128), BF16),
            vmem((2, NZ, NY, VR, 128), BF16),
            vmem((2, BLOCK, 128), F32),
            vmem((TOK, D), F32),
            vmem((TOK, KV), F32),
            vmem((TOK, KV), BF16),
            vmem((TOK, D), BF16),
            vmem((TOK, 128), F32),
            vmem((8, D), F32),
            vmem((8, D), F32),
            vmem((2, 8, 128), F32),
            vmem((NY, 8, 128), F32),
            vmem((NZ, 8, 128), F32),
            vmem((NZ, 8, 128), F32),
            vmem((NZ, 8, 128), F32),
            vmem((NE, 8, 128), F32),
            vmem((NX, 40, 128), F32),
            vmem((2, 40, 128), F32),
            vmem((ROWS * FRAGS, 128), F32),
            vmem((1, ROWS), F32),
            vmem((ROWS, 1, FW), F32),
            vmem((ROWS, FW), F32),
            vmem((ROWS, FW), F32),
            vmem((ROWS * FRAGS, 128), F32),
            vmem((1, ROWS), F32),
            vmem((ROWS, FW), F32),
            vmem((ROWS, FW), F32),
            dma((7,)), dma((6,)),
            dma((2, NZ // 2)), dma((NZ // 2,)), dma, dma((NZ // 2,)),
            dma, dma((2, NZ)),
            dma, dma((NZ,)),
            dma((2,)), dma((2,)),
            dma((2,)), dma((2, NZ)),
            dma, dma((NZ // 2,)),
            dma, dma((2, NZ // 2)),
            dma, dma((2, NZ)),
            dma((2,)), dma((2,)),
            dma, dma,
            dma, dma,
            dma, dma((2,)),
            dma((2, NZ // 2)), dma((NZ // 2,)), dma, dma,
            dma, dma, dma, dma,
            dma, dma((2,)),
            dma, dma,
            pltpu.SemaphoreType.REGULAR((7,)),
        ],
        compiler_params=pltpu.CompilerParams(
            collective_id=0, has_side_effects=True, vmem_limit_bytes=56 * 1024 * 1024,
        ),
        cost_estimate=pl.CostEstimate(flops=3 * 2 * TOK * D * KV, bytes_accessed=4_000_000, transcendentals=0),
    )(
        fragment_index, hidden, grad_values, weights.reshape(ROWS * FRAGS, 128), gains,
        snapshot.reshape(ROWS, 1, FW), outer_frag, outer_moment,
    )
    values, grad_hidden, new_weights, new_gains, new_outer, new_moment = pl.pallas_call(
        place_kernel,
        out_shape=shapes,
        in_specs=[anywhere] * 6,
        out_specs=(anywhere,) * 6,
        scratch_shapes=[vmem(shape.shape, shape.dtype) for shape in shapes] + [dma((10,)), dma((10,))],
        compiler_params=pltpu.CompilerParams(vmem_limit_bytes=60 * 1024 * 1024),
    )(*results)
    return (values, grad_hidden, new_weights.reshape(1, ROWS, KV), new_gains, new_outer, new_moment)


def solution(mesh):
    return jax.shard_map(
        body,
        mesh=mesh,
        in_specs=(
            P(("group", "fsdp"), None),
            P(("group", "fsdp"), None),
            P("group", "fsdp", None),
            P("group", "fsdp"),
            P("group", "fsdp", None),
            P("fsdp", None),
            P("fsdp", None),
            P(),
        ),
        out_specs=(
            P(("group", "fsdp"), None),
            P(("group", "fsdp"), None),
            P("group", "fsdp", None),
            P("group", "fsdp"),
            P("fsdp", None),
            P("fsdp", None),
        ),
        check_vma=False,
    )
```

```python
import functools

import jax
import jax.numpy as jnp
from jax import lax
from jax.experimental import pallas as pl
from jax.experimental.pallas import tpu as pltpu
from jax.sharding import PartitionSpec as P

MESH = pl.DeviceIdType.MESH
F32 = jnp.float32
BF16 = jnp.bfloat16

D = 2304
KV = 1024
FW = 128
FRAGS = 8
TOK = 256
NZ = 8
NY = 4
NE = 8
NX = 4
ROWS = 36
CHIP = 72
SLAB = 288
HALF = 512

epsilon = 1e-06
inner_rate = 0.05
gain_rate = 0.002
momentum = 0.9
outer_rate = 0.7
mixing = 0.5
FACTOR = D ** (-0.5)
BLOCK = 288
AH = BLOCK // 2
ZH = 112
VR = 64
VH = VR // 2


def window_start(z):
    return (SLAB * z) // 128


def order(z, s):
    pair, odd = z // 2, z % 2
    near = 3 - s // 2
    low = jnp.where(pair % 3 == 0, near, jnp.where(near < 2, 1 - near, near))
    which = jnp.where(pair > 1, 3 - low, low)
    return 2 * which + jnp.where(s % 2 == 0, 1 - odd, odd)


def step_kernel(
    frag_ref, hid_hbm, gv_hbm, w_hbm, gains_hbm, snap_hbm, outer_hbm, mom_hbm,
    values_hbm, gh_hbm, neww_hbm, newg_hbm, newo_hbm, newm_hbm,
    hid, gx, nbx, nbg, wp, w, stage, pack, dw, s1, r1, s2, r2, racc, sp, rp, sz, rz,
    vacc, vs1, vr1, vs2, vr2, vz, rv, fbuf,
    ig, vf, vout, gh, invb, grow, gacc, g0, g1, g2, hsrc, h1, h2, sx, szh,
    w_ref, gains_ref, snap_ref, outer_ref, mom_ref, neww_ref, newg_ref, newo_ref, newm_ref,
    in_sem, out_sem, agz_s, agz_r, agp_s, agp_r, ay_s, ay_r, tw_s, tw_r, nx_s, nx_r,
    ry_s, ry_r, rp_s, rp_r, rz_s, rz_r, rv_s, rv_r, vy_s, vy_r, f_s, f_r,
    g0_s, g0_r, g1_s, g1_r, g2_s, g2_r, gm_s, gm_r, h1_s, h1_r, h2_s, h2_r, sx_s, sx_r, szh_s, szh_r, token,
):
    g = lax.axis_index("group")
    f = lax.axis_index("fsdp")
    x, zh = g // 2, g % 2
    z, e = f // NE, f % NE
    y, c = e // 2, e % 2
    yr, yl, yo = (y + 1) % NY, (y + 3) % NY, (y + 2) % NY
    twin = (g, f + 1 - 2 * c)

    def at(zz, yy):
        return (g, zz * NE + yy * 2 + c)

    right, left = at(z, yr), at(z, yl)
    up, down = at(z + 1, y), at(z - 1, y)
    mate, up_two, down_two = at(z + 1 - 2 * (z % 2), y), at(z + 2, y), at(z - 2, y)
    pair, z_mate = z // 2, z + 1 - 2 * (z % 2)
    pairs = NZ // 2
    e_peers = [((e + k) % NE, (g, z * NE + (e + k) % NE)) for k in range(1, NE)]
    z_peers = [((z + k) % NZ, (g, ((z + k) % NZ) * NE + e)) for k in range(1, NZ)]
    xr, xl, xo = (x + 1) % NX, (x + 3) % NX, (x + 2) % NX
    x_right, x_left = (xr * 2 + zh, f), (xl * 2 + zh, f)
    after = (x * 2 + (zh + (z + 1) // NZ) % 2, ((z + 1) % NZ) * NE + e)
    before = (x * 2 + (zh + (NZ - z) // NZ) % 2, ((z + NZ - 1) % NZ) * NE + e)
    zh_peer = (x * 2 + 1 - zh, f)

    def remote(src, dst, send, recv, device):
        return pltpu.make_async_remote_copy(
            src_ref=src, dst_ref=dst, send_sem=send, recv_sem=recv, device_id=device, device_id_type=MESH
        )

    def received(ref, sem):
        remote(ref, ref, sem, sem, twin).wait_recv()

    def sent(ref, sem):
        remote(ref, ref, sem, sem, twin).wait_send()

    barrier = pltpu.get_barrier_semaphore()
    peers = [before, after, right, left, x_right, x_left, twin]
    two_after, two_before = at((z + 2) % NZ, y), at((z + NZ - 2) % NZ, y)
    peers += [two_after, two_before]
    for peer in peers:
        pl.semaphore_signal(barrier, inc=1, device_id=peer, device_id_type=MESH)

    w_in = pltpu.make_async_copy(w_hbm, w_ref, in_sem.at[0])
    gains_in = pltpu.make_async_copy(gains_hbm, gains_ref, in_sem.at[1])
    snap_in = pltpu.make_async_copy(snap_hbm, snap_ref, in_sem.at[2])
    hid_in = pltpu.make_async_copy(hid_hbm, hid, in_sem.at[3])
    gv_in = pltpu.make_async_copy(gv_hbm, gx.at[c], in_sem.at[4])
    outer_in = pltpu.make_async_copy(outer_hbm, outer_ref, in_sem.at[5])
    mom_in = pltpu.make_async_copy(mom_hbm, mom_ref, in_sem.at[6])
    for copy in (gains_in, w_in, hid_in, gv_in, snap_in, outer_in, mom_in):
        copy.start()

    def own_columns(j):
        return pl.ds(j, ROWS, stride=FRAGS)

    def pack_own():
        w_in.wait()
        for q in range(FRAGS):
            pack[ROWS * q : ROWS * (q + 1), :] = w_ref[own_columns(q), :]
        wp[c, z, y] = pack[...].astype(BF16)

    first_lane = ROWS * f - 128 * window_start(z)
    spot = lax.broadcasted_iota(jnp.int32, (ROWS, 128), 0) + first_lane
    lane = lax.broadcasted_iota(jnp.int32, (ROWS, 128), 1)

    def place_gains():
        gains_in.wait()
        gain_own = jnp.broadcast_to(gains_ref[...].astype(BF16), (8, ROWS))
        g0[c] = jnp.zeros((8, 128), F32)
        for r in range(3):
            hot = jnp.where(spot == lane + 128 * r, 1.0, 0.0).astype(BF16)
            g0[c, r : r + 1, :] = jnp.dot(gain_own, hot, preferred_element_type=F32)[0:1]

    def gain_twin(core):
        return remote(g0.at[core], g0.at[core], g0_s, g0_r, twin)

    def gain_y(kind):
        row = y if kind < 2 else yl
        return remote(
            g1.at[row], g1.at[row], g1_s, g1_r.at[0 if kind == 0 else 1], left if kind == 1 else right
        )

    def gain_z(direction, slab):
        ref = g2.at[slab]
        return remote(
            ref, ref, g2_s.at[direction, slab // 2], g2_r.at[slab // 2], up_two if direction == 0 else down_two
        )

    def gain_mate(slab):
        return remote(g2.at[slab], g2.at[slab], gm_s, gm_r, mate)

    def gain_chip():
        gain_twin(1 - c).wait_recv()
        g1[y] = g0[0] + g0[1]
        gain_y(0).start()
        gain_y(1).start()

    def gain_near():
        received(g1.at[yl], g1_r.at[0])
        gain_y(2).start()

    def gain_slab():
        received(g1.at[pl.ds(0, 2)], g1_r.at[1])
        g2[z] = total(g1, NY)
        both_ways_two(lambda direction: gain_z(direction, z).start())
        gain_mate(z).start()

    def gather_gain(t):
        for direction, slab, here, more in (
            (0, z - 2 * t, pair >= t, pair < pairs - 1), (1, z + 2 * t, pair + t < pairs, pair > 0),
        ):
            @pl.when(here)
            def _():
                gain_z(direction, slab).wait_recv()

                @pl.when(more)
                def _():
                    gain_z(direction, slab).start()

                gain_mate(slab).start()

    def gain_all():
        received(g2.at[pl.ds(0, pairs)], gm_r)

    def snap_x(kind):
        row = x if kind < 2 else xl
        return remote(
            sx.at[row], sx.at[row], sx_s, sx_r.at[0 if kind == 0 else 1], x_left if kind == 1 else x_right
        )

    def place_snapshot():
        snap_in.wait()
        sx[x] = jnp.zeros((40, 128), F32)
        sx[x, 0:ROWS, :] = snap_ref[...].reshape(ROWS, 128)
        snap_x(0).start()
        snap_x(1).start()

    def snapshot_near():
        received(sx.at[xl], sx_r.at[0])
        snap_x(2).start()

    def pass_token(t):
        if t > 0:
            pl.semaphore_wait(token.at[t - 1], 1)
        if t < NZ - 1:
            pl.semaphore_signal(token.at[t], inc=1, device_id=after, device_id_type=MESH)

    def barrier_wait():
        pl.semaphore_wait(barrier, len(peers))

    def spread_start(buf, own, peer_list, send, recv):
        for _, peer in peer_list:
            remote(buf.at[own], buf.at[own], send, recv, peer).start()

    def total(buf, count):
        result = buf[0]
        for index in range(1, count):
            result = result + buf[index]
        return result

    halves = (pl.ds(0, AH), pl.ds(AH, AH))

    def z_copy(direction, slab):
        ref = wp.at[c, slab, y]
        return remote(
            ref, ref, agz_s.at[direction, slab // 2], agz_r.at[slab // 2], up_two if direction == 0 else down_two
        )

    def mate_copy(slab):
        ref = wp.at[c, slab, y]
        return remote(ref, ref, agp_s, agp_r.at[slab // 2], mate)

    def y_copy(kind, slab):
        device = right if kind in (0, 2) else left
        if kind < 2:
            ref = wp.at[c, slab, y]
        elif kind == 2:
            ref = wp.at[c, slab, yl, halves[0]]
        else:
            ref = wp.at[c, slab, yr, halves[1]]
        return remote(ref, ref, ay_s, ay_r.at[kind // 2, slab], device)

    low, high = pl.ds(0, VH), pl.ds(VH, VH)

    def twin_copy(slab, core):
        return remote(wp.at[core, slab], wp.at[core, slab], tw_s, tw_r.at[slab], twin)

    def both_ways_two(send):
        @pl.when(pair < pairs - 1)
        def _():
            send(0)

        @pl.when(pair > 0)
        def _():
            send(1)

    def gather_own():
        both_ways_two(lambda direction: z_copy(direction, z).start())
        y_copy(0, z).start()
        y_copy(1, z).start()
        mate_copy(z).start()

    def gather_z(t):
        for direction, slab, here, more in (
            (0, z - 2 * t, pair >= t, pair < pairs - 1), (1, z + 2 * t, pair + t < pairs, pair > 0),
        ):
            @pl.when(here)
            def _():
                z_copy(direction, slab).wait_recv()

                @pl.when(more)
                def _():
                    z_copy(direction, slab).start()

                mate_copy(slab).start()
                y_copy(0, slab).start()
                y_copy(1, slab).start()

    def gather_mate(t):
        sides = ((z_mate, pair >= 0),) if t == 0 else ((z_mate - 2 * t, pair >= t), (z_mate + 2 * t, pair + t < pairs))
        for slab, here in sides:
            @pl.when(here)
            def _():
                mate_copy(slab).wait_recv()
                y_copy(0, slab).start()
                y_copy(1, slab).start()

    def gather_y(j):
        slab = order(z, 7 - j)
        received(wp.at[c, slab, pl.ds(0, 2)], ay_r.at[0, slab])
        y_copy(2, slab).start()
        y_copy(3, slab).start()

    def gather_twin(j):
        slab = order(z, 7 - j)
        received(wp.at[c, slab, yo], ay_r.at[1, slab])
        twin_copy(slab, c).start()

    def unpack(lo, hi):
        def one(j, _):
            slab = order(z, 7 - j)
            twin_copy(slab, 1 - c).wait_recv()
            for core in range(2):
                for yy in range(NY):
                    block = wp[core, slab, yy].astype(F32)
                    base = ROWS * (2 * yy + core)
                    for q in range(FRAGS):
                        stage[base : base + ROWS, 128 * q : 128 * (q + 1)] = block[ROWS * q : ROWS * (q + 1)]
            w[pl.ds(pl.multiple_of(SLAB * slab, 16), SLAB), :] = stage[...].astype(BF16)
            return 0

        lax.fori_loop(lo, hi, one, 0)

    def normalise(lo, hi):
        def one(r, _):
            rows = pl.ds(pl.multiple_of(32 * r, 32), 32)
            tokens = hid[rows, :].astype(F32)
            inverse = lax.rsqrt(jnp.sum(tokens * tokens, axis=-1, keepdims=True) / D + epsilon)
            invb[rows, :] = jnp.broadcast_to(inverse, (32, 128))
            nbx[c, rows, :] = (tokens * inverse).astype(BF16)
            return 0

        lax.fori_loop(lo, hi, one, 0)

    def gain_vector():
        grow[...] = jnp.zeros((8, D), F32)
        for slab in range(NZ):
            for r in range(3):
                lanes = slice(128 * (window_start(slab) + r), 128 * (window_start(slab) + r + 1))
                grow[0:1, lanes] = grow[0:1, lanes] + g2[slab, r : r + 1, :]

    def apply_gain():
        def one(r, _):
            rows = pl.ds(pl.multiple_of(32 * r, 32), 32)
            normed = hid[rows, :].astype(F32) * invb[rows, 0:1]
            nbg[rows, :] = (normed * grow[0:1, :]).astype(BF16)
            return 0

        lax.fori_loop(0, TOK // 32, one, 0)

    def nx_nb(core, half):
        ref = nbx.at[core, pl.ds(half * TOK // 2, TOK // 2)]
        return remote(ref, ref, nx_s.at[0], nx_r.at[0], twin)

    def nx_gv(core):
        return remote(gx.at[core], gx.at[core], nx_s.at[1], nx_r.at[1], twin)

    def weight_terms(core, lo, hi):
        columns = pl.ds(pl.multiple_of(HALF * c, 128), HALF)

        def one(k, _):
            feats = pl.ds(pl.multiple_of(256 * k, 256), 256)
            terms = lax.dot_general(
                nbx[core, :, feats], gx[core, :, columns], (((0,), (0,)), ((), ())), preferred_element_type=F32
            )
            dw[feats, :] = terms if core is c else dw[feats, :] + terms
            return 0

        lax.fori_loop(lo, hi, one, 0)

    def term(slab, yy, row, count):
        base = pl.multiple_of(CHIP * (NY * slab + yy), 8)
        parts, end = [], row + count
        while row < end:
            q, r = row // CHIP, row % CHIP
            count = min(CHIP - r, end - row)
            parts.append(dw[pl.ds(base + r, count), 128 * q : 128 * (q + 1)])
            row += count
        return jnp.concatenate(parts, axis=0)

    def far_copy(kind, slab):
        return remote(
            s1.at[slab, kind], r1.at[slab, kind], ry_s.at[0], ry_r.at[0, slab], right if kind == 0 else left
        )

    def near_copy(kind, slab):
        return remote(
            s2.at[slab, kind], r2.at[slab, kind], ry_s.at[1], ry_r.at[1, slab],
            right if kind == 0 else left,
        )

    def chain_copy(direction, slab):
        return remote(
            sz.at[slab], rz.at[direction, slab], rz_s, rz_r.at[direction, slab // 2],
            up_two if direction == 0 else down_two,
        )

    def pair_copy(slab):
        return remote(sp.at[slab // 2], rp.at[slab // 2], rp_s, rp_r.at[slab // 2], mate)

    def reduce_pair(i):
        slab = order(z, 2 * i)
        sp[slab // 2] = racc[slab].astype(BF16)
        pair_copy(slab).start()

    def reduce_pair_wait(i):
        slab = order(z, 2 * i + 1)
        pair_copy(slab).wait_recv()
        racc[slab] = racc[slab] + rp[slab // 2].astype(F32)

    def chain_v_copy(direction, slab):
        return remote(
            vz.at[slab], rv.at[direction, slab], rv_s, rv_r.at[direction, slab], up if direction == 0 else down
        )

    def reduce_far(s):
        slab = order(z, s)
        for kind in range(2):
            s1[slab, kind] = term(slab, yo, ZH * kind, ZH).astype(BF16)
            far_copy(kind, slab).start()

    def reduce_near(s):
        slab = order(z, s)
        received(r1.at[slab], ry_r.at[0, slab])
        for kind, yy in ((0, yr), (1, yl)):
            s2[slab, kind, kind] = (term(slab, yy, ZH * kind, ZH) + r1[slab, kind].astype(F32)).astype(BF16)
            s2[slab, kind, 1 - kind] = term(slab, yy, ZH * (1 - kind), ZH).astype(BF16)
            near_copy(kind, slab).start()

    def reduce_row(s):
        slab = order(z, s)
        received(r2.at[slab], ry_r.at[1, slab])
        for p in range(2):
            racc[slab, p] = term(slab, y, ZH * p, ZH) + r2[slab, 0, p].astype(F32) + r2[slab, 1, p].astype(F32)

    def reduce_chain(u):
        reduce_pair_wait(u)
        if u == pairs - 1:
            for direction, here in ((0, pair > 0), (1, pair < pairs - 1)):
                @pl.when(here)
                def _():
                    chain_copy(direction, z).wait_recv()
                    racc[z] = racc[z] + rz[direction, z].astype(F32)

            return

        far = pairs - 1 - u
        for direction, slab, here, later in (
            (0, z + 2 * far, pair <= u, pair > 0), (1, z - 2 * far, pair >= far, pair < pairs - 1),
        ):
            @pl.when(here)
            def _():
                @pl.when(later)
                def _():
                    chain_copy(direction, slab).wait_recv()
                    sz[slab] = (racc[slab] + rz[direction, slab].astype(F32)).astype(BF16)

                @pl.when(jnp.logical_not(later))
                def _():
                    sz[slab] = racc[slab].astype(BF16)

                chain_copy(direction, slab).start()

    def reduce_v(u):
        if u == NZ - 1:
            for direction, here in ((0, z > 0), (1, z < NZ - 1)):
                @pl.when(here)
                def _():
                    chain_v_copy(direction, z).wait_recv()

            for k in (2, 1, 3, 0):
                yy = (y + k) % NY
                vacc[k] = term(z, yy, 2 * ZH, VR)
                for direction, here in ((0, z > 0), (1, z < NZ - 1)):
                    @pl.when(here)
                    def _():
                        vacc[k] = vacc[k] + rv[direction, z, yy].astype(F32)

                if k == 2:
                    vs1[...] = vacc[2].astype(BF16)
                    v_far(0).start()
                    v_far(1).start()
            return

        for direction, slab, here, later in (
            (0, NZ - 1 + z - u, z <= u, z > 0), (1, z - (NZ - 1) + u, z >= NZ - 1 - u, z < NZ - 1),
        ):
            @pl.when(here)
            def _():
                @pl.when(later)
                def _():
                    chain_v_copy(direction, slab).wait_recv()
                    for yy in range(NY):
                        vz[slab, yy] = (term(slab, yy, 2 * ZH, VR) + rv[direction, slab, yy].astype(F32)).astype(BF16)

                @pl.when(jnp.logical_not(later))
                def _():
                    for yy in range(NY):
                        vz[slab, yy] = term(slab, yy, 2 * ZH, VR).astype(BF16)

                chain_v_copy(direction, slab).start()

    def v_far(kind):
        part = low if kind == 0 else high
        return remote(vs1.at[part], vr1.at[part], vy_s.at[0], vy_r.at[0], right if kind == 0 else left)

    def v_near(kind):
        return remote(vs2.at[kind], vr2.at[kind], vy_s.at[1], vy_r.at[1], right if kind == 0 else left)

    def reduce_v_near():
        received(vr1, vy_r.at[0])
        vs2[0] = jnp.concatenate(
            [vacc[1, 0:VH] + vr1[0:VH].astype(F32), vacc[1, VH:VR]], axis=0
        ).astype(BF16)
        v_near(0).start()
        vs2[1] = jnp.concatenate(
            [vacc[3, 0:VH], vacc[3, VH:VR] + vr1[VH:VR].astype(F32)], axis=0
        ).astype(BF16)
        v_near(1).start()

    def reduce_v_row():
        received(vr2, vy_r.at[1])
        fbuf[c, 2 * ZH : BLOCK] = vacc[0] + vr2[0].astype(F32) + vr2[1].astype(F32)

    near_half, far_half = z // 4, 1 - z // 4

    def last_values(core):
        @pl.when(c == core)
        def _():
            make_values(far_half, True)
            out(0).start()

    def make_values(half, done):
        feats = pl.ds(pl.multiple_of(D // 2 * half, 128), D // 2)

        def one(n, _):
            columns = pl.ds(pl.multiple_of(512 * n, 512), 512)
            part = jnp.dot(nbg[:, feats], w[feats, columns], preferred_element_type=F32)
            if done:
                vout[:, columns] = ((vf[:, columns] + part) * FACTOR).astype(BF16)
            else:
                vf[:, columns] = part
            return 0

        lax.fori_loop(0, KV // 512, one, 0)

    def input_gradient(half):
        def one(k, _):
            feats = pl.ds(pl.multiple_of(D // 2 * half + 384 * k, 128), 384)
            grad = lax.dot_general(gx[c], w[feats, :], (((1,), (1,)), ((), ())), preferred_element_type=F32) * FACTOR
            ig[:, feats] = grad
            normed = hid[:, feats].astype(F32) * invb[:, 0:1]
            gacc[:, feats] = jnp.sum((grad * normed).reshape(TOK // 8, 8, 384), axis=0)
            return 0

        lax.fori_loop(0, D // 2 // 384, one, 0)

    def hidden_gradient(lo, hi):
        def one(r, _):
            rows = pl.ds(pl.multiple_of(32 * r, 32), 32)
            inverse = invb[rows, 0:1]
            normed = hid[rows, :].astype(F32) * inverse
            grad = ig[rows, :]
            along = grad * normed
            gain = grow[0:1, :]
            mean = jnp.sum(along * gain, axis=-1, keepdims=True) / D
            gh[rows, :] = (inverse * (grad * gain - normed * mean)).astype(BF16)
            return 0

        lax.fori_loop(lo, hi, one, 0)

    def gain_terms(half):
        for side in range(2):
            @pl.when(half == side)
            def _():
                for slab in range(4 * side, 4 * side + 4):
                    hsrc[slab] = jnp.zeros((8, 128), F32)
                    for r in range(3):
                        lanes = slice(128 * (window_start(slab) + r), 128 * (window_start(slab) + r + 1))
                        hsrc[slab, r : r + 1, :] = jnp.sum(gacc[:, lanes], axis=0, keepdims=True)

                    @pl.when(z != slab)
                    def _():
                        remote(hsrc.at[slab], h1.at[z], h1_s, h1_r, (g, slab * NE + e)).start()

    def gain_second():
        received(h1.at[pl.ds(0, NZ - 1)], h1_r)
        h1[z] = hsrc[z]
        h2[e] = total(h1, NZ)
        spread_start(h2, e, e_peers, h2_s, h2_r)

    def gain_step():
        received(h2.at[pl.ds(0, NE - 1)], h2_r)
        window = total(h2, NE)
        gain_grad = jnp.zeros((8, ROWS), F32)
        for r in range(3):
            hot = jnp.where(spot == lane + 128 * r, 1.0, 0.0)
            gain_grad = gain_grad + lax.dot_general(
                jnp.broadcast_to(window[r : r + 1], (8, 128)), hot, (((1,), (1,)), ((), ())),
                precision=lax.Precision.HIGHEST, preferred_element_type=F32,
            )
        newg_ref[...] = gains_ref[...] - gain_rate * gain_grad[0:1]
        out(3).start()

    def snapshot_second():
        received(sx.at[pl.ds(0, 2)], sx_r.at[1])
        szh[zh] = total(sx, NX)
        szh_copy(zh).start()

    def szh_copy(half):
        return remote(szh.at[half], szh.at[half], szh_s, szh_r, zh_peer)

    def outer_step():
        outer_in.wait()
        mom_in.wait()
        szh_copy(1 - zh).wait_recv()
        change = outer_ref[...] - (szh[0] + szh[1])[0:ROWS] / (2 * NX)
        new_moment = momentum * mom_ref[...] + change
        newm_ref[...] = new_moment
        newo_ref[...] = outer_ref[...] - outer_rate * (change + momentum * new_moment)
        out(4).start()
        out(5).start()

    def last(core):
        return remote(fbuf.at[core], fbuf.at[core], f_s, f_r, twin)

    def inner_step():
        last(1 - c).wait_recv()
        row_of = lax.broadcasted_iota(jnp.int32, (ROWS, ROWS), 0)
        column_of = lax.broadcasted_iota(jnp.int32, (ROWS, ROWS), 1)
        gain_bf = jnp.broadcast_to(gains_ref[...].astype(BF16).astype(F32), (ROWS, ROWS))
        scale = jnp.sum(jnp.where(row_of == column_of, gain_bf, 0.0), axis=1, keepdims=True) * FACTOR
        for core in range(2):
            @pl.when(c == core)
            def _():
                for j in range(FRAGS):
                    row = CHIP * (j % 4) + ROWS * core
                    grad = fbuf[j // 4, row : row + ROWS, :] * scale
                    inner = w_ref[own_columns(j), :] - inner_rate * grad
                    mixed = mixing * inner + (1.0 - mixing) * newo_ref[...]
                    neww_ref[own_columns(j), :] = jnp.where(frag_ref[0] == j, mixed, inner)

        out(2).start()

    results = (
        (vout, values_hbm), (gh, gh_hbm), (neww_ref, neww_hbm), (newg_ref, newg_hbm), (newo_ref, newo_hbm),
        (newm_ref, newm_hbm),
    )

    def out(index):
        return pltpu.make_async_copy(results[index][0], results[index][1], out_sem.at[index])

    def results_wait():
        for index in range(6):
            out(index).wait()

    def drain():
        for t in range(pairs):
            for direction, slab, here in (
                (0, z - 2 * t, jnp.logical_and(pair >= t, pair < pairs - 1)),
                (1, z + 2 * t, jnp.logical_and(pair + t < pairs, pair > 0)),
            ):
                @pl.when(here)
                def _():
                    z_copy(direction, slab).wait_send()
                    gain_z(direction, slab).wait_send()

        sent(wp.at[0, 0], agp_s)
        sent(wp.at[0, pl.ds(0, 6)], ay_s)
        sent(wp.at[0], tw_s)
        sent(s1, ry_s.at[0])
        sent(s2, ry_s.at[1])
        sent(sp, rp_s)
        sent(sz.at[pl.ds(0, pairs - 1)], rz_s)
        sent(vz.at[pl.ds(0, NZ - 1)], rv_s)
        sent(vs1, vy_s.at[0])
        sent(vs2, vy_s.at[1])
        sent(nbx.at[0], nx_s.at[0])
        sent(gx.at[0], nx_s.at[1])
        sent(fbuf.at[0], f_s)
        sent(szh.at[0], szh_s)
        sent(g0.at[0], g0_s)
        sent(g1.at[pl.ds(0, 3)], g1_s)
        sent(g2.at[pl.ds(0, pairs)], gm_s)
        sent(sx.at[pl.ds(0, 3)], sx_s)
        sent(hsrc.at[pl.ds(0, NZ - 1)], h1_s)
        sent(h2.at[pl.ds(0, NE - 1)], h2_s)

    place_gains()
    pack_own()
    barrier_wait()
    gain_twin(c).start()
    gather_own()
    pass_token(0)
    gv_in.wait()
    nx_gv(c).start()
    hid_in.wait()
    normalise(0, 4)
    nx_nb(c, 0).start()
    normalise(4, 8)
    nx_nb(c, 1).start()
    gain_chip()
    place_snapshot()
    weight_terms(c, 0, 5)
    weight_terms(c, 5, 9)
    gain_near()
    gather_y(0)
    gather_mate(0)
    nx_gv(1 - c).wait_recv()
    received(nbx.at[1 - c], nx_r.at[0])
    weight_terms(1 - c, 0, 5)
    gather_z(1)
    pass_token(1)
    weight_terms(1 - c, 5, 9)
    reduce_v(0)
    reduce_far(0)
    reduce_far(1)
    pass_token(2)
    gain_slab()
    gather_y(1)
    gather_twin(0)
    gather_mate(1)
    gather_z(2)
    snapshot_near()
    reduce_v(1)
    pass_token(3)
    reduce_near(0)
    reduce_near(1)
    gather_y(2)
    gather_gain(1)
    gather_mate(2)
    pass_token(4)
    gather_twin(1)
    reduce_v(2)
    gather_y(3)
    gather_z(3)
    pass_token(5)
    reduce_far(2)
    reduce_far(3)
    reduce_v(3)
    gather_twin(2)
    gather_gain(2)
    gather_y(4)
    gather_mate(3)
    gather_twin(3)
    pass_token(6)
    gather_y(5)
    reduce_row(0)
    reduce_row(1)
    reduce_pair(0)
    reduce_v(4)
    reduce_near(2)
    reduce_near(3)
    pass_token(7)
    snapshot_second()
    gather_gain(3)
    gather_twin(4)
    gather_y(6)
    unpack(0, 4)
    reduce_far(4)
    reduce_far(5)
    reduce_chain(0)
    input_gradient(near_half)
    gain_terms(near_half)
    gather_twin(5)
    gather_y(7)
    reduce_v(5)
    reduce_row(2)
    reduce_row(3)
    reduce_pair(1)
    gain_all()
    gain_vector()
    apply_gain()
    reduce_near(4)
    reduce_near(5)
    reduce_far(6)
    reduce_far(7)
    gather_twin(6)
    gather_twin(7)
    reduce_v(6)
    reduce_chain(1)
    unpack(4, 8)
    input_gradient(far_half)
    gain_terms(far_half)
    reduce_row(4)
    reduce_row(5)
    reduce_pair(2)
    reduce_near(6)
    reduce_near(7)
    reduce_v(7)
    make_values(near_half, False)
    reduce_chain(2)
    reduce_row(6)
    reduce_pair(3)
    reduce_row(7)
    reduce_v_near()
    hidden_gradient(0, 8)
    out(1).start()
    gain_second()
    reduce_v_row()
    reduce_chain(3)
    fbuf[c, 0 : 2 * ZH] = racc[z].reshape(2 * ZH, 128)
    last(c).start()
    outer_step()
    last_values(1)
    inner_step()
    last_values(0)
    drain()
    gain_step()
    results_wait()


def place_kernel(*refs):
    sources, targets, held, in_sem, out_sem = refs[:6], refs[6:12], refs[12:18], refs[18], refs[19]
    slices = [(1, pl.ds(64 * k, 64)) for k in range(4)] + [(0, pl.ds(128 * k, 128)) for k in range(2)]
    parts = [(s.at[rows], h.at[rows], t.at[rows]) for i, rows in slices for s, h, t in [(sources[i], held[i], targets[i])]]
    parts += [(sources[i], held[i], targets[i]) for i in range(2, 6)]
    arrive = [pltpu.make_async_copy(s, h, in_sem.at[k]) for k, (s, h, _) in enumerate(parts)]
    leave = [pltpu.make_async_copy(h, t, out_sem.at[k]) for k, (_, h, t) in enumerate(parts)]
    for copy in arrive:
        copy.start()
    for one, other in zip(arrive, leave):
        one.wait()
        other.start()
    for copy in leave:
        copy.wait()


def body(hidden, grad_values, weights, gains, snapshot, outer_frag, outer_moment, fragment_index):
    anywhere = pl.BlockSpec(memory_space=pl.ANY)
    dma = pltpu.SemaphoreType.DMA
    vmem = pltpu.VMEM
    shapes = (
        jax.ShapeDtypeStruct((TOK, KV), BF16),
        jax.ShapeDtypeStruct((TOK, D), BF16),
        jax.ShapeDtypeStruct((ROWS * FRAGS, 128), F32),
        jax.ShapeDtypeStruct((1, ROWS), F32),
        jax.ShapeDtypeStruct((ROWS, FW), F32),
        jax.ShapeDtypeStruct((ROWS, FW), F32),
    )
    results = pl.pallas_call(
        step_kernel,
        out_shape=shapes,
        in_specs=[pl.BlockSpec(memory_space=pltpu.SMEM)] + [anywhere] * 7,
        out_specs=(anywhere,) * 6,
        scratch_shapes=[
            vmem((TOK, D), BF16),
            vmem((2, TOK, KV), BF16),
            vmem((2, TOK, D), BF16),
            vmem((TOK, D), BF16),
            vmem((2, NZ, NY, BLOCK, 128), BF16),
            vmem((D, KV), BF16),
            vmem((SLAB, KV), F32),
            vmem((BLOCK, 128), F32),
            vmem((D, HALF), F32),
            vmem((NZ, 2, ZH, 128), BF16),
            vmem((NZ, 2, ZH, 128), BF16),
            vmem((NZ, 2, 2, ZH, 128), BF16),
            vmem((NZ, 2, 2, ZH, 128), BF16),
            vmem((NZ, 2, ZH, 128), F32),
            vmem((NZ // 2, 2, ZH, 128), BF16),
            vmem((NZ // 2, 2, ZH, 128), BF16),
            vmem((NZ, 2, ZH, 128), BF16),
            vmem((2, NZ, 2, ZH, 128), BF16),
            vmem((NY, VR, 128), F32),
            vmem((VR, 128), BF16),
            vmem((VR, 128), BF16),
            vmem((2, VR, 128), BF16),
            vmem((2, VR, 128), BF16),
            vmem((NZ, NY, VR, 128), BF16),
            vmem((2, NZ, NY, VR, 128), BF16),
            vmem((2, BLOCK, 128), F32),
            vmem((TOK, D), F32),
            vmem((TOK, KV), F32),
            vmem((TOK, KV), BF16),
            vmem((TOK, D), BF16),
            vmem((TOK, 128), F32),
            vmem((8, D), F32),
            vmem((8, D), F32),
            vmem((2, 8, 128), F32),
            vmem((NY, 8, 128), F32),
            vmem((NZ, 8, 128), F32),
            vmem((NZ, 8, 128), F32),
            vmem((NZ, 8, 128), F32),
            vmem((NE, 8, 128), F32),
            vmem((NX, 40, 128), F32),
            vmem((2, 40, 128), F32),
            vmem((ROWS * FRAGS, 128), F32),
            vmem((1, ROWS), F32),
            vmem((ROWS, 1, FW), F32),
            vmem((ROWS, FW), F32),
            vmem((ROWS, FW), F32),
            vmem((ROWS * FRAGS, 128), F32),
            vmem((1, ROWS), F32),
            vmem((ROWS, FW), F32),
            vmem((ROWS, FW), F32),
            dma((7,)), dma((6,)),
            dma((2, NZ // 2)), dma((NZ // 2,)), dma, dma((NZ // 2,)),
            dma, dma((2, NZ)),
            dma, dma((NZ,)),
            dma((2,)), dma((2,)),
            dma((2,)), dma((2, NZ)),
            dma, dma((NZ // 2,)),
            dma, dma((2, NZ // 2)),
            dma, dma((2, NZ)),
            dma((2,)), dma((2,)),
            dma, dma,
            dma, dma,
            dma, dma((2,)),
            dma((2, NZ // 2)), dma((NZ // 2,)), dma, dma,
            dma, dma, dma, dma,
            dma, dma((2,)),
            dma, dma,
            pltpu.SemaphoreType.REGULAR((7,)),
        ],
        compiler_params=pltpu.CompilerParams(
            collective_id=0, has_side_effects=True, vmem_limit_bytes=56 * 1024 * 1024,
        ),
        cost_estimate=pl.CostEstimate(flops=3 * 2 * TOK * D * KV, bytes_accessed=4_000_000, transcendentals=0),
    )(
        fragment_index, hidden, grad_values, weights.reshape(ROWS * FRAGS, 128), gains,
        snapshot.reshape(ROWS, 1, FW), outer_frag, outer_moment,
    )
    values, grad_hidden, new_weights, new_gains, new_outer, new_moment = pl.pallas_call(
        place_kernel,
        out_shape=shapes,
        in_specs=[anywhere] * 6,
        out_specs=(anywhere,) * 6,
        scratch_shapes=[vmem(shape.shape, shape.dtype) for shape in shapes] + [dma((10,)), dma((10,))],
        compiler_params=pltpu.CompilerParams(vmem_limit_bytes=60 * 1024 * 1024),
    )(*results)
    return (values, grad_hidden, new_weights.reshape(1, ROWS, KV), new_gains, new_outer, new_moment)


def solution(mesh):
    return jax.shard_map(
        body,
        mesh=mesh,
        in_specs=(
            P(("group", "fsdp"), None),
            P(("group", "fsdp"), None),
            P("group", "fsdp", None),
            P("group", "fsdp"),
            P("group", "fsdp", None),
            P("fsdp", None),
            P("fsdp", None),
            P(),
        ),
        out_specs=(
            P(("group", "fsdp"), None),
            P(("group", "fsdp"), None),
            P("group", "fsdp", None),
            P("group", "fsdp"),
            P("fsdp", None),
            P("fsdp", None),
        ),
        check_vma=False,
    )
```
